128 devices in a mesh: band: 16 (over y, x_lo, core), cross: 8 (over z, x_hi).
Axes of the slice: x: 4 (x_hi: 2, x_lo: 2; x = x_hi * 2 + x_lo), y: 4, z: 4, core: 2. Of those that a mesh axis runs over, the one named last changes fastest.
Arguments:
- rasters: int32 [4, 512, 8192], P(None, 'cross', 'band'), may hold values 0 or 1
- aerial: float32 [512, 8192], P('cross', 'band'), may hold values from -6 to 6
- w_in: float32 [32, 4], replicated, may hold values from -3 to 3
- aerial_gain: float32 [32], replicated, may hold values from -4 to 4
- b_in: float32 [32], replicated, may hold values from -2 to 2
- w_conv1: bfloat16 [32, 288], replicated, may hold values from -0.375 to 0.375
- b_conv1: float32 [32], replicated, may hold values from -2 to 2
- w_proj: bfloat16 [128, 32], replicated, may hold values from -1 to 1
- b_proj: float32 [128], replicated, may hold values from -2 to 2
- w_ctx: bfloat16 [128, 1920], replicated, may hold values from -0.25 to 0.25
- w_up: bfloat16 [32, 128], replicated, may hold values from -0.5 to 0.5
- b_up: float32 [32], replicated, may hold values from -2 to 2
- w_head: bfloat16 [2, 800], replicated, may hold values from -0.21875 to 0.21875
- b_head: float32 [2], replicated, may hold values from -3 to 3
Outputs:
- logits: float32 [2, 512, 8192], P(None, 'cross', 'band')
The draws below stay inside these ranges and needn't reach their ends.
All inputs are finite; a program needn't handle non-finite values. No bound on the sum of `rasters` on one device may be relied on, other than what follows from the above.
Results may differ from the reference program's by a relative error of at most 0.015.
Values may be sent and summed in bfloat16 or wider, within the bound.
No kernel may reach another device: no remote copies, remote signals or barrier semaphores. Data moves between devices by JAX's collectives and lax.ppermute only.
A program may use at most 192 MiB of HBM per device.

```python
import jax
import jax.numpy as jnp
from jax import lax

LAYERS = 4
C0 = 32
C1 = 128
NCLS = 2
TILE_H = 64
TILE_W = 512
NH = 512
NW = 8192
N_CROSS = 8


def with_ends(entries, rng, least, high):
    index_at = [jax.random.randint(jax.random.fold_in(rng, axis), (), 0, length) for axis, length in enumerate(entries.shape)]
    longest = entries.shape.index(max(entries.shape))
    next_to = index_at[:longest] + [(index_at[longest] + 1) % entries.shape[longest]] + index_at[longest + 1:]
    return entries.at[tuple(index_at)].set(least).at[tuple(next_to)].set(high)


def levels(key, dims, split, least, top_value):
    factor_of, own = 1.0, jax.random.fold_in(key, 6)
    for axis_at, parts in split:
        steps = jnp.exp(jax.random.uniform(jax.random.fold_in(own, axis_at), (parts,), jnp.float32, least / len(split), top_value / len(split)))
        factor_of = factor_of * jnp.repeat(steps, dims[axis_at] // parts).reshape([-1 if axis == axis_at else 1 for axis in range(len(dims))])
    return factor_of


def normal_values(rng, extent, spread, reach, pieces=(), kind=jnp.bfloat16):
    array = jax.random.normal(rng, extent, jnp.float32) * spread
    if len(pieces) > 0:
        array = levels(rng, extent, pieces, -0.22, 0.18) * array
    return jnp.clip(array, min=-reach, max=reach).astype(kind)


def setup_inputs(seed: int = 0) -> dict:
    keys = jax.random.split(jax.random.key(seed), 15)
    return {
        "rasters": with_ends((jax.random.randint(keys[0], (LAYERS, NH, NW), 0, 5) < 2).astype(jnp.int32), jax.random.fold_in(keys[0], 1), 0, 1),
        "aerial": normal_values(keys[1], (NH, NW), 1.0, 6.0, ((0, 8), (1, 16)), jnp.float32),
        "w_in": normal_values(keys[2], (C0, LAYERS), LAYERS ** -0.5, 3.0, (), jnp.float32),
        "aerial_gain": normal_values(keys[3], (C0,), 1.0, 4.0, (), jnp.float32),
        "b_in": normal_values(keys[4], (C0,), 0.5, 2.0, (), jnp.float32),
        "w_conv1": normal_values(keys[5], (C0, 9 * C0), (9 * C0) ** -0.5, 0.375),
        "b_conv1": normal_values(keys[6], (C0,), 0.5, 2.0, (), jnp.float32),
        "w_proj": normal_values(keys[7], (C1, C0), C0 ** -0.5, 1.0),
        "b_proj": normal_values(keys[8], (C1,), 0.5, 2.0, (), jnp.float32),
        "w_ctx": normal_values(keys[9], (C1, 15 * C1), (5 * C1) ** -0.5, 0.25),
        "w_up": normal_values(keys[10], (C0, C1), C1 ** -0.5, 0.5),
        "b_up": normal_values(keys[11], (C0,), 0.5, 2.0, (), jnp.float32),
        "w_head": normal_values(keys[12], (NCLS, 25 * C0), (25 * C0) ** -0.5, 0.21875),
        "b_head": normal_values(keys[13], (NCLS,), 1.0, 3.0, (), jnp.float32),
    }


def stem_layer(rasters, aerial, w_in, aerial_gain, b_in):
    layer_count, row_count, col_count = rasters.shape
    flat_rasters = rasters.reshape(layer_count, row_count * col_count).astype(jnp.float32)
    combined = jnp.dot(w_in, flat_rasters, precision=lax.Precision.HIGHEST)
    combined = combined.reshape(-1, row_count, col_count) + aerial_gain[:, None, None] * aerial[None] + b_in[:, None, None]
    return jax.nn.relu(combined).astype(jnp.bfloat16)


def conv_rows(padded, weights, taps, row_count, col_count):
    channels = padded.shape[0]
    stacked = jnp.concatenate([padded[:, :, offset:offset + col_count] for offset in range(taps)], axis=0)
    summed = jnp.zeros((weights.shape[0], row_count * col_count), jnp.float32)
    for row_off in range(taps):
        window = stacked[:, row_off:row_off + row_count, :].reshape(taps * channels, row_count * col_count)
        part_w = weights[:, row_off * taps * channels:(row_off + 1) * taps * channels]
        summed = summed + jnp.dot(part_w, window, preferred_element_type=jnp.float32)
    return summed.reshape(-1, row_count, col_count)


def pool_map(features):
    channels, row_count, col_count = features.shape
    blocks = features.reshape(channels, row_count // 4, 4, col_count // 4, 4).astype(jnp.float32)
    return jnp.mean(blocks, axis=(2, 4)).astype(jnp.bfloat16)


def reference(rasters, aerial, w_in, aerial_gain, b_in, w_conv1, b_conv1, w_proj, b_proj, w_ctx, w_up, b_up, w_head, b_head):
    stem_out = stem_layer(rasters, aerial, w_in, aerial_gain, b_in)
    stem_pad = jnp.pad(stem_out, ((0, 0), (1, 1), (1, 1)))

    def strip_conv(strip_index):
        first_row = (strip_index * TILE_H).astype(jnp.int32)
        window = lax.dynamic_slice_in_dim(stem_pad, first_row, TILE_H + 2, 1)
        result = conv_rows(window, w_conv1, 3, TILE_H, NW) + b_conv1[:, None, None]
        return jax.nn.relu(result).astype(jnp.bfloat16)

    strips = lax.map(strip_conv, jnp.arange(N_CROSS, dtype=jnp.int32))
    features = jnp.transpose(strips, (1, 0, 2, 3)).reshape(C0, NH, NW)
    pooled = pool_map(features)
    pool_rows = NH // 4
    pool_cols = NW // 4
    proj_map = jnp.dot(w_proj, pooled.reshape(C0, pool_rows * pool_cols), preferred_element_type=jnp.float32)
    proj_map = jax.nn.relu(proj_map + b_proj[:, None]).astype(jnp.bfloat16).reshape(C1, pool_rows, pool_cols)
    tile_rows = TILE_H // 4
    tile_cols = TILE_W // 4
    map_pad = jnp.pad(proj_map, ((0, 0), (tile_rows, tile_rows), (2 * tile_cols, 2 * tile_cols)))
    context = proj_map.astype(jnp.float32).reshape(C1, pool_rows * pool_cols)
    for row_off in range(3):
        for col_off in range(5):
            tap_index = row_off * 5 + col_off
            shifted = map_pad[:, row_off * tile_rows:row_off * tile_rows + pool_rows, col_off * tile_cols:col_off * tile_cols + pool_cols]
            context = context + jnp.dot(w_ctx[:, tap_index * C1:(tap_index + 1) * C1], shifted.reshape(C1, pool_rows * pool_cols), preferred_element_type=jnp.float32)
    mixed_map = jax.nn.relu(context).astype(jnp.bfloat16)
    lifted = jnp.dot(w_up, mixed_map, preferred_element_type=jnp.float32).reshape(C0, pool_rows, 1, pool_cols, 1)
    lifted = jnp.broadcast_to(lifted, (C0, pool_rows, 4, pool_cols, 4)).reshape(C0, NH, NW)
    decoded = jax.nn.relu(features.astype(jnp.float32) + lifted + b_up[:, None, None]).astype(jnp.bfloat16)
    decoded_pad = jnp.pad(decoded, ((0, 0), (2, 2), (2, 2)))
    flipped = w_head.reshape(NCLS, 5, 5, C0)[:, ::-1, ::-1, :].reshape(NCLS, 25 * C0)

    def strip_head(strip_index):
        first_row = (strip_index * TILE_H).astype(jnp.int32)
        window = lax.dynamic_slice_in_dim(decoded_pad, first_row, TILE_H + 4, 1)
        return conv_rows(window, flipped, 5, TILE_H, NW) + b_head[:, None, None]

    head_strips = lax.map(strip_head, jnp.arange(N_CROSS, dtype=jnp.int32))
    return jnp.transpose(head_strips, (1, 0, 2, 3)).reshape(NCLS, NH, NW)
```

```python
import functools

import jax
import jax.numpy as jnp
from jax import lax
from jax.experimental import pallas as pl
from jax.experimental.pallas import tpu as pltpu
from jax.sharding import PartitionSpec as P

ROWS, COLS = 64, 512
CH, WIDE, KINDS = 32, 128, 8
POOL_ROWS, POOL_COLS = 16, 128
SPOTS = POOL_ROWS * POOL_COLS
VMEM = pl.BlockSpec(memory_space=pltpu.VMEM)
SMEM = pl.BlockSpec(memory_space=pltpu.SMEM)
F32, BF16 = jnp.float32, jnp.bfloat16


def iota(shape, dim):
    return lax.broadcasted_iota(jnp.int32, shape, dim)


def shape_of(*dims, dtype=F32):
    return jax.ShapeDtypeStruct(dims, dtype)


def params():
    return pltpu.CompilerParams(vmem_limit_bytes=56 * 1024 * 1024)


def mm(a, b):
    return jnp.dot(a, b, preferred_element_type=F32)


def column(row):
    count = row.shape[1]
    eye = iota((count, count), 0) == iota((count, count), 1)
    return jnp.sum(jnp.where(eye, row, 0.0), axis=1, keepdims=True)


def halo_kernel(rasters, aerial, col_low, col_high, row_low, row_high, corners):
    lane = iota((ROWS, 128), 1)
    for out, x, at in ((col_low, 0, 0), (col_high, COLS - 128, 127)):
        packed = jnp.zeros((ROWS, 128), F32)
        for kind in range(5):
            if kind < 4:
                slab = rasters[kind, :, x : x + 128].astype(F32)
            else:
                slab = aerial[:, x : x + 128]
            packed = jnp.where(lane == kind, slab[:, at : at + 1], packed)
        out[...] = packed
    rows = []
    for out, y in ((row_low, 0), (row_high, ROWS - 1)):
        parts = [rasters[kind, y : y + 1, :].astype(F32) for kind in range(4)]
        parts += [aerial[y : y + 1, :], jnp.zeros((3, COLS), F32)]
        rows.append(jnp.concatenate(parts, axis=0))
        out[...] = rows[-1]
    lane = iota((KINDS, 128), 1)
    packed = jnp.zeros((KINDS, 128), F32)
    spots = [(0, 0), (0, COLS - 1), (1, 0), (1, COLS - 1)]
    for spot, (which, x) in enumerate(spots):
        packed = jnp.where(lane == spot, rows[which][:, x : x + 1], packed)
    corners[...] = packed


def features_kernel(
    cells, place, rasters, aerial, left, right, above, below, c_tl, c_tr, c_bl, c_br,
    kinds_w, conv_w, conv_b, features, pooled, stem_w, wide_w, pool_w, stem3,
):
    last_cross, last_band = cells
    has_above = (place[0] > 0).astype(F32)
    has_below = (place[0] < last_cross).astype(F32)
    has_left = (place[1] > 0).astype(F32)
    has_right = (place[1] < last_band).astype(F32)

    kinds = kinds_w[...]
    spread = jnp.where(iota((KINDS, 64), 1) // 8 == iota((KINDS, 64), 0), 1.0, 0.0).astype(BF16)
    same = iota((256, 64), 0) // CH == iota((256, 64), 1) % 8
    high = kinds.astype(BF16)
    low = (kinds - high.astype(F32)).astype(BF16)
    halves = []
    for part in (high, low):
        rows = mm(jnp.concatenate([part] * 8, axis=0), spread)
        halves.append(jnp.where(same, rows, 0.0))
    stem_w[...] = jnp.concatenate(halves, axis=1).astype(BF16)

    pool_w[...] = jnp.where(
        iota((COLS, POOL_COLS), 0) // 4 == iota((COLS, POOL_COLS), 1), 1.0 / 16, 0.0
    ).astype(BF16)

    wide_w[...] = jnp.zeros(wide_w.shape, BF16)
    taps = conv_w[...]
    for y in range(8):
        wide_w[y * CH : (y + 1) * CH, y * 96 : y * 96 + 288] = taps

    def stem(values, aerial_part, ones):
        top = aerial_part.astype(BF16)
        rest = (aerial_part - top.astype(F32)).astype(BF16)
        x = jnp.concatenate(
            [values.astype(BF16), jnp.concatenate([top, rest], axis=0),
             jnp.concatenate([ones, jnp.zeros_like(ones)], axis=0).astype(BF16)], axis=0
        )
        out = mm(stem_w[...], jnp.concatenate([x, x], axis=0))
        return jnp.maximum(out, 0.0)

    def put(first, s):
        shifted_up = pltpu.roll(s, 1, 1)[:, :COLS].astype(BF16)
        shifted_down = pltpu.roll(s, COLS + 127, 1)[:, :COLS].astype(BF16)
        middle = s[:, :COLS].astype(BF16)
        stem3[pl.ds(first, 96), :] = jnp.concatenate([shifted_up, middle, shifted_down], axis=0)

    lane8 = iota((8, 128), 1)

    def stem_rows(block, carry):
        y = pl.multiple_of(block * 8, 8)
        low_cols = left[pl.ds(y, 8), :] * has_left
        high_cols = right[pl.ds(y, 8), :] * has_right

        def edge(kind):
            return jnp.where(
                lane8 == 127, low_cols[:, kind : kind + 1],
                jnp.where(lane8 == 0, high_cols[:, kind : kind + 1], 0.0),
            )

        values = [
            jnp.concatenate([rasters[k, pl.ds(y, 8), :].astype(F32), edge(k)], axis=1)
            for k in range(4)
        ]
        aerial_part = jnp.concatenate([aerial[pl.ds(y, 8), :], edge(4)], axis=1)
        edge_ones = jnp.where(lane8 == 127, has_left, jnp.where(lane8 == 0, has_right, 0.0))
        ones = jnp.concatenate([jnp.ones((8, COLS), F32), edge_ones], axis=1)
        out = stem(jnp.concatenate(values, axis=0), aerial_part, ones)
        for r in range(8):
            first = pl.multiple_of((block * 8 + r + 1) * 96, 96)
            put(first, out[r * CH : (r + 1) * CH, :])
        return carry

    lax.fori_loop(0, ROWS // 8, stem_rows, 0)

    row8 = iota((8, 640), 0)
    upper, lower = above[...] * has_above, below[...] * has_below
    tl = c_tl[...] * (has_above * has_left)
    tr = c_tr[...] * (has_above * has_right)
    bl = c_bl[...] * (has_below * has_left)
    br = c_br[...] * (has_below * has_right)

    def rim(kind):
        up = jnp.where(
            lane8 == 127, tl[kind : kind + 1, 3:4],
            jnp.where(lane8 == 0, tr[kind : kind + 1, 2:3], 0.0),
        )
        down = jnp.where(
            lane8 == 127, bl[kind : kind + 1, 1:2],
            jnp.where(lane8 == 0, br[kind : kind + 1, 0:1], 0.0),
        )
        up = jnp.concatenate([jnp.broadcast_to(upper[kind : kind + 1, :], (8, COLS)), up], axis=1)
        down = jnp.concatenate([jnp.broadcast_to(lower[kind : kind + 1, :], (8, COLS)), down], axis=1)
        return jnp.where(row8 == 0, up, jnp.where(row8 == 1, down, 0.0))

    up = jnp.where(lane8 == 127, has_left, jnp.where(lane8 == 0, has_right, 0.0))
    side = jnp.concatenate([jnp.ones((8, COLS), F32), up], axis=1)
    ones = jnp.where(row8 == 0, side * has_above, jnp.where(row8 == 1, side * has_below, 0.0))
    out = stem(jnp.concatenate([rim(k) for k in range(4)], axis=0), rim(4), ones)
    put(0, out[:CH, :])
    put((ROWS + 1) * 96, out[CH : 2 * CH, :])

    bias = jnp.concatenate([jnp.broadcast_to(column(conv_b[...]), (CH, COLS))] * 8, axis=0)

    def conv_rows(block, carry):
        first = pl.multiple_of(block * 8 * 96, 96)
        out = mm(wide_w[...], stem3[pl.ds(first, 960), :])
        value = jnp.maximum(out + bias, 0.0).astype(BF16)
        features[pl.ds(pl.multiple_of(block * 256, 256), 256), :] = value
        means = mm(value, pool_w[...])
        for half in range(2):
            part = means[half * 128 : (half + 1) * 128, :]
            total = (part[:32] + part[32:64]) + (part[64:96] + part[96:])
            at = pl.multiple_of((block * 2 + half) * POOL_COLS, POOL_COLS)
            pooled[:, pl.ds(at, POOL_COLS)] = total.astype(BF16)
        return carry

    lax.fori_loop(0, ROWS // 8, conv_rows, 0)


def logits_kernel(
    cells, place, features, *rest,
):
    (maps, (proj_w, proj_b, ctx_w, up_w, up_b, head_w, rim_w, head_b),
     (logits, col_out, row_out, corner_out),
     (weights, proj, low_up, lifted, decoded)) = (rest[:15], rest[15:23], rest[23:27], rest[27:])
    last_cross, last_band = cells
    cross, band = place[0], place[1]
    core = band % 2
    sign = 1 - 2 * core

    for at in range(15):
        u, v = at // 5 - 1, at % 5 - 2
        row, col = cross + u, band + v * sign
        inside = (row >= 0) & (row <= last_cross) & (col >= 0) & (col <= last_band)
        mirrored = (at // 5) * 5 + (4 - at % 5)
        one = ctx_w[:, at * WIDE : (at + 1) * WIDE]
        two = ctx_w[:, mirrored * WIDE : (mirrored + 1) * WIDE]
        chosen = jnp.where(core == 0, one, two)
        weights[:, at * WIDE : (at + 1) * WIDE] = jnp.where(inside, chosen, jnp.zeros_like(chosen))

    p_bias = jnp.broadcast_to(column(proj_b[...]), (WIDE, 256))
    u_bias = jnp.broadcast_to(column(up_b[...]), (CH, 256))

    def context_part(part, carry):
        at = pl.multiple_of(part * 256, 256)
        for k in range(15):
            out = mm(proj_w[...], maps[k][:, pl.ds(at, 256)])
            proj[k * WIDE : (k + 1) * WIDE, :] = jnp.maximum(out + p_bias, 0.0).astype(BF16)
        context = mm(weights[...], proj[...]) + proj[7 * WIDE : 8 * WIDE, :].astype(F32)
        mixed = jnp.maximum(context, 0.0).astype(BF16)
        up = mm(up_w[...], mixed) + u_bias
        high = up.astype(BF16)
        low = (up - high.astype(F32)).astype(BF16)
        both = [
            jnp.concatenate([high[:, h * 128 : (h + 1) * 128], low[:, h * 128 : (h + 1) * 128]], axis=1)
            for h in range(2)
        ]
        low_up[pl.ds(pl.multiple_of(part * 64, 64), 64), :] = jnp.concatenate(both, axis=0)
        return carry

    lax.fori_loop(0, SPOTS // 256, context_part, 0)

    widen = jnp.where(
        iota((256, COLS), 0) % 128 == iota((256, COLS), 1) // 4, 1.0, 0.0
    ).astype(BF16)
    lifted[...] = mm(low_up[...], widen)

    decoded[0:64, :] = jnp.zeros((64, COLS), BF16)
    decoded[66 * CH :, :] = jnp.zeros((64, COLS), BF16)

    def decode(p, carry):
        up = lifted[pl.ds(pl.multiple_of(p * CH, CH), CH), :]
        for r in range(4):
            at = pl.multiple_of((4 * p + r) * CH, CH)
            value = jnp.maximum(features[pl.ds(at, CH), :].astype(F32) + up, 0.0).astype(BF16)
            decoded[pl.ds(pl.multiple_of(at + 64, CH), CH), :] = value
        return carry

    lax.fori_loop(0, POOL_ROWS, decode, 0)

    def gather_taps(z, count):
        total = None
        for dx in range(5):
            part = z[dx * count : (dx + 1) * count, :]
            part = jnp.concatenate([part, jnp.zeros((count, 128), F32)], axis=1)
            if dx != 2:
                part = pltpu.roll(part, (dx - 2) % 640, 1)
            total = part if total is None else total + part
        return total

    lane16 = iota((16, 128), 1)
    first_lanes = (lane16 < 2) | (lane16 >= 126)

    def head(block, carry):
        first = pl.multiple_of(block * 16 * CH, 16 * CH)
        total = gather_taps(mm(head_w[...], decoded[pl.ds(first, 20 * CH), :]), 32)
        y = pl.multiple_of(block * 16, 16)
        for k in range(2):
            logits[k, pl.ds(y, 16), :] = total[k * 16 : (k + 1) * 16, :COLS] + head_b[k]
        rim = total[:, COLS:]
        col_out[pl.ds(y, 16), :] = jnp.where(first_lanes, rim[:16], pltpu.roll(rim[16:], 4, 1))
        return carry

    lax.fori_loop(0, ROWS // 16, head, 0)

    ends = jnp.concatenate([decoded[64:128, :], decoded[64 * CH : 66 * CH, :]], axis=0)
    total = gather_taps(mm(rim_w[...], ends), 8)
    row_out[...] = total[:, :COLS]
    corner_out[...] = total[:, COLS:]


def sum_kernel(cells, place, inner, left, right, above, below, c_tl, c_tr, c_bl, c_br, out):
    last_cross, last_band = cells
    has_above = (place[0] > 0).astype(F32)
    has_below = (place[0] < last_cross).astype(F32)
    has_left = (place[1] > 0).astype(F32)
    has_right = (place[1] < last_band).astype(F32)
    out[...] = inner[...]
    lane = iota((ROWS, 128), 1)
    low, high = left[...] * has_left, right[...] * has_right
    for k in range(2):
        part = low if k == 0 else pltpu.roll(low, 124, 1)
        out[k, :, 0:128] += jnp.where(lane < 2, part, 0.0)
        part = high if k == 0 else pltpu.roll(high, 124, 1)
        out[k, :, COLS - 128 : COLS] += jnp.where(lane >= 126, part, 0.0)
    lane2 = iota((2, 128), 1)
    upper, lower = above[...] * has_above, below[...] * has_below
    tl = c_tl[...] * (has_above * has_left)
    tr = c_tr[...] * (has_above * has_right)
    bl = c_bl[...] * (has_below * has_left)
    br = c_br[...] * (has_below * has_right)
    none = jnp.zeros((2, COLS - 256), F32)
    for k in range(2):
        arrived = slice(4 * k + 2, 4 * k + 4)
        sides = [jnp.where(lane2 < 2, tl[arrived], 0.0), none, jnp.where(lane2 >= 126, tr[arrived], 0.0)]
        out[k, 0:2, :] += upper[arrived] + jnp.concatenate(sides, axis=1)
        arrived = slice(4 * k, 4 * k + 2)
        sides = [jnp.where(lane2 < 2, bl[arrived], 0.0), none, jnp.where(lane2 >= 126, br[arrived], 0.0)]
        out[k, ROWS - 2 : ROWS, :] += lower[arrived] + jnp.concatenate(sides, axis=1)


def call(kernel, outs, args, spaces=None, scratch=()):
    return pl.pallas_call(
        kernel,
        out_shape=outs,
        in_specs=spaces or [VMEM] * len(args),
        out_specs=jax.tree.map(lambda _: VMEM, outs),
        scratch_shapes=list(scratch),
        compiler_params=params(),
    )(*args)


def body(
    n_cross, n_band, rasters, aerial, w_in, aerial_gain, b_in, w_conv1, b_conv1, w_proj, b_proj,
    w_ctx, w_up, b_up, w_head, b_head,
):
    cells = (n_cross - 1, n_band - 1)
    place = jnp.stack([lax.axis_index("cross"), lax.axis_index("band")]).astype(jnp.int32)

    def moved(x, source):
        route = []
        for cross in range(n_cross):
            for band in range(n_band):
                c, b = source(cross, band)
                route.append(((b % n_band) * n_cross + c % n_cross, band * n_cross + cross))
        return lax.ppermute(x, ("band", "cross"), route)

    def fetched(x, u, v):
        return moved(x, lambda c, b: (c + u, b + v))

    def around(cols, rows, corners):
        return [
            fetched(cols[0], 0, -1), fetched(cols[1], 0, 1),
            fetched(rows[0], -1, 0), fetched(rows[1], 1, 0),
            fetched(corners, -1, -1), fetched(corners, -1, 1),
            fetched(corners, 1, -1), fetched(corners, 1, 1),
        ]

    col_low, col_high, row_low, row_high, corners = call(
        halo_kernel,
        [shape_of(ROWS, 128)] * 2 + [shape_of(KINDS, COLS)] * 2 + [shape_of(KINDS, 128)],
        [rasters, aerial],
    )
    rims = around((col_high, col_low), (row_high, row_low), corners)

    gain = aerial_gain[:, None]
    kinds_w = jnp.concatenate([w_in, gain, gain, b_in[:, None], jnp.zeros_like(gain)], axis=1)
    features, pooled = call(
        functools.partial(features_kernel, cells),
        [shape_of(ROWS * CH, COLS, dtype=BF16), shape_of(CH, SPOTS, dtype=BF16)],
        [place, rasters, aerial, *rims, kinds_w, w_conv1, b_conv1[None, :]],
        [SMEM] + [VMEM] * 13,
        [
            pltpu.VMEM((256, 128), BF16),
            pltpu.VMEM((256, 960), BF16),
            pltpu.VMEM((COLS, POOL_COLS), BF16),
            pltpu.VMEM(((ROWS + 2) * 96, COLS), BF16),
        ],
    )

    def far(x, u):
        return moved(x, lambda c, b: (c + u, b + 2 - 4 * (b % 2)))

    def other(x, u):
        return moved(x, lambda c, b: (c + u, b - 2 + 4 * (b % 2)))

    def partner(x):
        return moved(x, lambda c, b: (c, b ^ 1))

    maps = []
    for u in (-1, 0, 1):
        own = pooled if u == 0 else fetched(pooled, u, 0)
        away = far(pooled, u)
        maps.append([other(pooled, u), partner(away), own, partner(own), away])
    maps = sum(maps, [])

    taps = w_head.reshape(2, 5, 5, CH)[:, ::-1].transpose(2, 0, 1, 3).reshape(10, 5 * CH)
    skewed = jnp.broadcast_to(jnp.pad(taps, ((0, 0), (0, 16 * CH)))[:, None, :], (10, 16, 21 * CH))
    head_w = skewed.reshape(10, 16 * 21 * CH)[:, : 16 * 20 * CH].reshape(160, 20 * CH)
    gap = jnp.zeros((10, CH), BF16)
    at = [taps[:, (4 - d) * CH : (5 - d) * CH] for d in range(5)]
    rim_rows = [[at[0], gap, gap, gap], [at[1], at[0], gap, gap], [gap, gap, at[4], at[3]], [gap, gap, gap, at[4]]]
    rim_w = jnp.stack([jnp.concatenate(r, axis=1) for r in rim_rows], axis=1).reshape(40, 4 * CH)

    inner, col_out, row_out, corner_out = call(
        functools.partial(logits_kernel, cells),
        [shape_of(2, ROWS, COLS), shape_of(ROWS, 128), shape_of(8, COLS), shape_of(8, 128)],
        [place, features, *maps, w_proj, b_proj[None, :], w_ctx, w_up, b_up[None, :], head_w, rim_w, b_head],
        [SMEM] + [VMEM] * 23 + [SMEM],
        [
            pltpu.VMEM((WIDE, 15 * WIDE), BF16),
            pltpu.VMEM((15 * WIDE, 256), BF16),
            pltpu.VMEM((POOL_ROWS * CH, 256), BF16),
            pltpu.VMEM((POOL_ROWS * CH, COLS), F32),
            pltpu.VMEM(((ROWS + 4) * CH, COLS), BF16),
        ],
    )
    rims = around((col_out, col_out), (row_out, row_out), corner_out)
    return call(
        functools.partial(sum_kernel, cells),
        shape_of(2, ROWS, COLS),
        [place, inner, *rims],
        [SMEM] + [VMEM] * 9,
    )


def solution(mesh):
    sizes = dict(mesh.shape)
    return jax.shard_map(
        functools.partial(body, sizes["cross"], sizes["band"]),
        mesh=mesh,
        in_specs=(P(None, "cross", "band"), P("cross", "band")) + (P(),) * 12,
        out_specs=P(None, "cross", "band"),
        check_vma=False,
    )
```

```python
import functools

import jax
import jax.numpy as jnp
from jax import lax
from jax.experimental import pallas as pl
from jax.experimental.pallas import tpu as pltpu
from jax.sharding import PartitionSpec as P

ROWS, COLS = 64, 512
CH, WIDE, KINDS = 32, 128, 8
POOL_ROWS, POOL_COLS = 16, 128
SPOTS = POOL_ROWS * POOL_COLS
HALF = ROWS // 2
VMEM = pl.BlockSpec(memory_space=pltpu.VMEM)
SMEM = pl.BlockSpec(memory_space=pltpu.SMEM)
F32, BF16 = jnp.float32, jnp.bfloat16


def iota(shape, dim):
    return lax.broadcasted_iota(jnp.int32, shape, dim)


def shape_of(*dims, dtype=F32):
    return jax.ShapeDtypeStruct(dims, dtype)


def mm(a, b):
    return jnp.dot(a, b, preferred_element_type=F32)


def split(x):
    high = x.astype(BF16)
    return high, (x - high.astype(F32)).astype(BF16)


def column(row):
    count = row.shape[1]
    eye = iota((count, count), 0) == iota((count, count), 1)
    return jnp.sum(jnp.where(eye, row, 0.0), axis=1, keepdims=True)


def flags(place, last_cross, last_band):
    one = lambda truth: truth.astype(F32)
    return (
        one(place[0] > 0), one(place[0] < last_cross), one(place[1] > 0), one(place[1] < last_band)
    )


def pool_weights():
    x, q = iota((COLS, POOL_COLS), 0), iota((COLS, POOL_COLS), 1)
    inner = (x // 4 == q) & (x > 0) & (x < COLS - 1)
    return jnp.where(inner, 1.0 / 16, 0.0).astype(BF16)


def halo_kernel(rasters, aerial, rows, cols, message):
    ones, none = jnp.ones((1, COLS), F32), jnp.zeros((2, COLS), F32)
    for at, y in enumerate((0, 1, ROWS - 2, ROWS - 1)):
        parts = [rasters[kind, y : y + 1, :].astype(F32) for kind in range(4)]
        rows[at * 8 : (at + 1) * 8, :] = jnp.concatenate(parts + [aerial[y : y + 1, :], ones, none], axis=0)
    lane = iota((ROWS, 128), 1)
    packed = jnp.where((lane < 32) & (lane % 8 == 5), 1.0, 0.0)
    for at, x in enumerate((0, 1, COLS - 2, COLS - 1)):
        first = x // 128 * 128
        for kind in range(5):
            if kind < 4:
                slab = rasters[kind, :, first : first + 128].astype(F32)
            else:
                slab = aerial[:, first : first + 128]
            packed = jnp.where(lane == at * 8 + kind, slab[:, x - first : x - first + 1], packed)
    turned = jnp.transpose(jnp.concatenate([packed, jnp.zeros((128 - ROWS, 128), F32)], axis=0))
    cols[...] = turned[:32]
    message[...] = jnp.concatenate([turned[:8], turned[24:32]], axis=0)


def sides(place, partner, outer, low, high):
    even = place[1] % 2 == 0
    left = jnp.where(even, outer[high], partner[high])
    right = jnp.where(even, partner[low], outer[low])
    return left, right


def row_message_kernel(cells, place, rows, partner, outer, even_message, odd_message):
    _, _, has_left, has_right = flags(place, *cells)
    left, right = sides(place, partner, outer, slice(0, 8), slice(8, 16))
    left, right = left * has_left, right * has_right
    lane = iota((8, 128), 1)

    def row(at, y):
        side = jnp.where(lane == 0, right[:, y : y + 1], jnp.where(lane == 1, left[:, y : y + 1], 0.0))
        return jnp.concatenate([rows[at * 8 : (at + 1) * 8, :], side], axis=1)

    low, high = row(0, 0), row(3, ROWS - 1)
    even = place[0] % 2 == 0
    even_message[...] = jnp.where(even, high, low)
    odd_message[...] = jnp.where(even, low, high)


def inner_kernel(half, rasters, aerial, kinds_w, conv_w, conv_b, features, sums, stem_w, wide_w, stem3):
    spread = jnp.where(iota((KINDS, 64), 1) // 8 == iota((KINDS, 64), 0), 1.0, 0.0).astype(BF16)
    same = iota((256, 64), 0) // CH == iota((256, 64), 1) % 8
    halves = []
    for part in split(kinds_w[...]):
        rows = mm(jnp.concatenate([part] * 8, axis=0), spread)
        halves.append(jnp.where(same, rows, 0.0))
    stem_w[...] = jnp.concatenate(halves, axis=1).astype(BF16)
    wide_w[...] = jnp.zeros(wide_w.shape, BF16)
    taps = conv_w[...]
    for y in range(8):
        wide_w[y * CH : (y + 1) * CH, y * 96 : y * 96 + 288] = taps
    pool_w = pool_weights()
    bias = jnp.broadcast_to(column(conv_b[...]), (CH, COLS))
    bias = jnp.concatenate([bias] * 8, axis=0)

    blocks = range(5) if half == 0 else range(3, 8)
    base = half * HALF - 1
    edge = 0 if half == 0 else HALF + 1
    stem3[edge * 96 : (edge + 1) * 96, :] = jnp.zeros((96, COLS), BF16)
    for block in blocks:
        y = block * 8
        values = jnp.concatenate([rasters[k, y : y + 8, :] for k in range(4)], axis=0).astype(F32)
        high, low = split(aerial[y : y + 8, :])
        tail = jnp.concatenate([jnp.ones((8, COLS), BF16), jnp.zeros((8, COLS), BF16)], axis=0)
        x = jnp.concatenate([values.astype(BF16), high, low, tail], axis=0)
        out = jnp.maximum(mm(stem_w[...], jnp.concatenate([x, x], axis=0)), 0.0)
        for r in range(8):
            at = y + r - base
            if at < 0 or at > HALF + 1:
                continue
            s = out[r * CH : (r + 1) * CH, :]
            parts = [pltpu.roll(s, 1, 1), s, pltpu.roll(s, COLS - 1, 1)]
            stem3[at * 96 : (at + 1) * 96, :] = jnp.concatenate(parts, axis=0).astype(BF16)

    for block in range(HALF // 8):
        out = mm(wide_w[...], stem3[block * 768 : block * 768 + 960, :])
        value = jnp.maximum(out + bias, 0.0).astype(BF16)
        features[block * 256 : (block + 1) * 256, :] = value
        means = mm(value, pool_w)
        for p in range(2):
            rows = [means[p * 128 + r * 32 : p * 128 + (r + 1) * 32, :] for r in range(4)]
            if half == 0 and block == 0 and p == 0:
                rows = rows[1:]
            if half == 1 and block == HALF // 8 - 1 and p == 1:
                rows = rows[:3]
            at = (block * 2 + p) * POOL_COLS
            sums[:, at : at + POOL_COLS] = sum(rows[1:], rows[0])


def rim_kernel(
    cells, place, rows, cols, partner, outer, even_message, odd_message, sums_low, sums_high,
    kinds_w, conv_w, conv_b, rim_rows, rim_cols, pooled,
):
    has_above, has_below, has_left, has_right = flags(place, *cells)
    left, right = sides(place, partner, outer, slice(0, 8), slice(8, 16))
    left, right = left * has_left, right * has_right
    even = place[0] % 2 == 0
    above = jnp.where(even, odd_message[...], even_message[...]) * has_above
    below = jnp.where(even, even_message[...], odd_message[...]) * has_below
    kind_high, kind_low = split(kinds_w[...])
    stem_w = jnp.concatenate([kind_high, kind_high, kind_low], axis=1)
    bias = column(conv_b[...])

    def stem(x):
        high, low = split(x)
        high = high.astype(F32)
        stacked = jnp.concatenate([high, low.astype(F32), high], axis=0).astype(BF16)
        return jnp.maximum(mm(stem_w, stacked), 0.0)

    def conv(stacked):
        return jnp.maximum(mm(conv_w[...], stacked) + bias, 0.0).astype(BF16)

    def row(at):
        return rows[at * 8 : (at + 1) * 8, :]

    pool_w = pool_weights()
    row_sums = []
    trios = [(above[:, :COLS], row(0), row(1)), (row(2), row(3), below[:, :COLS])]
    for at, trio in enumerate(trios):
        stacked = []
        for x in trio:
            s = stem(x)
            stacked += [pltpu.roll(s, 1, 1), s, pltpu.roll(s, COLS - 1, 1)]
        value = conv(jnp.concatenate(stacked, axis=0).astype(BF16))
        rim_rows[at * CH : (at + 1) * CH, :] = value
        row_sums.append(mm(value, pool_w))

    lane = iota((8, 128), 1)

    def line(inside, top, bottom, x):
        top, bottom = top[:, x : x + 1], bottom[:, x : x + 1]
        return jnp.where(lane < ROWS, inside, jnp.where(lane == ROWS, bottom, 0.0)), top

    x_of = {-1: COLS + 1, COLS: COLS}
    lines = {-1: left, COLS: right}
    for at, x in enumerate((0, 1, COLS - 2, COLS - 1)):
        lines[x] = cols[at * 8 : (at + 1) * 8, :]
    columns = []
    for dx in (-1, 0, 1):
        low, low_top = line(lines[dx], above, below, x_of.get(dx, dx))
        x = COLS - 1 + dx
        high, high_top = line(lines[x], above, below, x_of.get(x, x))
        low = jnp.where(lane == 127, high_top, low)
        high = jnp.where(lane == 127, low_top, high)
        columns.append(stem(jnp.concatenate([low, high], axis=1)))
    s = jnp.concatenate(columns, axis=0)
    stacked = [pltpu.roll(s, 1, 1), s, pltpu.roll(s, 255, 1)]
    value = conv(jnp.concatenate(stacked, axis=0).astype(BF16))
    rim_cols[...] = value
    y, at = iota((256, SPOTS), 0), iota((256, SPOTS), 1)
    p, q = at // POOL_COLS, at % POOL_COLS
    picked = ((y // 4 == p) & (q == 0)) | (((y - 128) // 4 == p) & (y >= 128) & (q == POOL_COLS - 1))
    col_sums = mm(value, jnp.where(picked, 1.0 / 16, 0.0).astype(BF16))
    for p in range(POOL_ROWS):
        at = p * POOL_COLS
        near = sums_low if p < POOL_ROWS // 2 else sums_high
        first = at % (SPOTS // 2)
        total = near[:, first : first + POOL_COLS] + col_sums[:, at : at + POOL_COLS]
        if p == 0:
            total += row_sums[0]
        if p == POOL_ROWS - 1:
            total += row_sums[1]
        pooled[:, at : at + POOL_COLS] = total.astype(BF16)


def merge_kernel(low, high, rim_rows, rim_cols, features):
    lane = iota((CH, 128), 1)
    columns = rim_cols[...].astype(F32)
    for y in range(ROWS):
        if y == 0:
            f = rim_rows[0:CH, :]
        elif y == ROWS - 1:
            f = rim_rows[CH : 2 * CH, :]
        else:
            source = low if y < HALF else high
            at = y % HALF * CH
            f = source[at : at + CH, :]
        f = f.astype(F32)
        first = jnp.where(lane == 0, columns[:, y : y + 1], f[:, :128])
        last = jnp.where(lane == 127, columns[:, 128 + y : 129 + y], f[:, COLS - 128 :])
        f = jnp.concatenate([first, f[:, 128 : COLS - 128], last], axis=1)
        features[y * CH : (y + 1) * CH, :] = f.astype(BF16)


MAPS = {
    (0, -2): ("band", 0), (0, -1): ("band", 1), (0, 0): ("own", 0), (0, 1): ("own", 1), (0, 2): ("band_p", 1),
    (-1, -2): ("one", 0), (-1, -1): ("one", 1), (-1, 0): ("relay_p", 0), (-1, 1): ("relay_p", 1), (-1, 2): ("two_p", 1),
    (1, -2): ("two", 0), (1, -1): ("two", 1), (1, 0): ("relay", 1), (1, 1): ("relay", 0), (1, 2): ("one_p", 1),
}
NAMES = ("own", "band", "band_p", "one", "one_p", "two", "two_p", "relay", "relay_p")


def logits_kernel(
    cells, place, features, own, band_m, band_p, one_m, one_p, two_m, two_p, relay, relay_p,
    proj_w, proj_b, ctx_w, up_w, up_b, head_w, rim_w, head_b,
    logits, col_out, row_out, weights, proj, low_up, lifted, decoded,
):
    arrays = dict(zip(NAMES, (own, band_m, band_p, one_m, one_p, two_m, two_p, relay, relay_p)))
    last_cross, last_band = cells
    cross, band = place[0], place[1]
    core = band % 2
    sign = 1 - 2 * core
    maps = []

    for at in range(15):
        u, v = at // 5 - 1, at % 5 - 2
        maps.append(MAPS[(u, v)])
        row, col = cross + u * sign, band + v * sign
        inside = (row >= 0) & (row <= last_cross) & (col >= 0) & (col <= last_band)
        one = ctx_w[:, at * WIDE : (at + 1) * WIDE]
        two = ctx_w[:, (14 - at) * WIDE : (15 - at) * WIDE]
        chosen = jnp.where(core == 0, one, two)
        weights[:, at * WIDE : (at + 1) * WIDE] = jnp.where(inside, chosen, jnp.zeros_like(chosen))

    p_bias = jnp.broadcast_to(column(proj_b[...]), (WIDE, 256))
    u_bias = jnp.broadcast_to(column(up_b[...]), (CH, 256))

    def context_part(part, carry):
        at = pl.multiple_of(part * 256, 256)
        for k in range(15):
            name, half = maps[k]
            out = mm(proj_w[...], arrays[name][half, :, pl.ds(at, 256)])
            proj[k * WIDE : (k + 1) * WIDE, :] = jnp.maximum(out + p_bias, 0.0).astype(BF16)
        context = mm(weights[...], proj[...]) + proj[7 * WIDE : 8 * WIDE, :].astype(F32)
        mixed = jnp.maximum(context, 0.0).astype(BF16)
        up = mm(up_w[...], mixed) + u_bias
        high = up.astype(BF16)
        low = (up - high.astype(F32)).astype(BF16)
        both = [
            jnp.concatenate([high[:, h * 128 : (h + 1) * 128], low[:, h * 128 : (h + 1) * 128]], axis=1)
            for h in range(2)
        ]
        low_up[pl.ds(pl.multiple_of(part * 64, 64), 64), :] = jnp.concatenate(both, axis=0)
        return carry

    lax.fori_loop(0, SPOTS // 256, context_part, 0)

    widen = jnp.where(
        iota((256, COLS), 0) % 128 == iota((256, COLS), 1) // 4, 1.0, 0.0
    ).astype(BF16)
    lifted[...] = mm(low_up[...], widen)

    decoded[0:64, :] = jnp.zeros((64, COLS), BF16)
    decoded[66 * CH :, :] = jnp.zeros((64, COLS), BF16)

    def decode(p, carry):
        up = lifted[pl.ds(pl.multiple_of(p * CH, CH), CH), :]
        for r in range(4):
            at = pl.multiple_of((4 * p + r) * CH, CH)
            value = jnp.maximum(features[pl.ds(at, CH), :].astype(F32) + up, 0.0).astype(BF16)
            decoded[pl.ds(pl.multiple_of(at + 64, CH), CH), :] = value
        return carry

    lax.fori_loop(0, POOL_ROWS, decode, 0)

    def gather_taps(z, count):
        total = None
        for dx in range(5):
            part = z[dx * count : (dx + 1) * count, :]
            part = jnp.concatenate([part, jnp.zeros((count, 128), F32)], axis=1)
            if dx != 2:
                part = pltpu.roll(part, (dx - 2) % 640, 1)
            total = part if total is None else total + part
        return total

    lane16 = iota((16, 128), 1)
    first_lanes = (lane16 < 2) | (lane16 >= 126)

    def head(block, carry):
        first = pl.multiple_of(block * 16 * CH, 16 * CH)
        total = gather_taps(mm(head_w[...], decoded[pl.ds(first, 20 * CH), :]), 32)
        y = pl.multiple_of(block * 16, 16)
        for k in range(2):
            logits[k, pl.ds(y, 16), :] = total[k * 16 : (k + 1) * 16, :COLS] + head_b[k]
        rim = total[:, COLS:]
        col_out[pl.ds(y, 16), :] = jnp.where(first_lanes, rim[:16], pltpu.roll(rim[16:], 4, 1))
        return carry

    lax.fori_loop(0, ROWS // 16, head, 0)

    ends = jnp.concatenate([decoded[64:128, :], decoded[64 * CH : 66 * CH, :]], axis=0)
    total = gather_taps(mm(rim_w[...], ends), 8)
    row_out[...] = total[:, :COLS]
    col_out[ROWS : ROWS + 8, :] = total[:, COLS:]


def row_sum_kernel(cells, place, row_out, partner, outer, out):
    _, _, has_left, has_right = flags(place, *cells)
    corners = slice(ROWS, ROWS + 8)
    left, right = sides(place, partner, outer, corners, corners)
    lane = iota((8, 128), 1)
    out[...] = row_out[...] + jnp.concatenate(
        [
            jnp.where(lane < 2, left * has_left, 0.0),
            jnp.zeros((8, COLS - 256), F32),
            jnp.where(lane >= 126, right * has_right, 0.0),
        ],
        axis=1,
    )


def sum_kernel(cells, place, inner, partner, outer, even_message, odd_message, out):
    has_above, has_below, has_left, has_right = flags(place, *cells)
    even = place[0] % 2 == 0
    above = jnp.where(even, odd_message[...], even_message[...]) * has_above
    below = jnp.where(even, even_message[...], odd_message[...]) * has_below
    left, right = sides(place, partner, outer, slice(0, ROWS), slice(0, ROWS))
    left, right = left * has_left, right * has_right
    out[...] = inner[...]
    lane = iota((ROWS, 128), 1)
    for k in range(2):
        low = left if k == 0 else pltpu.roll(left, 124, 1)
        out[k, :, 0:128] += jnp.where(lane < 2, low, 0.0)
        high = right if k == 0 else pltpu.roll(right, 124, 1)
        out[k, :, COLS - 128 : COLS] += jnp.where(lane >= 126, high, 0.0)
        out[k, 0:2, :] += above[4 * k + 2 : 4 * k + 4]
        out[k, ROWS - 2 : ROWS, :] += below[4 * k : 4 * k + 2]


def call(kernel, outs, args, scratch=(), smem=(0,), flops=0):
    return pl.pallas_call(
        kernel,
        out_shape=outs,
        in_specs=[SMEM if at in smem else VMEM for at in range(len(args))],
        out_specs=jax.tree.map(lambda _: VMEM, outs),
        scratch_shapes=list(scratch),
        compiler_params=pltpu.CompilerParams(vmem_limit_bytes=56 * 1024 * 1024),
        cost_estimate=pl.CostEstimate(flops=flops, bytes_accessed=1 << 20, transcendentals=0),
    )(*args)


def body(
    n_cross, n_band, rasters, aerial, w_in, aerial_gain, b_in, w_conv1, b_conv1, w_proj, b_proj,
    w_ctx, w_up, b_up, w_head, b_head,
):
    cells = (n_cross - 1, n_band - 1)
    place = jnp.stack([lax.axis_index("cross"), lax.axis_index("band")]).astype(jnp.int32)

    def moved(x, source):
        route = []
        for cross in range(n_cross):
            for band in range(n_band):
                c, b = source(cross, band)
                route.append(((b % n_band) * n_cross + c % n_cross, band * n_cross + cross))
        return lax.ppermute(x, ("band", "cross"), route)

    def partner(x):
        return moved(x, lambda c, b: (c, b ^ 1))

    def outer(x):
        return moved(x, lambda c, b: (c, ((b + 1) ^ 1) - 1))

    def even_pair(x):
        return moved(x, lambda c, b: (c ^ 1, b))

    def odd_pair(x):
        return moved(x, lambda c, b: (((c + 1) ^ 1) - 1, b))

    def beside(x, u):
        return moved(x, lambda c, b: (c + u * (1 - 2 * (b % 2)), b - 2 + 4 * (b % 2)))

    rows, cols, message = call(
        halo_kernel,
        [shape_of(32, COLS), shape_of(32, 128), shape_of(16, 128)],
        [rasters, aerial],
        smem=(),
    )
    near, far = partner(message), outer(message)

    gain = aerial_gain[:, None]
    kinds_8 = jnp.concatenate([w_in, gain, gain, b_in[:, None], jnp.zeros_like(gain)], axis=1)
    kinds_5 = jnp.concatenate([w_in, gain, b_in[:, None], jnp.zeros((CH, 2), F32)], axis=1)
    conv_b = b_conv1[None, :]

    def inner(half):
        return call(
            functools.partial(inner_kernel, half),
            [shape_of(HALF * CH, COLS, dtype=BF16), shape_of(CH, SPOTS // 2)],
            [rasters, aerial, kinds_8, w_conv1, conv_b],
            [
                pltpu.VMEM((256, 128), BF16),
                pltpu.VMEM((256, 960), BF16),
                pltpu.VMEM(((HALF + 2) * 96, COLS), BF16),
            ],
            smem=(),
            flops=4 * 10**9,
        )

    feat_low, sums_low = inner(0)
    even_out, odd_out = call(
        functools.partial(row_message_kernel, cells), [shape_of(8, COLS + 128)] * 2, [place, rows, near, far]
    )
    even_in, odd_in = even_pair(even_out), odd_pair(odd_out)
    feat_high, sums_high = inner(1)

    taps = w_head.reshape(2, 5, 5, CH)[:, ::-1].transpose(2, 0, 1, 3).reshape(10, 5 * CH)
    skewed = jnp.broadcast_to(jnp.pad(taps, ((0, 0), (0, 16 * CH)))[:, None, :], (10, 16, 21 * CH))
    head_w = skewed.reshape(10, 16 * 21 * CH)[:, : 16 * 20 * CH].reshape(160, 20 * CH)
    gap = jnp.zeros((10, CH), BF16)
    at = [taps[:, (4 - d) * CH : (5 - d) * CH] for d in range(5)]
    ends = [[at[0], gap, gap, gap], [at[1], at[0], gap, gap], [gap, gap, at[4], at[3]], [gap, gap, gap, at[4]]]
    rim_w = jnp.stack([jnp.concatenate(r, axis=1) for r in ends], axis=1).reshape(40, 4 * CH)
    head_w, rim_w, rows = lax.optimization_barrier((head_w, rim_w, rows))

    rim_rows, rim_cols, pooled = call(
        functools.partial(rim_kernel, cells),
        [shape_of(2 * CH, COLS, dtype=BF16), shape_of(CH, 256, dtype=BF16), shape_of(CH, SPOTS, dtype=BF16)],
        [place, rows, cols, near, far, even_in, odd_in, sums_low, sums_high, kinds_5, w_conv1, conv_b],
    )

    own = jnp.stack([pooled, partner(pooled)])
    one = beside(own, -1)
    band = beside(own, 0)
    two = beside(own, 1)
    relay = outer(one)
    maps = [own, band, partner(band), one, partner(one), two, partner(two), relay, partner(relay)]

    features = call(
        merge_kernel, shape_of(ROWS * CH, COLS, dtype=BF16), [feat_low, feat_high, rim_rows, rim_cols], smem=(),
        flops=10**9,
    )
    inner_logits, col_out, row_out = call(
        functools.partial(logits_kernel, cells),
        [shape_of(2, ROWS, COLS), shape_of(ROWS + 8, 128), shape_of(8, COLS)],
        [place, features, *maps, w_proj, b_proj[None, :], w_ctx, w_up, b_up[None, :], head_w, rim_w, b_head],
        [
            pltpu.VMEM((WIDE, 15 * WIDE), BF16),
            pltpu.VMEM((15 * WIDE, 256), BF16),
            pltpu.VMEM((POOL_ROWS * CH, 256), BF16),
            pltpu.VMEM((POOL_ROWS * CH, COLS), F32),
            pltpu.VMEM(((ROWS + 4) * CH, COLS), BF16),
        ],
        smem=(0, 18),
    )
    near, far = partner(col_out), outer(col_out)
    row_out = call(
        functools.partial(row_sum_kernel, cells), shape_of(8, COLS), [place, row_out, near, far]
    )
    return call(
        functools.partial(sum_kernel, cells),
        shape_of(2, ROWS, COLS),
        [place, inner_logits, near, far, even_pair(row_out), odd_pair(row_out)],
    )


def solution(mesh):
    sizes = dict(mesh.shape)
    return jax.shard_map(
        functools.partial(body, sizes["cross"], sizes["band"]),
        mesh=mesh,
        in_specs=(P(None, "cross", "band"), P("cross", "band")) + (P(),) * 12,
        out_specs=P(None, "cross", "band"),
        check_vma=False,
    )
```

```python
import functools

import jax
import jax.numpy as jnp
from jax import lax
from jax.experimental import pallas as pl
from jax.experimental.pallas import tpu as pltpu
from jax.sharding import PartitionSpec as P

ROWS, COLS = 64, 512
CH, WIDE, KINDS = 32, 128, 8
POOL_ROWS, POOL_COLS = 16, 128
SPOTS = POOL_ROWS * POOL_COLS
HALF = ROWS // 2
HBM = pl.BlockSpec(memory_space=pltpu.HBM)
VMEM = pl.BlockSpec(memory_space=pltpu.VMEM)
SMEM = pl.BlockSpec(memory_space=pltpu.SMEM)
F32, BF16 = jnp.float32, jnp.bfloat16


def iota(shape, dim):
    return lax.broadcasted_iota(jnp.int32, shape, dim)


def shape_of(*dims, dtype=F32):
    return jax.ShapeDtypeStruct(dims, dtype)


def mm(a, b):
    return jnp.dot(a, b, preferred_element_type=F32)


def split(x):
    high = x.astype(BF16)
    return high, (x - high.astype(F32)).astype(BF16)


def column(row):
    count = row.shape[1]
    eye = iota((count, count), 0) == iota((count, count), 1)
    return jnp.sum(jnp.where(eye, row, 0.0), axis=1, keepdims=True)


def placed():
    return lax.axis_index("cross"), lax.axis_index("band")


def flags(last_cross, last_band):
    cross, band = placed()
    one = lambda truth: truth.astype(F32)
    return one(cross > 0), one(cross < last_cross), one(band > 0), one(band < last_band)


def kinds_of(w_in, gain, b_in, gains):
    lane = iota((CH, KINDS), 1)
    kinds = jnp.zeros((CH, KINDS), F32)
    parts = [w_in[k : k + 1, :] for k in range(4)] + [gain[...]] * gains + [b_in[...]]
    parts = [column(part) for part in parts]
    for kind, part in enumerate(parts):
        kinds = jnp.where(lane == kind, part, kinds)
    return kinds


def pool_weights():
    x, q = iota((COLS, POOL_COLS), 0), iota((COLS, POOL_COLS), 1)
    inner = (x // 4 == q) & (x > 0) & (x < COLS - 1)
    return jnp.where(inner, 1.0 / 16, 0.0).astype(BF16)


def halo_kernel(rasters, aerial, rows, cols, message, stem_in):
    ones, none = jnp.ones((1, COLS), F32), jnp.zeros((2, COLS), F32)
    for at, y in enumerate((0, 1, ROWS - 2, ROWS - 1)):
        parts = [rasters[kind, y : y + 1, :].astype(F32) for kind in range(4)]
        rows[at * 8 : (at + 1) * 8, :] = jnp.concatenate(parts + [aerial[y : y + 1, :], ones, none], axis=0)
    lane = iota((ROWS, 128), 1)
    packed = jnp.where((lane < 32) & (lane % 8 == 5), 1.0, 0.0)
    for at, x in enumerate((0, 1, COLS - 2, COLS - 1)):
        first = x // 128 * 128
        for kind in range(5):
            if kind < 4:
                slab = rasters[kind, :, first : first + 128].astype(F32)
            else:
                slab = aerial[:, first : first + 128]
            packed = jnp.where(lane == at * 8 + kind, slab[:, x - first : x - first + 1], packed)
    turned = jnp.transpose(jnp.concatenate([packed, jnp.zeros((128 - ROWS, 128), F32)], axis=0))
    cols[...] = turned[:32]
    message[...] = jnp.concatenate([turned[:8], turned[24:32]], axis=0)
    for y in range(0, ROWS, 8):
        values = jnp.concatenate([rasters[k, y : y + 8, :] for k in range(4)], axis=0).astype(F32)
        high, low = split(aerial[y : y + 8, :])
        tail = jnp.concatenate([jnp.ones((8, COLS), BF16), jnp.zeros((8, COLS), BF16)], axis=0)
        stem_in[y * 8 : y * 8 + 64, :] = jnp.concatenate([values.astype(BF16), high, low, tail], axis=0)


def sides(partner, outer, low, high):
    even = placed()[1] % 2 == 0
    left = jnp.where(even, outer[high], partner[high])
    right = jnp.where(even, partner[low], outer[low])
    return left, right


def row_messages(cells, rows, partner, outer):
    _, _, has_left, has_right = flags(*cells)
    left, right = sides(partner, outer, slice(0, 8), slice(8, 16))
    lane = lax.broadcasted_iota(jnp.int32, (8, 128), 1)

    def row(at, y):
        low, high = left[:, y : y + 1] * has_left, right[:, y : y + 1] * has_right
        side = jnp.where(lane == 0, high, jnp.where(lane == 1, low, 0.0))
        return jnp.concatenate([rows[at * 8 : (at + 1) * 8, :], side], axis=1)

    low, high = row(0, 0), row(3, ROWS - 1)
    even = placed()[0] % 2 == 0
    return jnp.where(even, high, low), jnp.where(even, low, high)


def inner_kernel(
    half, stem_in, w_in, gain, b_in, conv_w, conv_b, features, sums, stem_w, wide_w, stem3
):
    spread = jnp.where(iota((KINDS, 64), 1) // 8 == iota((KINDS, 64), 0), 1.0, 0.0).astype(BF16)
    same = iota((256, 64), 0) // CH == iota((256, 64), 1) % 8
    halves = []
    for part in split(kinds_of(w_in, gain, b_in, 2)):
        rows = mm(jnp.concatenate([part] * 8, axis=0), spread)
        halves.append(jnp.where(same, rows, 0.0))
    stem_w[...] = jnp.concatenate(halves, axis=1).astype(BF16)
    wide_w[...] = jnp.zeros(wide_w.shape, BF16)
    taps = conv_w[...]
    for y in range(8):
        wide_w[y * CH : (y + 1) * CH, y * 96 : y * 96 + 288] = taps
    pool_w = pool_weights()
    bias = jnp.broadcast_to(column(conv_b[...]), (CH, COLS))
    bias = jnp.concatenate([bias] * 8, axis=0)

    blocks = range(5) if half == 0 else range(3, 8)
    base = half * HALF - 1
    edge = 0 if half == 0 else HALF + 1
    stem3[edge * 96 : (edge + 1) * 96, :] = jnp.zeros((96, COLS), BF16)
    for block in blocks:
        y = block * 8
        x = stem_in[y * 8 : y * 8 + 64, :]
        out = jnp.maximum(mm(stem_w[...], jnp.concatenate([x, x], axis=0)), 0.0)
        for r in range(8):
            at = y + r - base
            if at < 0 or at > HALF + 1:
                continue
            s = out[r * CH : (r + 1) * CH, :]
            parts = [pltpu.roll(s, 1, 1), s, pltpu.roll(s, COLS - 1, 1)]
            stem3[at * 96 : (at + 1) * 96, :] = jnp.concatenate(parts, axis=0).astype(BF16)

    for block in range(HALF // 8):
        out = mm(wide_w[...], stem3[block * 768 : block * 768 + 960, :])
        value = jnp.maximum(out + bias, 0.0).astype(BF16)
        features[block * 256 : (block + 1) * 256, :] = value
        means = mm(value, pool_w)
        for p in range(2):
            rows = [means[p * 128 + r * 32 : p * 128 + (r + 1) * 32, :] for r in range(4)]
            if half == 0 and block == 0 and p == 0:
                rows = rows[1:]
            if half == 1 and block == HALF // 8 - 1 and p == 1:
                rows = rows[:3]
            at = (block * 2 + p) * POOL_COLS
            sums[:, at : at + POOL_COLS] = sum(rows[1:], rows[0])


def rim_kernel(
    cells, rows, cols, partner, outer, even_message, odd_message, sums_low, sums_high,
    w_in, gain, b_in, conv_w, conv_b, rim_rows, rim_cols, pooled,
):
    has_above, has_below, has_left, has_right = flags(*cells)
    left, right = sides(partner, outer, slice(0, 8), slice(8, 16))
    left, right = left * has_left, right * has_right
    even = placed()[0] % 2 == 0
    above = jnp.where(even, odd_message[...], even_message[...]) * has_above
    below = jnp.where(even, even_message[...], odd_message[...]) * has_below
    kind_high, kind_low = split(kinds_of(w_in, gain, b_in, 1))
    stem_w = jnp.concatenate([kind_high, kind_high, kind_low], axis=1)
    bias = column(conv_b[...])

    def stem(x):
        high, low = split(x)
        high = high.astype(F32)
        stacked = jnp.concatenate([high, low.astype(F32), high], axis=0).astype(BF16)
        return jnp.maximum(mm(stem_w, stacked), 0.0)

    def conv(stacked):
        return jnp.maximum(mm(conv_w[...], stacked) + bias, 0.0).astype(BF16)

    def row(at):
        return rows[at * 8 : (at + 1) * 8, :]

    pool_w = pool_weights()
    row_sums = []
    trios = [(above[:, :COLS], row(0), row(1)), (row(2), row(3), below[:, :COLS])]
    for at, trio in enumerate(trios):
        stacked = []
        for x in trio:
            s = stem(x)
            stacked += [pltpu.roll(s, 1, 1), s, pltpu.roll(s, COLS - 1, 1)]
        value = conv(jnp.concatenate(stacked, axis=0).astype(BF16))
        rim_rows[at * CH : (at + 1) * CH, :] = value
        row_sums.append(mm(value, pool_w))

    lane = iota((8, 128), 1)

    def line(inside, top, bottom, x):
        top, bottom = top[:, x : x + 1], bottom[:, x : x + 1]
        return jnp.where(lane < ROWS, inside, jnp.where(lane == ROWS, bottom, 0.0)), top

    x_of = {-1: COLS + 1, COLS: COLS}
    lines = {-1: left, COLS: right}
    for at, x in enumerate((0, 1, COLS - 2, COLS - 1)):
        lines[x] = cols[at * 8 : (at + 1) * 8, :]
    columns = []
    for dx in (-1, 0, 1):
        low, low_top = line(lines[dx], above, below, x_of.get(dx, dx))
        x = COLS - 1 + dx
        high, high_top = line(lines[x], above, below, x_of.get(x, x))
        low = jnp.where(lane == 127, high_top, low)
        high = jnp.where(lane == 127, low_top, high)
        columns.append(stem(jnp.concatenate([low, high], axis=1)))
    s = jnp.concatenate(columns, axis=0)
    stacked = [pltpu.roll(s, 1, 1), s, pltpu.roll(s, 255, 1)]
    value = conv(jnp.concatenate(stacked, axis=0).astype(BF16))
    rim_cols[...] = value
    y, at = iota((256, 128), 0), iota((256, 128), 1)
    picked = (y < ROWS) & (y // 4 == at) | (y >= 128) & (y < 128 + ROWS) & (y // 4 - 16 == at)
    col_sums = mm(value, jnp.where(picked, 1.0 / 16, 0.0).astype(BF16))
    lane = iota((CH, POOL_COLS), 1)
    for p in range(POOL_ROWS):
        at = p * POOL_COLS
        near = sums_low if p < POOL_ROWS // 2 else sums_high
        first = at % (SPOTS // 2)
        last = jnp.where(lane == POOL_COLS - 1, col_sums[:, 16 + p : 17 + p], 0.0)
        total = near[:, first : first + POOL_COLS] + jnp.where(lane == 0, col_sums[:, p : p + 1], last)
        if p == 0:
            total += row_sums[0]
        if p == POOL_ROWS - 1:
            total += row_sums[1]
        pooled[0, :, at : at + POOL_COLS] = total.astype(BF16)
    pooled[1, :, :] = jnp.zeros((CH, SPOTS), BF16)


def head_weights(w_head, row_y, row_count, col_y, col_count):
    shape = (10 * row_count, col_count * CH)
    rows = iota((10 * row_count, 2), 0) // row_count % 2 == iota((10 * row_count, 2), 1)
    pick = jnp.where(rows, 1.0, 0.0).astype(BF16)
    dx = iota((10 * row_count, 160), 0) // (2 * row_count) == iota((10 * row_count, 160), 1) // CH
    repeat = iota((160, shape[1]), 0) % CH == iota((160, shape[1]), 1) % CH
    repeat = jnp.where(repeat, 1.0, 0.0).astype(BF16)
    dy = row_y(iota(shape, 0) % row_count) - col_y(iota(shape, 1) // CH)
    total = jnp.zeros(shape, F32)
    for tap in range(5):
        taps = mm(pick, w_head[:, tap * 160 : (tap + 1) * 160])
        taps = mm(jnp.where(dx, taps, 0.0).astype(BF16), repeat)
        total = jnp.where(dy == tap - 2, taps, total)
    return total.astype(BF16)


def merge_kernel(low, high, rim_rows, rim_cols, w_head, features, head_w, rim_w):
    head_w[...] = head_weights(w_head[...], lambda r: r, 16, lambda r: r - 2, 20)
    outside = lambda r: jnp.where(r < 2, r - 2, ROWS - 2 + r)
    rim_w[...] = head_weights(w_head[...], outside, 4, lambda r: jnp.where(r < 2, r, ROWS - 4 + r), 4)
    lane = iota((CH, 128), 1)
    columns = rim_cols[...].astype(F32)
    for y in range(ROWS):
        if y == 0:
            f = rim_rows[0:CH, :]
        elif y == ROWS - 1:
            f = rim_rows[CH : 2 * CH, :]
        else:
            source = low if y < HALF else high
            at = y % HALF * CH
            f = source[at : at + CH, :]
        f = f.astype(F32)
        first = jnp.where(lane == 0, columns[:, y : y + 1], f[:, :128])
        last = jnp.where(lane == 127, columns[:, 128 + y : 129 + y], f[:, COLS - 128 :])
        f = jnp.concatenate([first, f[:, 128 : COLS - 128], last], axis=1)
        features[y * CH : (y + 1) * CH, :] = f.astype(BF16)


MAPS = {
    (0, -2): ("band", 0), (0, -1): ("band", 1), (0, 0): ("own", 0), (0, 1): ("own", 1), (0, 2): ("band_p", 1),
    (-1, -2): ("one", 0), (-1, -1): ("one", 1), (-1, 0): ("relay_p", 0), (-1, 1): ("relay_p", 1), (-1, 2): ("two_p", 1),
    (1, -2): ("two", 0), (1, -1): ("two", 1), (1, 0): ("relay", 1), (1, 1): ("relay", 0), (1, 2): ("one_p", 1),
}
NAMES = ("own", "band", "band_p", "one", "one_p", "two", "two_p", "relay", "relay_p")


EARLY = [at for at in range(15) if MAPS[(at // 5 - 1, at % 5 - 2)][0] in NAMES[:4]]
LATE = [at for at in range(15) if at not in EARLY]


def context_sum(cells, which, arrays, proj_w, proj_b, ctx_w, weights, proj, finish):
    last_cross, last_band = cells
    cross, band = placed()
    core = band % 2
    sign = 1 - 2 * core
    for k, at in enumerate(which):
        row, col = cross + (at // 5 - 1) * sign, band + (at % 5 - 2) * sign
        inside = (row >= 0) & (row <= last_cross) & (col >= 0) & (col <= last_band)
        one = ctx_w[:, at * WIDE : (at + 1) * WIDE]
        two = ctx_w[:, (14 - at) * WIDE : (15 - at) * WIDE]
        chosen = jnp.where(core == 0, one, two)
        weights[:, k * WIDE : (k + 1) * WIDE] = jnp.where(inside, chosen, jnp.zeros_like(chosen))
    p_bias = jnp.broadcast_to(column(proj_b[...]), (WIDE, 256))

    def part(at, carry):
        spots = pl.ds(pl.multiple_of(at * 256, 256), 256)
        for k, tile in enumerate(which):
            name, half = MAPS[(tile // 5 - 1, tile % 5 - 2)]
            out = mm(proj_w[...], arrays[name][half, :, spots])
            proj[k * WIDE : (k + 1) * WIDE, :] = jnp.maximum(out + p_bias, 0.0).astype(BF16)
        finish(at, spots, mm(weights[...], proj[...]))
        return carry

    lax.fori_loop(0, SPOTS // 256, part, 0, unroll=True)


def early_kernel(cells, *refs):
    arrays = dict(zip(NAMES[:4], refs[:4]))
    proj_w, proj_b, ctx_w, context, weights, proj = refs[4:]
    own = EARLY.index(7)

    def finish(at, spots, total):
        context[:, spots] = total + proj[own * WIDE : (own + 1) * WIDE, :].astype(F32)

    context_sum(cells, EARLY, arrays, proj_w, proj_b, ctx_w, weights, proj, finish)


def logits_kernel(
    cells, features, context, one_p, two_m, two_p, relay, relay_p,
    proj_w, proj_b, ctx_w, up_w, up_b, head_w, rim_w, head_b,
    logits, col_out, row_out, weights, proj, low_up, lifted, decoded,
):
    arrays = dict(zip(NAMES[4:], (one_p, two_m, two_p, relay, relay_p)))
    u_bias = jnp.broadcast_to(column(up_b[...]), (CH, 256))

    def finish(part, spots, total):
        mixed = jnp.maximum(total + context[:, spots], 0.0).astype(BF16)
        up = mm(up_w[...], mixed) + u_bias
        high, low = split(up)
        both = [
            jnp.concatenate([high[:, h * 128 : (h + 1) * 128], low[:, h * 128 : (h + 1) * 128]], axis=1)
            for h in range(2)
        ]
        low_up[pl.ds(pl.multiple_of(part * 64, 64), 64), :] = jnp.concatenate(both, axis=0)

    context_sum(cells, LATE, arrays, proj_w, proj_b, ctx_w, weights, proj, finish)

    widen = jnp.where(
        iota((256, COLS), 0) % 128 == iota((256, COLS), 1) // 4, 1.0, 0.0
    ).astype(BF16)
    lifted[...] = mm(low_up[...], widen)

    decoded[0:64, :] = jnp.zeros((64, COLS), BF16)
    decoded[66 * CH :, :] = jnp.zeros((64, COLS), BF16)

    def decode(p, carry):
        up = lifted[pl.ds(pl.multiple_of(p * CH, CH), CH), :]
        for r in range(4):
            at = pl.multiple_of((4 * p + r) * CH, CH)
            value = jnp.maximum(features[pl.ds(at, CH), :].astype(F32) + up, 0.0).astype(BF16)
            decoded[pl.ds(pl.multiple_of(at + 64, CH), CH), :] = value
        return carry

    lax.fori_loop(0, POOL_ROWS, decode, 0, unroll=4)

    def gather_taps(z, count):
        total = None
        for dx in range(5):
            part = z[dx * count : (dx + 1) * count, :]
            part = jnp.concatenate([part, jnp.zeros((count, 128), F32)], axis=1)
            if dx != 2:
                part = pltpu.roll(part, (dx - 2) % 640, 1)
            total = part if total is None else total + part
        return total

    lane16 = iota((16, 128), 1)
    first_lanes = (lane16 < 2) | (lane16 >= 126)

    def head(block, carry):
        first = pl.multiple_of(block * 16 * CH, 16 * CH)
        total = gather_taps(mm(head_w[...], decoded[pl.ds(first, 20 * CH), :]), 32)
        y = pl.multiple_of(block * 16, 16)
        for k in range(2):
            logits[k, pl.ds(y, 16), :] = total[k * 16 : (k + 1) * 16, :COLS] + head_b[k]
        rim = total[:, COLS:]
        col_out[pl.ds(y, 16), :] = jnp.where(first_lanes, rim[:16], pltpu.roll(rim[16:], 4, 1))
        return carry

    lax.fori_loop(0, ROWS // 16, head, 0, unroll=True)

    ends = jnp.concatenate([decoded[64:128, :], decoded[64 * CH : 66 * CH, :]], axis=0)
    total = gather_taps(mm(rim_w[...], ends), 8)
    row_out[...] = total[:, :COLS]
    col_out[ROWS : ROWS + 8, :] = total[:, COLS:]


def row_sums(cells, row_out, partner, outer):
    _, _, has_left, has_right = flags(*cells)
    corners = slice(ROWS, ROWS + 8)
    left, right = sides(partner, outer, corners, corners)
    lane = lax.broadcasted_iota(jnp.int32, (8, 128), 1)
    low = jnp.where(lane < 2, left * has_left, 0.0)
    high = jnp.where(lane >= 126, right * has_right, 0.0)
    return row_out + jnp.concatenate([low, jnp.zeros((8, COLS - 256), F32), high], axis=1)


def sum_kernel(cells, inner, partner, outer, even_message, odd_message, out):
    has_above, has_below, has_left, has_right = flags(*cells)
    even = placed()[0] % 2 == 0
    above = jnp.where(even, odd_message[...], even_message[...]) * has_above
    below = jnp.where(even, even_message[...], odd_message[...]) * has_below
    left, right = sides(partner, outer, slice(0, ROWS), slice(0, ROWS))
    left, right = left * has_left, right * has_right
    out[...] = inner[...]
    lane = iota((ROWS, 128), 1)
    for k in range(2):
        low = left if k == 0 else pltpu.roll(left, 124, 1)
        out[k, :, 0:128] += jnp.where(lane < 2, low, 0.0)
        high = right if k == 0 else pltpu.roll(right, 124, 1)
        out[k, :, COLS - 128 : COLS] += jnp.where(lane >= 126, high, 0.0)
        out[k, 0:2, :] += above[4 * k + 2 : 4 * k + 4]
        out[k, ROWS - 2 : ROWS, :] += below[4 * k : 4 * k + 2]


def call(kernel, outs, args, scratch=(), smem=(), hbm=(), flops=0):
    scratch = list(scratch)

    def fetching(*refs):
        ins, rest = list(refs[: len(args)]), refs[len(args) :]
        buffers, sems = rest[-len(hbm) - 1 : -1], rest[-1]
        copies = [pltpu.make_async_copy(ins[at], buffers[i], sems.at[i]) for i, at in enumerate(hbm)]
        for copy in copies:
            copy.start()
        for copy in copies:
            copy.wait()
        for at, buffer in zip(hbm, buffers):
            ins[at] = buffer
        kernel(*ins, *rest[: -len(hbm) - 1])

    if hbm:
        scratch += [pltpu.VMEM(args[at].shape, args[at].dtype) for at in hbm]
        scratch += [pltpu.SemaphoreType.DMA((len(hbm),))]
    return pl.pallas_call(
        fetching if hbm else kernel,
        out_shape=outs,
        in_specs=[SMEM if at in smem else HBM if at in hbm else VMEM for at in range(len(args))],
        out_specs=jax.tree.map(lambda _: VMEM, outs),
        scratch_shapes=scratch,
        compiler_params=pltpu.CompilerParams(vmem_limit_bytes=24 * 1024 * 1024),
        cost_estimate=pl.CostEstimate(flops=flops, bytes_accessed=1 << 20, transcendentals=0),
    )(*args)


def body(
    n_cross, n_band, rasters, aerial, w_in, aerial_gain, b_in, w_conv1, b_conv1, w_proj, b_proj,
    w_ctx, w_up, b_up, w_head, b_head,
):
    cells = (n_cross - 1, n_band - 1)
    tie = lax.optimization_barrier

    def moved(x, source):
        route = []
        for cross in range(n_cross):
            for band in range(n_band):
                c, b = source(cross, band)
                route.append(((b % n_band) * n_cross + c % n_cross, band * n_cross + cross))
        return lax.ppermute(x, ("band", "cross"), route)

    def partner(x):
        return moved(x, lambda c, b: (c, b ^ 1))

    def outer(x):
        return moved(x, lambda c, b: (c, ((b + 1) ^ 1) - 1))

    def even_pair(x):
        return moved(x, lambda c, b: (c ^ 1, b))

    def odd_pair(x):
        return moved(x, lambda c, b: (((c + 1) ^ 1) - 1, b))

    def beside(x, u):
        return moved(x, lambda c, b: (c + u * (1 - 2 * (b % 2)), b - 2 + 4 * (b % 2)))

    rows, cols, message, stem_in = call(
        halo_kernel,
        [shape_of(32, COLS), shape_of(32, 128), shape_of(16, 128), shape_of(8 * ROWS, COLS, dtype=BF16)],
        [rasters, aerial],
        flops=2 * 10**10,
    )
    near, far = partner(message), outer(message)

    stem_args = [w_in.T, aerial_gain[None, :], b_in[None, :], w_conv1, b_conv1[None, :]]
    proj_args = [w_proj, b_proj[None, :], w_ctx]

    def inner(half, stem_in):
        return call(
            functools.partial(inner_kernel, half),
            [shape_of(HALF * CH, COLS, dtype=BF16), shape_of(CH, SPOTS // 2)],
            [stem_in, *stem_args],
            [
                pltpu.VMEM((256, 128), BF16),
                pltpu.VMEM((256, 960), BF16),
                pltpu.VMEM(((HALF + 2) * 96, COLS), BF16),
            ],
            flops=4 * 10**9,
        )

    feat_low, sums_low = inner(0, stem_in)
    near, far, sums_low = tie((near, far, sums_low))
    even_out, odd_out = row_messages(cells, rows, near, far)
    even_out, odd_out, stem_in = tie((even_out, odd_out, stem_in))
    even_in, odd_in = even_pair(even_out), odd_pair(odd_out)
    feat_high, sums_high = inner(1, stem_in)

    rim_rows, rim_cols, own = call(
        functools.partial(rim_kernel, cells),
        [shape_of(2 * CH, COLS, dtype=BF16), shape_of(CH, 256, dtype=BF16), shape_of(2, CH, SPOTS, dtype=BF16)],
        [rows, cols, near, far, even_in, odd_in, sums_low, sums_high, *stem_args],
    )

    own = own.at[1].set(partner(own)[0])
    own, rim_rows = tie((own, rim_rows))
    one = beside(own, -1)
    band = beside(own, 0)
    two = beside(own, 1)
    features, head_w, rim_w = call(
        merge_kernel,
        [shape_of(ROWS * CH, COLS, dtype=BF16), shape_of(160, 20 * CH, dtype=BF16), shape_of(40, 4 * CH, dtype=BF16)],
        [feat_low, feat_high, rim_rows, rim_cols, w_head],
    )
    one, features = tie((one, features))
    relay = outer(one)
    band_p, one_p = partner(band), partner(one)
    context = call(
        functools.partial(early_kernel, cells), shape_of(WIDE, SPOTS), [own, band, band_p, one, *proj_args],
        [pltpu.VMEM((WIDE, len(EARLY) * WIDE), BF16), pltpu.VMEM((len(EARLY) * WIDE, 256), BF16)],
    )
    relay, two, context = tie((relay, two, context))
    two_p, relay_p = partner(two), partner(relay)

    inner_logits, col_out, row_out = call(
        functools.partial(logits_kernel, cells),
        [shape_of(2, ROWS, COLS), shape_of(ROWS + 8, 128), shape_of(8, COLS)],
        [
            features, context, one_p, two, two_p, relay, relay_p,
            *proj_args, w_up, b_up[None, :], head_w, rim_w, b_head,
        ],
        [
            pltpu.VMEM((WIDE, len(LATE) * WIDE), BF16),
            pltpu.VMEM((len(LATE) * WIDE, 256), BF16),
            pltpu.VMEM((POOL_ROWS * CH, 256), BF16),
            pltpu.VMEM((POOL_ROWS * CH, COLS), F32),
            pltpu.VMEM(((ROWS + 4) * CH, COLS), BF16),
        ],
        smem=(14,),
    )
    near, far = partner(col_out), outer(col_out)
    row_out = row_sums(cells, row_out, near, far)
    return call(
        functools.partial(sum_kernel, cells),
        shape_of(2, ROWS, COLS),
        [inner_logits, near, far, even_pair(row_out), odd_pair(row_out)],
    )


def solution(mesh):
    sizes = dict(mesh.shape)
    return jax.shard_map(
        functools.partial(body, sizes["cross"], sizes["band"]),
        mesh=mesh,
        in_specs=(P(None, "cross", "band"), P("cross", "band")) + (P(),) * 12,
        out_specs=P(None, "cross", "band"),
        check_vma=False,
    )
```

```python
import functools

import jax
import jax.numpy as jnp
from jax import lax
from jax.experimental import pallas as pl
from jax.experimental.pallas import tpu as pltpu
from jax.sharding import PartitionSpec as P

ROWS, COLS = 64, 512
CH, WIDE, KINDS = 32, 128, 8
POOL_ROWS, POOL_COLS = 16, 128
SPOTS = POOL_ROWS * POOL_COLS
FIRST = 16
HBM = pl.BlockSpec(memory_space=pltpu.HBM)
VMEM = pl.BlockSpec(memory_space=pltpu.VMEM)
SMEM = pl.BlockSpec(memory_space=pltpu.SMEM)
F32, BF16 = jnp.float32, jnp.bfloat16


def iota(shape, dim):
    return lax.broadcasted_iota(jnp.int32, shape, dim)


def shape_of(*dims, dtype=F32):
    return jax.ShapeDtypeStruct(dims, dtype)


def mm(a, b):
    return jnp.dot(a, b, preferred_element_type=F32)


def split(x):
    high = x.astype(BF16)
    return high, (x - high.astype(F32)).astype(BF16)


def column(row):
    count = row.shape[1]
    eye = iota((count, count), 0) == iota((count, count), 1)
    return jnp.sum(jnp.where(eye, row, 0.0), axis=1, keepdims=True)


def placed():
    return lax.axis_index("cross"), lax.axis_index("band")


def flags(last_cross, last_band):
    cross, band = placed()
    one = lambda truth: truth.astype(F32)
    return one(cross > 0), one(cross < last_cross), one(band > 0), one(band < last_band)


def kinds_of(w_in, gain, b_in, gains):
    lane = iota((CH, KINDS), 1)
    kinds = jnp.zeros((CH, KINDS), F32)
    parts = [w_in[k : k + 1, :] for k in range(4)] + [gain[...]] * gains + [b_in[...]]
    parts = [column(part) for part in parts]
    for kind, part in enumerate(parts):
        kinds = jnp.where(lane == kind, part, kinds)
    return kinds


def pool_weights():
    x, q = iota((COLS, POOL_COLS), 0), iota((COLS, POOL_COLS), 1)
    inner = (x // 4 == q) & (x > 0) & (x < COLS - 1)
    return jnp.where(inner, 1.0 / 16, 0.0).astype(BF16)


def halo_kernel(rasters, aerial, rows, cols, message, stem_in):
    ones, none = jnp.ones((1, COLS), F32), jnp.zeros((2, COLS), F32)
    for at, y in enumerate((0, 1, ROWS - 2, ROWS - 1)):
        parts = [rasters[kind, y : y + 1, :].astype(F32) for kind in range(4)]
        rows[at * 8 : (at + 1) * 8, :] = jnp.concatenate(parts + [aerial[y : y + 1, :], ones, none], axis=0)
    lane = iota((ROWS, 128), 1)
    packed = jnp.where((lane < 32) & (lane % 8 == 5), 1.0, 0.0)
    for at, x in enumerate((0, 1, COLS - 2, COLS - 1)):
        first = x // 128 * 128
        for kind in range(5):
            if kind < 4:
                slab = rasters[kind, :, first : first + 128].astype(F32)
            else:
                slab = aerial[:, first : first + 128]
            packed = jnp.where(lane == at * 8 + kind, slab[:, x - first : x - first + 1], packed)
    turned = jnp.transpose(jnp.concatenate([packed, jnp.zeros((128 - ROWS, 128), F32)], axis=0))
    cols[...] = turned[:32]
    message[...] = jnp.concatenate([turned[:8], turned[24:32]], axis=0)
    for y in range(0, ROWS, 8):
        values = jnp.concatenate([rasters[k, y : y + 8, :] for k in range(4)], axis=0).astype(F32)
        high, low = split(aerial[y : y + 8, :])
        tail = jnp.concatenate([jnp.ones((8, COLS), BF16), jnp.zeros((8, COLS), BF16)], axis=0)
        stem_in[y * 8 : y * 8 + 64, :] = jnp.concatenate([values.astype(BF16), high, low, tail], axis=0)


def sides(partner, outer, low, high):
    even = placed()[1] % 2 == 0
    left = jnp.where(even, outer[high], partner[high])
    right = jnp.where(even, partner[low], outer[low])
    return left, right


def row_messages(cells, rows, partner, outer):
    _, _, has_left, has_right = flags(*cells)
    left, right = sides(partner, outer, slice(0, 8), slice(8, 16))
    lane = lax.broadcasted_iota(jnp.int32, (8, 128), 1)

    def row(at, y):
        low, high = left[:, y : y + 1] * has_left, right[:, y : y + 1] * has_right
        side = jnp.where(lane == 0, high, jnp.where(lane == 1, low, 0.0))
        return jnp.concatenate([rows[at * 8 : (at + 1) * 8, :], side], axis=1)

    low, high = row(0, 0), row(3, ROWS - 1)
    even = placed()[0] % 2 == 0
    return jnp.where(even, high, low), jnp.where(even, low, high)


def inner_kernel(
    part, stem_in, w_in, gain, b_in, conv_w, conv_b, features, sums, stem_w, wide_w, stem3
):
    spread = jnp.where(iota((KINDS, 64), 1) // 8 == iota((KINDS, 64), 0), 1.0, 0.0).astype(BF16)
    same = iota((256, 64), 0) // CH == iota((256, 64), 1) % 8
    halves = []
    for piece in split(kinds_of(w_in, gain, b_in, 2)):
        rows = mm(jnp.concatenate([piece] * 8, axis=0), spread)
        halves.append(jnp.where(same, rows, 0.0))
    stem_w[...] = jnp.concatenate(halves, axis=1).astype(BF16)
    wide_w[...] = jnp.zeros(wide_w.shape, BF16)
    taps = conv_w[...]
    for y in range(8):
        wide_w[y * CH : (y + 1) * CH, y * 96 : y * 96 + 288] = taps
    pool_w = pool_weights()
    bias = jnp.broadcast_to(column(conv_b[...]), (CH, COLS))
    bias = jnp.concatenate([bias] * 8, axis=0)

    start, count = (0, FIRST) if part == 0 else (FIRST, ROWS - FIRST)
    blocks = range(max(start // 8 - 1, 0), min((start + count) // 8 + 1, ROWS // 8))
    base = start - 1
    edge = 0 if part == 0 else count + 1
    stem3[edge * 96 : (edge + 1) * 96, :] = jnp.zeros((96, COLS), BF16)
    for block in blocks:
        y = block * 8
        x = stem_in[y * 8 : y * 8 + 64, :]
        out = jnp.maximum(mm(stem_w[...], jnp.concatenate([x, x], axis=0)), 0.0)
        for r in range(8):
            at = y + r - base
            if at < 0 or at > count + 1:
                continue
            s = out[r * CH : (r + 1) * CH, :]
            parts = [pltpu.roll(s, 1, 1), s, pltpu.roll(s, COLS - 1, 1)]
            stem3[at * 96 : (at + 1) * 96, :] = jnp.concatenate(parts, axis=0).astype(BF16)

    for block in range(count // 8):
        out = mm(wide_w[...], stem3[block * 768 : block * 768 + 960, :])
        value = jnp.maximum(out + bias, 0.0).astype(BF16)
        features[block * 256 : (block + 1) * 256, :] = value
        means = mm(value, pool_w)
        for p in range(2):
            rows = [means[p * 128 + r * 32 : p * 128 + (r + 1) * 32, :] for r in range(4)]
            if part == 0 and block == 0 and p == 0:
                rows = rows[1:]
            if part == 1 and block == count // 8 - 1 and p == 1:
                rows = rows[:3]
            at = (block * 2 + p) * POOL_COLS
            sums[:, at : at + POOL_COLS] = sum(rows[1:], rows[0])


def rim_kernel(
    cells, rows, cols, partner, outer, even_message, odd_message, sums_low, sums_high,
    w_in, gain, b_in, conv_w, conv_b, rim_rows, rim_cols, pooled, own,
):
    has_above, has_below, has_left, has_right = flags(*cells)
    left, right = sides(partner, outer, slice(0, 8), slice(8, 16))
    left, right = left * has_left, right * has_right
    even = placed()[0] % 2 == 0
    above = jnp.where(even, odd_message[...], even_message[...]) * has_above
    below = jnp.where(even, even_message[...], odd_message[...]) * has_below
    kind_high, kind_low = split(kinds_of(w_in, gain, b_in, 1))
    stem_w = jnp.concatenate([kind_high, kind_high, kind_low], axis=1)
    bias = column(conv_b[...])

    def stem(x):
        high, low = split(x)
        high = high.astype(F32)
        stacked = jnp.concatenate([high, low.astype(F32), high], axis=0).astype(BF16)
        return jnp.maximum(mm(stem_w, stacked), 0.0)

    def conv(stacked):
        return jnp.maximum(mm(conv_w[...], stacked) + bias, 0.0).astype(BF16)

    def row(at):
        return rows[at * 8 : (at + 1) * 8, :]

    pool_w = pool_weights()
    row_sums = []
    trios = [(above[:, :COLS], row(0), row(1)), (row(2), row(3), below[:, :COLS])]
    for at, trio in enumerate(trios):
        stacked = []
        for x in trio:
            s = stem(x)
            stacked += [pltpu.roll(s, 1, 1), s, pltpu.roll(s, COLS - 1, 1)]
        value = conv(jnp.concatenate(stacked, axis=0).astype(BF16))
        rim_rows[at * CH : (at + 1) * CH, :] = value
        row_sums.append(mm(value, pool_w))

    lane = iota((8, 128), 1)

    def line(inside, top, bottom, x):
        top, bottom = top[:, x : x + 1], bottom[:, x : x + 1]
        return jnp.where(lane < ROWS, inside, jnp.where(lane == ROWS, bottom, 0.0)), top

    x_of = {-1: COLS + 1, COLS: COLS}
    lines = {-1: left, COLS: right}
    for at, x in enumerate((0, 1, COLS - 2, COLS - 1)):
        lines[x] = cols[at * 8 : (at + 1) * 8, :]
    columns = []
    for dx in (-1, 0, 1):
        low, low_top = line(lines[dx], above, below, x_of.get(dx, dx))
        x = COLS - 1 + dx
        high, high_top = line(lines[x], above, below, x_of.get(x, x))
        low = jnp.where(lane == 127, high_top, low)
        high = jnp.where(lane == 127, low_top, high)
        columns.append(stem(jnp.concatenate([low, high], axis=1)))
    s = jnp.concatenate(columns, axis=0)
    stacked = [pltpu.roll(s, 1, 1), s, pltpu.roll(s, 255, 1)]
    value = conv(jnp.concatenate(stacked, axis=0).astype(BF16))
    rim_cols[...] = value
    y, at = iota((256, 128), 0), iota((256, 128), 1)
    picked = (y < ROWS) & (y // 4 == at) | (y >= 128) & (y < 128 + ROWS) & (y // 4 - 16 == at)
    col_sums = mm(value, jnp.where(picked, 1.0 / 16, 0.0).astype(BF16))
    lane = iota((CH, POOL_COLS), 1)
    for p in range(POOL_ROWS):
        at = p * POOL_COLS
        near = sums_low if p < FIRST // 4 else sums_high
        first = at if p < FIRST // 4 else at - FIRST // 4 * POOL_COLS
        last = jnp.where(lane == POOL_COLS - 1, col_sums[:, 16 + p : 17 + p], 0.0)
        total = near[:, first : first + POOL_COLS] + jnp.where(lane == 0, col_sums[:, p : p + 1], last)
        if p == 0:
            total += row_sums[0]
        if p == POOL_ROWS - 1:
            total += row_sums[1]
        pooled[:, at : at + POOL_COLS] = total.astype(BF16)
        own[0, :, at : at + POOL_COLS] = total.astype(BF16)
    own[1, :, :] = jnp.zeros((CH, SPOTS), BF16)


def head_weights(w_head, row_y, row_count, col_y, col_count):
    shape = (10 * row_count, col_count * CH)
    rows = iota((10 * row_count, 2), 0) // row_count % 2 == iota((10 * row_count, 2), 1)
    pick = jnp.where(rows, 1.0, 0.0).astype(BF16)
    dx = iota((10 * row_count, 160), 0) // (2 * row_count) == iota((10 * row_count, 160), 1) // CH
    repeat = iota((160, shape[1]), 0) % CH == iota((160, shape[1]), 1) % CH
    repeat = jnp.where(repeat, 1.0, 0.0).astype(BF16)
    dy = row_y(iota(shape, 0) % row_count) - col_y(iota(shape, 1) // CH)
    total = jnp.zeros(shape, F32)
    for tap in range(5):
        taps = mm(pick, w_head[:, tap * 160 : (tap + 1) * 160])
        taps = mm(jnp.where(dx, taps, 0.0).astype(BF16), repeat)
        total = jnp.where(dy == tap - 2, taps, total)
    return total.astype(BF16)


MAPS = {
    (0, -2): ("band", 0), (0, -1): ("band", 1), (0, 0): ("own", 0), (0, 1): ("own", 1), (0, 2): ("band_p", 1),
    (-1, -2): ("one", 0), (-1, -1): ("one", 1), (-1, 0): ("relay_p", 0), (-1, 1): ("relay_p", 1), (-1, 2): ("two_p", 1),
    (1, -2): ("two", 0), (1, -1): ("two", 1), (1, 0): ("relay", 1), (1, 1): ("relay", 0), (1, 2): ("one_p", 1),
}
PHASES = (("own", "one", "one_p", "band"), ("two", "two_p", "relay", "relay_p", "band_p"))
TILES = [[at for at in range(15) if MAPS[(at // 5 - 1, at % 5 - 2)][0] in names] for names in PHASES]


def context_sum(cells, which, arrays, proj_w, proj_b, ctx_w, weights, proj, finish):
    last_cross, last_band = cells
    cross, band = placed()
    core = band % 2
    sign = 1 - 2 * core
    for k, at in enumerate(which):
        row, col = cross + (at // 5 - 1) * sign, band + (at % 5 - 2) * sign
        inside = (row >= 0) & (row <= last_cross) & (col >= 0) & (col <= last_band)
        one = ctx_w[:, at * WIDE : (at + 1) * WIDE]
        two = ctx_w[:, (14 - at) * WIDE : (15 - at) * WIDE]
        chosen = jnp.where(core == 0, one, two)
        weights[:, k * WIDE : (k + 1) * WIDE] = jnp.where(inside, chosen, jnp.zeros_like(chosen))
    p_bias = jnp.broadcast_to(column(proj_b[...]), (WIDE, 256))
    proj_w = jnp.transpose(proj_w[...].astype(F32)).astype(BF16)

    def part(at, carry):
        spots = pl.ds(pl.multiple_of(at * 256, 256), 256)
        for k, tile in enumerate(which):
            name, half = MAPS[(tile // 5 - 1, tile % 5 - 2)]
            out = mm(proj_w, arrays[name][half, :, spots])
            proj[k * WIDE : (k + 1) * WIDE, :] = jnp.maximum(out + p_bias, 0.0).astype(BF16)
        finish(at, spots, mm(weights[...], proj[...]))
        return carry

    lax.fori_loop(0, SPOTS // 256, part, 0, unroll=True)


def early_kernel(cells, *refs):
    count = len(PHASES[0])
    arrays = dict(zip(PHASES[0], refs[:count]))
    proj_w, proj_b, ctx_w, w_head, up_b, context, head_w, rim_w, up_bias, weights, proj = refs[count:]
    up_bias[...] = jnp.broadcast_to(column(up_b[...]), (CH, 256))
    head_w[...] = head_weights(w_head[...], lambda r: r, 16, lambda r: r - 2, 20)
    outside = lambda r: jnp.where(r < 2, r - 2, ROWS - 2 + r)
    rim_w[...] = head_weights(w_head[...], outside, 4, lambda r: jnp.where(r < 2, r, ROWS - 4 + r), 4)
    own = TILES[0].index(7)

    def finish(at, spots, total):
        context[:, spots] = total + proj[own * WIDE : (own + 1) * WIDE, :].astype(F32)

    context_sum(cells, TILES[0], arrays, proj_w, proj_b, ctx_w, weights, proj, finish)


def logits_kernel(
    cells, low, high, rim_rows, rim_cols, context, two, two_p, relay, relay_p, band_p,
    proj_w, proj_b, ctx_w, up_w, up_b, head_w, rim_w, head_b,
    logits, col_out, row_out, weights, proj, low_up, lifted, decoded,
):
    arrays = dict(zip(PHASES[1], (two, two_p, relay, relay_p, band_p)))

    def finish(part, spots, total):
        mixed = jnp.maximum(total + context[:, spots], 0.0).astype(BF16)
        up = mm(up_w[...], mixed) + up_b[...]
        high, low = split(up)
        both = [
            jnp.concatenate([high[:, h * 128 : (h + 1) * 128], low[:, h * 128 : (h + 1) * 128]], axis=1)
            for h in range(2)
        ]
        low_up[pl.ds(pl.multiple_of(part * 64, 64), 64), :] = jnp.concatenate(both, axis=0)

    context_sum(cells, TILES[1], arrays, proj_w, proj_b, ctx_w, weights, proj, finish)

    widen = jnp.where(
        iota((256, COLS), 0) % 128 == iota((256, COLS), 1) // 4, 1.0, 0.0
    ).astype(BF16)
    lifted[...] = mm(low_up[...], widen)

    decoded[0:64, :] = jnp.zeros((64, COLS), BF16)
    decoded[66 * CH :, :] = jnp.zeros((64, COLS), BF16)

    lane = iota((CH, 128), 1)
    columns = rim_cols[...].astype(F32)
    for y in range(ROWS):
        if y == 0:
            f = rim_rows[0:CH, :]
        elif y == ROWS - 1:
            f = rim_rows[CH : 2 * CH, :]
        else:
            at = (y if y < FIRST else y - FIRST) * CH
            f = (low if y < FIRST else high)[at : at + CH, :]
        f = f.astype(F32)
        first = jnp.where(lane == 0, columns[:, y : y + 1], f[:, :128])
        last = jnp.where(lane == 127, columns[:, 128 + y : 129 + y], f[:, COLS - 128 :])
        f = jnp.concatenate([first, f[:, 128 : COLS - 128], last], axis=1)
        value = f + lifted[y // 4 * CH : (y // 4 + 1) * CH, :]
        decoded[(y + 2) * CH : (y + 3) * CH, :] = jnp.maximum(value, 0.0).astype(BF16)

    def gather_taps(z, count):
        total = None
        for dx in range(5):
            part = z[dx * count : (dx + 1) * count, :]
            part = jnp.concatenate([part, jnp.zeros((count, 128), F32)], axis=1)
            if dx != 2:
                part = pltpu.roll(part, (dx - 2) % 640, 1)
            total = part if total is None else total + part
        return total

    lane16 = iota((16, 128), 1)
    first_lanes = (lane16 < 2) | (lane16 >= 126)

    def head(block, carry):
        first = pl.multiple_of(block * 16 * CH, 16 * CH)
        total = gather_taps(mm(head_w[...], decoded[pl.ds(first, 20 * CH), :]), 32)
        y = pl.multiple_of(block * 16, 16)
        for k in range(2):
            logits[k, pl.ds(y, 16), :] = total[k * 16 : (k + 1) * 16, :COLS] + head_b[k]
        rim = total[:, COLS:]
        col_out[pl.ds(y, 16), :] = jnp.where(first_lanes, rim[:16], pltpu.roll(rim[16:], 4, 1))
        return carry

    lax.fori_loop(0, ROWS // 16, head, 0, unroll=True)

    ends = jnp.concatenate([decoded[64:128, :], decoded[64 * CH : 66 * CH, :]], axis=0)
    total = gather_taps(mm(rim_w[...], ends), 8)
    row_out[...] = total[:, :COLS]
    col_out[ROWS : ROWS + 8, :] = total[:, COLS:]


def row_sums(cells, row_out, partner, outer):
    _, _, has_left, has_right = flags(*cells)
    corners = slice(ROWS, ROWS + 8)
    left, right = sides(partner, outer, corners, corners)
    lane = lax.broadcasted_iota(jnp.int32, (8, 128), 1)
    low = jnp.where(lane < 2, left * has_left, 0.0)
    high = jnp.where(lane >= 126, right * has_right, 0.0)
    return row_out + jnp.concatenate([low, jnp.zeros((8, COLS - 256), F32), high], axis=1)


def sum_kernel(cells, inner, partner, outer, even_message, odd_message, out):
    has_above, has_below, has_left, has_right = flags(*cells)
    even = placed()[0] % 2 == 0
    above = jnp.where(even, odd_message[...], even_message[...]) * has_above
    below = jnp.where(even, even_message[...], odd_message[...]) * has_below
    left, right = sides(partner, outer, slice(0, ROWS), slice(0, ROWS))
    left, right = left * has_left, right * has_right
    out[...] = inner[...]
    lane = iota((ROWS, 128), 1)
    for k in range(2):
        low = left if k == 0 else pltpu.roll(left, 124, 1)
        out[k, :, 0:128] += jnp.where(lane < 2, low, 0.0)
        high = right if k == 0 else pltpu.roll(right, 124, 1)
        out[k, :, COLS - 128 : COLS] += jnp.where(lane >= 126, high, 0.0)
        out[k, 0:2, :] += above[4 * k + 2 : 4 * k + 4]
        out[k, ROWS - 2 : ROWS, :] += below[4 * k : 4 * k + 2]


def call(kernel, outs, args, scratch=(), smem=(), hbm=(), flops=0):
    scratch = list(scratch)

    def fetching(*refs):
        ins, rest = list(refs[: len(args)]), refs[len(args) :]
        buffers, sems = rest[-len(hbm) - 1 : -1], rest[-1]
        copies = [pltpu.make_async_copy(ins[at], buffers[i], sems.at[i]) for i, at in enumerate(hbm)]
        for copy in copies:
            copy.start()
        for copy in copies:
            copy.wait()
        for at, buffer in zip(hbm, buffers):
            ins[at] = buffer
        kernel(*ins, *rest[: -len(hbm) - 1])

    if hbm:
        scratch += [pltpu.VMEM(args[at].shape, args[at].dtype) for at in hbm]
        scratch += [pltpu.SemaphoreType.DMA((len(hbm),))]
    return pl.pallas_call(
        fetching if hbm else kernel,
        out_shape=outs,
        in_specs=[SMEM if at in smem else HBM if at in hbm else VMEM for at in range(len(args))],
        out_specs=jax.tree.map(lambda _: VMEM, outs),
        scratch_shapes=scratch,
        compiler_params=pltpu.CompilerParams(vmem_limit_bytes=24 * 1024 * 1024),
        cost_estimate=pl.CostEstimate(flops=flops, bytes_accessed=1 << 20, transcendentals=0),
    )(*args)


def body(
    n_cross, n_band, rasters, aerial, w_in, aerial_gain, b_in, w_conv1, b_conv1, w_proj, b_proj,
    w_ctx, w_up, b_up, w_head, b_head,
):
    cells = (n_cross - 1, n_band - 1)
    tie = lax.optimization_barrier

    def moved(x, source):
        route = []
        for cross in range(n_cross):
            for band in range(n_band):
                c, b = source(cross, band)
                route.append(((b % n_band) * n_cross + c % n_cross, band * n_cross + cross))
        return lax.ppermute(x, ("band", "cross"), route)

    def partner(x):
        return moved(x, lambda c, b: (c, b ^ 1))

    def outer(x):
        return moved(x, lambda c, b: (c, ((b + 1) ^ 1) - 1))

    def even_pair(x):
        return moved(x, lambda c, b: (c ^ 1, b))

    def odd_pair(x):
        return moved(x, lambda c, b: (((c + 1) ^ 1) - 1, b))

    def beside(x, u):
        return moved(x, lambda c, b: (c + u * (1 - 2 * (b % 2)), b - 2 + 4 * (b % 2)))

    rows, cols, message, stem_in = call(
        halo_kernel,
        [shape_of(32, COLS), shape_of(32, 128), shape_of(16, 128), shape_of(8 * ROWS, COLS, dtype=BF16)],
        [rasters, aerial],
        flops=8 * 10**10,
    )
    near, far = partner(message), outer(message)

    stem_args = [w_in.T, aerial_gain[None, :], b_in[None, :], w_conv1, b_conv1[None, :]]
    proj_args = [w_proj.T, b_proj[None, :], w_ctx]

    def inner(part, stem_in):
        count = FIRST if part == 0 else ROWS - FIRST
        return call(
            functools.partial(inner_kernel, part),
            [shape_of(count * CH, COLS, dtype=BF16), shape_of(CH, count // 4 * POOL_COLS)],
            [stem_in, *stem_args],
            [
                pltpu.VMEM((256, 128), BF16),
                pltpu.VMEM((256, 960), BF16),
                pltpu.VMEM(((count + 2) * 96, COLS), BF16),
            ],
            flops=4 * 10**9,
        )

    feat_low, sums_low = inner(0, stem_in)
    near, far, sums_low = tie((near, far, sums_low))
    even_out, odd_out = row_messages(cells, rows, near, far)
    even_out, odd_out, stem_in = tie((even_out, odd_out, stem_in))
    even_in, odd_in = even_pair(even_out), odd_pair(odd_out)
    feat_high, sums_high = inner(1, stem_in)

    rim_rows, rim_cols, pooled, own = call(
        functools.partial(rim_kernel, cells),
        [
            shape_of(2 * CH, COLS, dtype=BF16), shape_of(CH, 256, dtype=BF16), shape_of(CH, SPOTS, dtype=BF16),
            shape_of(2, CH, SPOTS, dtype=BF16),
        ],
        [rows, cols, near, far, even_in, odd_in, sums_low, sums_high, *stem_args],
    )

    own = own.at[1].set(partner(pooled))
    one, band = beside(own, -1), beside(own, 0)
    own, one = tie((own, one))
    relay, two = outer(one), beside(own, 1)
    sent = dict(own=own, one=one, band=band, one_p=partner(one))

    def context_call(kernel, phase, outs, args, scratch=(), **more):
        count = len(TILES[phase]) * WIDE
        buffers = [pltpu.VMEM((WIDE, count), BF16), pltpu.VMEM((count, 256), BF16)]
        return call(functools.partial(kernel, cells), outs, args, buffers + list(scratch), **more)

    context, head_w, rim_w, up_bias = context_call(
        early_kernel, 0,
        [
            shape_of(WIDE, SPOTS), shape_of(160, 20 * CH, dtype=BF16), shape_of(40, 4 * CH, dtype=BF16),
            shape_of(CH, 256),
        ],
        [*(sent[name] for name in PHASES[0]), *proj_args, w_head, b_up[None, :]],
    )
    relay, two, context = tie((relay, two, context))
    relay_p, two_p = partner(relay), partner(two)
    band_p = partner(band)

    inner_logits, col_out, row_out = context_call(
        logits_kernel, 1,
        [shape_of(2, ROWS, COLS), shape_of(ROWS + 8, 128), shape_of(8, COLS)],
        [
            feat_low, feat_high, rim_rows, rim_cols, context, two, two_p, relay, relay_p, band_p,
            *proj_args, w_up, up_bias, head_w, rim_w, b_head,
        ],
        [
            pltpu.VMEM((POOL_ROWS * CH, 256), BF16),
            pltpu.VMEM((POOL_ROWS * CH, COLS), F32),
            pltpu.VMEM(((ROWS + 4) * CH, COLS), BF16),
        ],
        smem=(18,),
    )
    near, far = partner(col_out), outer(col_out)
    row_out = row_sums(cells, row_out, near, far)
    return call(
        functools.partial(sum_kernel, cells),
        shape_of(2, ROWS, COLS),
        [inner_logits, near, far, even_pair(row_out), odd_pair(row_out)],
    )


def solution(mesh):
    sizes = dict(mesh.shape)
    return jax.shard_map(
        functools.partial(body, sizes["cross"], sizes["band"]),
        mesh=mesh,
        in_specs=(P(None, "cross", "band"), P("cross", "band")) + (P(),) * 12,
        out_specs=P(None, "cross", "band"),
        check_vma=False,
    )
```

```python
import functools

import jax
import jax.numpy as jnp
from jax import lax
from jax.experimental import pallas as pl
from jax.experimental.pallas import tpu as pltpu
from jax.sharding import PartitionSpec as P

ROWS, COLS = 64, 512
CH, WIDE, KINDS = 32, 128, 8
POOL_ROWS, POOL_COLS = 16, 128
SPOTS = POOL_ROWS * POOL_COLS
FIRST = 16
HBM = pl.BlockSpec(memory_space=pltpu.HBM)
VMEM = pl.BlockSpec(memory_space=pltpu.VMEM)
SMEM = pl.BlockSpec(memory_space=pltpu.SMEM)
F32, BF16 = jnp.float32, jnp.bfloat16


def iota(shape, dim):
    return lax.broadcasted_iota(jnp.int32, shape, dim)


def shape_of(*dims, dtype=F32):
    return jax.ShapeDtypeStruct(dims, dtype)


def mm(a, b):
    return jnp.dot(a, b, preferred_element_type=F32)


def split(x):
    high = x.astype(BF16)
    return high, (x - high.astype(F32)).astype(BF16)


def column(row):
    count = row.shape[1]
    eye = iota((count, count), 0) == iota((count, count), 1)
    return jnp.sum(jnp.where(eye, row, 0.0), axis=1, keepdims=True)


def placed():
    return lax.axis_index("cross"), lax.axis_index("band")


def flags(last_cross, last_band):
    cross, band = placed()
    one = lambda truth: truth.astype(F32)
    return one(cross > 0), one(cross < last_cross), one(band > 0), one(band < last_band)


def kinds_of(w_in, gain, b_in, gains):
    lane = iota((CH, KINDS), 1)
    kinds = jnp.zeros((CH, KINDS), F32)
    parts = [w_in[k : k + 1, :] for k in range(4)] + [gain[...]] * gains + [b_in[...]]
    parts = [column(part) for part in parts]
    for kind, part in enumerate(parts):
        kinds = jnp.where(lane == kind, part, kinds)
    return kinds


def pool_weights():
    x, q = iota((COLS, POOL_COLS), 0), iota((COLS, POOL_COLS), 1)
    inner = (x // 4 == q) & (x > 0) & (x < COLS - 1)
    return jnp.where(inner, 1.0 / 16, 0.0).astype(BF16)


def halo_kernel(rasters, aerial, rows, cols, message, stem_in):
    ones, none = jnp.ones((1, COLS), F32), jnp.zeros((2, COLS), F32)
    for at, y in enumerate((0, 1, ROWS - 2, ROWS - 1)):
        parts = [rasters[kind, y : y + 1, :].astype(F32) for kind in range(4)]
        rows[at * 8 : (at + 1) * 8, :] = jnp.concatenate(parts + [aerial[y : y + 1, :], ones, none], axis=0)
    lane = iota((ROWS, 128), 1)
    packed = jnp.where((lane < 32) & (lane % 8 == 5), 1.0, 0.0)
    for at, x in enumerate((0, 1, COLS - 2, COLS - 1)):
        first = x // 128 * 128
        for kind in range(5):
            if kind < 4:
                slab = rasters[kind, :, first : first + 128].astype(F32)
            else:
                slab = aerial[:, first : first + 128]
            packed = jnp.where(lane == at * 8 + kind, slab[:, x - first : x - first + 1], packed)
    turned = jnp.transpose(jnp.concatenate([packed, jnp.zeros((128 - ROWS, 128), F32)], axis=0))
    cols[...] = turned[:32]
    message[...] = jnp.concatenate([turned[:8], turned[24:32]], axis=0)
    for y in range(0, ROWS, 8):
        values = jnp.concatenate([rasters[k, y : y + 8, :] for k in range(4)], axis=0).astype(F32)
        high, low = split(aerial[y : y + 8, :])
        tail = jnp.concatenate([jnp.ones((8, COLS), BF16), jnp.zeros((8, COLS), BF16)], axis=0)
        stem_in[y * 8 : y * 8 + 64, :] = jnp.concatenate([values.astype(BF16), high, low, tail], axis=0)


def sides(partner, outer, low, high):
    even = placed()[1] % 2 == 0
    left = jnp.where(even, outer[high], partner[high])
    right = jnp.where(even, partner[low], outer[low])
    return left, right


def row_messages(cells, rows, partner, outer):
    _, _, has_left, has_right = flags(*cells)
    left, right = sides(partner, outer, slice(0, 8), slice(8, 16))
    lane = lax.broadcasted_iota(jnp.int32, (8, 128), 1)

    def row(at, y):
        low, high = left[:, y : y + 1] * has_left, right[:, y : y + 1] * has_right
        side = jnp.where(lane == 0, high, jnp.where(lane == 1, low, 0.0))
        return jnp.concatenate([rows[at * 8 : (at + 1) * 8, :], side], axis=1)

    low, high = row(0, 0), row(3, ROWS - 1)
    even = placed()[0] % 2 == 0
    return jnp.where(even, high, low), jnp.where(even, low, high)


def inner_kernel(
    part, stem_in, w_in, gain, b_in, conv_w, conv_b, features, sums, stem_w, wide_w, stem3
):
    spread = jnp.where(iota((KINDS, 64), 1) // 8 == iota((KINDS, 64), 0), 1.0, 0.0).astype(BF16)
    same = iota((256, 64), 0) // CH == iota((256, 64), 1) % 8
    halves = []
    for piece in split(kinds_of(w_in, gain, b_in, 2)):
        rows = mm(jnp.concatenate([piece] * 8, axis=0), spread)
        halves.append(jnp.where(same, rows, 0.0))
    stem_w[...] = jnp.concatenate(halves, axis=1).astype(BF16)
    wide_w[...] = jnp.zeros(wide_w.shape, BF16)
    taps = conv_w[...]
    for y in range(8):
        wide_w[y * CH : (y + 1) * CH, y * 96 : y * 96 + 288] = taps
    pool_w = pool_weights()
    bias = jnp.broadcast_to(column(conv_b[...]), (CH, COLS))
    bias = jnp.concatenate([bias] * 8, axis=0)

    start, count = (0, FIRST) if part == 0 else (FIRST, ROWS - FIRST)
    blocks = range(max(start // 8 - 1, 0), min((start + count) // 8 + 1, ROWS // 8))
    base = start - 1
    edge = 0 if part == 0 else count + 1
    stem3[edge * 96 : (edge + 1) * 96, :] = jnp.zeros((96, COLS), BF16)
    for block in blocks:
        y = block * 8
        x = stem_in[y * 8 : y * 8 + 64, :]
        out = jnp.maximum(mm(stem_w[...], jnp.concatenate([x, x], axis=0)), 0.0)
        for r in range(8):
            at = y + r - base
            if at < 0 or at > count + 1:
                continue
            s = out[r * CH : (r + 1) * CH, :]
            parts = [pltpu.roll(s, 1, 1), s, pltpu.roll(s, COLS - 1, 1)]
            stem3[at * 96 : (at + 1) * 96, :] = jnp.concatenate(parts, axis=0).astype(BF16)

    for block in range(count // 8):
        out = mm(wide_w[...], stem3[block * 768 : block * 768 + 960, :])
        value = jnp.maximum(out + bias, 0.0).astype(BF16)
        features[block * 256 : (block + 1) * 256, :] = value
        means = mm(value, pool_w)
        for p in range(2):
            rows = [means[p * 128 + r * 32 : p * 128 + (r + 1) * 32, :] for r in range(4)]
            if part == 0 and block == 0 and p == 0:
                rows = rows[1:]
            if part == 1 and block == count // 8 - 1 and p == 1:
                rows = rows[:3]
            at = (block * 2 + p) * POOL_COLS
            sums[:, at : at + POOL_COLS] = sum(rows[1:], rows[0])


def rim_kernel(
    cells, rows, cols, partner, outer, even_message, odd_message, sums_low, sums_high,
    w_in, gain, b_in, conv_w, conv_b, rim_rows, rim_cols, pooled, own,
):
    has_above, has_below, has_left, has_right = flags(*cells)
    left, right = sides(partner, outer, slice(0, 8), slice(8, 16))
    left, right = left * has_left, right * has_right
    even = placed()[0] % 2 == 0
    above = jnp.where(even, odd_message[...], even_message[...]) * has_above
    below = jnp.where(even, even_message[...], odd_message[...]) * has_below
    kind_high, kind_low = split(kinds_of(w_in, gain, b_in, 1))
    stem_w = jnp.concatenate([kind_high, kind_high, kind_low], axis=1)
    bias = column(conv_b[...])

    def stem(x):
        high, low = split(x)
        high = high.astype(F32)
        stacked = jnp.concatenate([high, low.astype(F32), high], axis=0).astype(BF16)
        return jnp.maximum(mm(stem_w, stacked), 0.0)

    def conv(stacked):
        return jnp.maximum(mm(conv_w[...], stacked) + bias, 0.0).astype(BF16)

    def row(at):
        return rows[at * 8 : (at + 1) * 8, :]

    pool_w = pool_weights()
    row_sums = []
    trios = [(above[:, :COLS], row(0), row(1)), (row(2), row(3), below[:, :COLS])]
    for at, trio in enumerate(trios):
        stacked = []
        for x in trio:
            s = stem(x)
            stacked += [pltpu.roll(s, 1, 1), s, pltpu.roll(s, COLS - 1, 1)]
        value = conv(jnp.concatenate(stacked, axis=0).astype(BF16))
        rim_rows[at * CH : (at + 1) * CH, :] = value
        row_sums.append(mm(value, pool_w))

    lane = iota((8, 128), 1)

    def line(inside, top, bottom, x):
        top, bottom = top[:, x : x + 1], bottom[:, x : x + 1]
        return jnp.where(lane < ROWS, inside, jnp.where(lane == ROWS, bottom, 0.0)), top

    x_of = {-1: COLS + 1, COLS: COLS}
    lines = {-1: left, COLS: right}
    for at, x in enumerate((0, 1, COLS - 2, COLS - 1)):
        lines[x] = cols[at * 8 : (at + 1) * 8, :]
    columns = []
    for dx in (-1, 0, 1):
        low, low_top = line(lines[dx], above, below, x_of.get(dx, dx))
        x = COLS - 1 + dx
        high, high_top = line(lines[x], above, below, x_of.get(x, x))
        low = jnp.where(lane == 127, high_top, low)
        high = jnp.where(lane == 127, low_top, high)
        columns.append(stem(jnp.concatenate([low, high], axis=1)))
    s = jnp.concatenate(columns, axis=0)
    stacked = [pltpu.roll(s, 1, 1), s, pltpu.roll(s, 255, 1)]
    value = conv(jnp.concatenate(stacked, axis=0).astype(BF16))
    rim_cols[...] = value
    y, at = iota((256, 128), 0), iota((256, 128), 1)
    picked = (y < ROWS) & (y // 4 == at) | (y >= 128) & (y < 128 + ROWS) & (y // 4 - 16 == at)
    col_sums = mm(value, jnp.where(picked, 1.0 / 16, 0.0).astype(BF16))
    lane = iota((CH, POOL_COLS), 1)
    for p in range(POOL_ROWS):
        at = p * POOL_COLS
        near = sums_low if p < FIRST // 4 else sums_high
        first = at if p < FIRST // 4 else at - FIRST // 4 * POOL_COLS
        last = jnp.where(lane == POOL_COLS - 1, col_sums[:, 16 + p : 17 + p], 0.0)
        total = near[:, first : first + POOL_COLS] + jnp.where(lane == 0, col_sums[:, p : p + 1], last)
        if p == 0:
            total += row_sums[0]
        if p == POOL_ROWS - 1:
            total += row_sums[1]
        pooled[:, at : at + POOL_COLS] = total.astype(BF16)
        own[0, :, at : at + POOL_COLS] = total.astype(BF16)
    own[1, :, :] = jnp.zeros((CH, SPOTS), BF16)


def head_weights(w_head, row_y, row_count, col_y, col_count):
    shape = (10 * row_count, col_count * CH)
    rows = iota((10 * row_count, 2), 0) // row_count % 2 == iota((10 * row_count, 2), 1)
    pick = jnp.where(rows, 1.0, 0.0).astype(BF16)
    dx = iota((10 * row_count, 160), 0) // (2 * row_count) == iota((10 * row_count, 160), 1) // CH
    repeat = iota((160, shape[1]), 0) % CH == iota((160, shape[1]), 1) % CH
    repeat = jnp.where(repeat, 1.0, 0.0).astype(BF16)
    dy = row_y(iota(shape, 0) % row_count) - col_y(iota(shape, 1) // CH)
    total = jnp.zeros(shape, F32)
    for tap in range(5):
        taps = mm(pick, w_head[:, tap * 160 : (tap + 1) * 160])
        taps = mm(jnp.where(dx, taps, 0.0).astype(BF16), repeat)
        total = jnp.where(dy == tap - 2, taps, total)
    return total.astype(BF16)


MAPS = {
    (0, -2): ("band", 0), (0, -1): ("band", 1), (0, 0): ("own", 0), (0, 1): ("own", 1), (0, 2): ("band_p", 1),
    (-1, -2): ("one", 0), (-1, -1): ("one", 1), (-1, 0): ("relay_p", 0), (-1, 1): ("relay_p", 1), (-1, 2): ("two_p", 1),
    (1, -2): ("two", 0), (1, -1): ("two", 1), (1, 0): ("relay", 1), (1, 1): ("relay", 0), (1, 2): ("one_p", 1),
}
PHASES = (("own", "one", "band"), ("two", "two_p", "relay", "relay_p", "band_p", "one_p"))
TILES = [[at for at in range(15) if MAPS[(at // 5 - 1, at % 5 - 2)][0] in names] for names in PHASES]


def context_sum(cells, which, arrays, proj_w, proj_b, ctx_w, weights, proj, finish):
    last_cross, last_band = cells
    cross, band = placed()
    core = band % 2
    sign = 1 - 2 * core
    for k, at in enumerate(which):
        row, col = cross + (at // 5 - 1) * sign, band + (at % 5 - 2) * sign
        inside = (row >= 0) & (row <= last_cross) & (col >= 0) & (col <= last_band)
        one = ctx_w[:, at * WIDE : (at + 1) * WIDE]
        two = ctx_w[:, (14 - at) * WIDE : (15 - at) * WIDE]
        chosen = jnp.where(core == 0, one, two)
        weights[:, k * WIDE : (k + 1) * WIDE] = jnp.where(inside, chosen, jnp.zeros_like(chosen))
    p_bias = jnp.broadcast_to(column(proj_b[...]), (WIDE, 256))
    proj_w = jnp.transpose(proj_w[...].astype(F32)).astype(BF16)

    def part(at, carry):
        spots = pl.ds(pl.multiple_of(at * 256, 256), 256)
        for k, tile in enumerate(which):
            name, half = MAPS[(tile // 5 - 1, tile % 5 - 2)]
            out = mm(proj_w, arrays[name][half, :, spots])
            proj[k * WIDE : (k + 1) * WIDE, :] = jnp.maximum(out + p_bias, 0.0).astype(BF16)
        finish(at, spots, mm(weights[...], proj[...]))
        return carry

    lax.fori_loop(0, SPOTS // 256, part, 0, unroll=True)


def early_kernel(cells, *refs):
    count = len(PHASES[0])
    arrays = dict(zip(PHASES[0], refs[:count]))
    proj_w, proj_b, ctx_w, w_head, up_b, context, head_w, rim_w, up_bias, weights, proj = refs[count:]
    up_bias[...] = jnp.broadcast_to(column(up_b[...]), (CH, 256))
    head_w[...] = head_weights(w_head[...], lambda r: r, 16, lambda r: r - 2, 20)
    outside = lambda r: jnp.where(r < 2, r - 2, ROWS - 2 + r)
    rim_w[...] = head_weights(w_head[...], outside, 4, lambda r: jnp.where(r < 2, r, ROWS - 4 + r), 4)
    own = TILES[0].index(7)

    def finish(at, spots, total):
        context[:, spots] = total + proj[own * WIDE : (own + 1) * WIDE, :].astype(F32)

    context_sum(cells, TILES[0], arrays, proj_w, proj_b, ctx_w, weights, proj, finish)


def logits_kernel(
    cells, low, high, rim_rows, rim_cols, context, two, two_p, relay, relay_p, band_p, one_p,
    proj_w, proj_b, ctx_w, up_w, up_b, head_w, rim_w, head_b,
    logits, col_out, row_out, weights, proj, low_up, lifted, decoded,
):
    arrays = dict(zip(PHASES[1], (two, two_p, relay, relay_p, band_p, one_p)))

    def finish(part, spots, total):
        mixed = jnp.maximum(total + context[:, spots], 0.0).astype(BF16)
        up = mm(up_w[...], mixed) + up_b[...]
        high, low = split(up)
        both = [
            jnp.concatenate([high[:, h * 128 : (h + 1) * 128], low[:, h * 128 : (h + 1) * 128]], axis=1)
            for h in range(2)
        ]
        low_up[pl.ds(pl.multiple_of(part * 64, 64), 64), :] = jnp.concatenate(both, axis=0)

    context_sum(cells, TILES[1], arrays, proj_w, proj_b, ctx_w, weights, proj, finish)

    widen = jnp.where(
        iota((256, COLS), 0) % 128 == iota((256, COLS), 1) // 4, 1.0, 0.0
    ).astype(BF16)
    lifted[...] = mm(low_up[...], widen)

    decoded[0:64, :] = jnp.zeros((64, COLS), BF16)
    decoded[66 * CH :, :] = jnp.zeros((64, COLS), BF16)

    lane = iota((CH, 128), 1)
    columns = rim_cols[...].astype(F32)
    for y in range(ROWS):
        if y == 0:
            f = rim_rows[0:CH, :]
        elif y == ROWS - 1:
            f = rim_rows[CH : 2 * CH, :]
        else:
            at = (y if y < FIRST else y - FIRST) * CH
            f = (low if y < FIRST else high)[at : at + CH, :]
        f = f.astype(F32)
        first = jnp.where(lane == 0, columns[:, y : y + 1], f[:, :128])
        last = jnp.where(lane == 127, columns[:, 128 + y : 129 + y], f[:, COLS - 128 :])
        f = jnp.concatenate([first, f[:, 128 : COLS - 128], last], axis=1)
        value = f + lifted[y // 4 * CH : (y // 4 + 1) * CH, :]
        decoded[(y + 2) * CH : (y + 3) * CH, :] = jnp.maximum(value, 0.0).astype(BF16)

    def gather_taps(z, count):
        total = None
        for dx in range(5):
            part = z[dx * count : (dx + 1) * count, :]
            part = jnp.concatenate([part, jnp.zeros((count, 128), F32)], axis=1)
            if dx != 2:
                part = pltpu.roll(part, (dx - 2) % 640, 1)
            total = part if total is None else total + part
        return total

    lane16 = iota((16, 128), 1)
    first_lanes = (lane16 < 2) | (lane16 >= 126)

    def head(block, carry):
        first = pl.multiple_of(block * 16 * CH, 16 * CH)
        total = gather_taps(mm(head_w[...], decoded[pl.ds(first, 20 * CH), :]), 32)
        y = pl.multiple_of(block * 16, 16)
        for k in range(2):
            logits[k, pl.ds(y, 16), :] = total[k * 16 : (k + 1) * 16, :COLS] + head_b[k]
        rim = total[:, COLS:]
        col_out[pl.ds(y, 16), :] = jnp.where(first_lanes, rim[:16], pltpu.roll(rim[16:], 4, 1))
        return carry

    lax.fori_loop(0, ROWS // 16, head, 0, unroll=True)

    ends = jnp.concatenate([decoded[64:128, :], decoded[64 * CH : 66 * CH, :]], axis=0)
    total = gather_taps(mm(rim_w[...], ends), 8)
    row_out[...] = total[:, :COLS]
    col_out[ROWS : ROWS + 8, :] = total[:, COLS:]


def row_sums(cells, row_out, partner, outer):
    _, _, has_left, has_right = flags(*cells)
    corners = slice(ROWS, ROWS + 8)
    left, right = sides(partner, outer, corners, corners)
    lane = lax.broadcasted_iota(jnp.int32, (8, 128), 1)
    low = jnp.where(lane < 2, left * has_left, 0.0)
    high = jnp.where(lane >= 126, right * has_right, 0.0)
    return row_out + jnp.concatenate([low, jnp.zeros((8, COLS - 256), F32), high], axis=1)


def sum_kernel(cells, inner, partner, outer, even_message, odd_message, out):
    has_above, has_below, has_left, has_right = flags(*cells)
    even = placed()[0] % 2 == 0
    above = jnp.where(even, odd_message[...], even_message[...]) * has_above
    below = jnp.where(even, even_message[...], odd_message[...]) * has_below
    left, right = sides(partner, outer, slice(0, ROWS), slice(0, ROWS))
    left, right = left * has_left, right * has_right
    out[...] = inner[...]
    lane = iota((ROWS, 128), 1)
    for k in range(2):
        low = left if k == 0 else pltpu.roll(left, 124, 1)
        out[k, :, 0:128] += jnp.where(lane < 2, low, 0.0)
        high = right if k == 0 else pltpu.roll(right, 124, 1)
        out[k, :, COLS - 128 : COLS] += jnp.where(lane >= 126, high, 0.0)
        out[k, 0:2, :] += above[4 * k + 2 : 4 * k + 4]
        out[k, ROWS - 2 : ROWS, :] += below[4 * k : 4 * k + 2]


def call(kernel, outs, args, scratch=(), smem=(), hbm=(), flops=0):
    scratch = list(scratch)

    def fetching(*refs):
        ins, rest = list(refs[: len(args)]), refs[len(args) :]
        buffers, sems = rest[-len(hbm) - 1 : -1], rest[-1]
        copies = [pltpu.make_async_copy(ins[at], buffers[i], sems.at[i]) for i, at in enumerate(hbm)]
        for copy in copies:
            copy.start()
        for copy in copies:
            copy.wait()
        for at, buffer in zip(hbm, buffers):
            ins[at] = buffer
        kernel(*ins, *rest[: -len(hbm) - 1])

    if hbm:
        scratch += [pltpu.VMEM(args[at].shape, args[at].dtype) for at in hbm]
        scratch += [pltpu.SemaphoreType.DMA((len(hbm),))]
    return pl.pallas_call(
        fetching if hbm else kernel,
        out_shape=outs,
        in_specs=[SMEM if at in smem else HBM if at in hbm else VMEM for at in range(len(args))],
        out_specs=jax.tree.map(lambda _: VMEM, outs),
        scratch_shapes=scratch,
        compiler_params=pltpu.CompilerParams(vmem_limit_bytes=24 * 1024 * 1024),
        cost_estimate=pl.CostEstimate(flops=flops, bytes_accessed=1 << 20, transcendentals=0),
    )(*args)


def body(
    n_cross, n_band, rasters, aerial, w_in, aerial_gain, b_in, w_conv1, b_conv1, w_proj, b_proj,
    w_ctx, w_up, b_up, w_head, b_head,
):
    cells = (n_cross - 1, n_band - 1)
    tie = lax.optimization_barrier

    def moved(x, source):
        route = []
        for cross in range(n_cross):
            for band in range(n_band):
                c, b = source(cross, band)
                route.append(((b % n_band) * n_cross + c % n_cross, band * n_cross + cross))
        return lax.ppermute(x, ("band", "cross"), route)

    def partner(x):
        return moved(x, lambda c, b: (c, b ^ 1))

    def outer(x):
        return moved(x, lambda c, b: (c, ((b + 1) ^ 1) - 1))

    def even_pair(x):
        return moved(x, lambda c, b: (c ^ 1, b))

    def odd_pair(x):
        return moved(x, lambda c, b: (((c + 1) ^ 1) - 1, b))

    def beside(x, u):
        return moved(x, lambda c, b: (c + u * (1 - 2 * (b % 2)), b - 2 + 4 * (b % 2)))

    rows, cols, message, stem_in = call(
        halo_kernel,
        [shape_of(32, COLS), shape_of(32, 128), shape_of(16, 128), shape_of(8 * ROWS, COLS, dtype=BF16)],
        [rasters, aerial],
        flops=8 * 10**10,
    )
    near, far = partner(message), outer(message)

    stem_args = [w_in.T, aerial_gain[None, :], b_in[None, :], w_conv1, b_conv1[None, :]]
    proj_args = [w_proj.T, b_proj[None, :], w_ctx]

    def inner(part, stem_in):
        count = FIRST if part == 0 else ROWS - FIRST
        return call(
            functools.partial(inner_kernel, part),
            [shape_of(count * CH, COLS, dtype=BF16), shape_of(CH, count // 4 * POOL_COLS)],
            [stem_in, *stem_args],
            [
                pltpu.VMEM((256, 128), BF16),
                pltpu.VMEM((256, 960), BF16),
                pltpu.VMEM(((count + 2) * 96, COLS), BF16),
            ],
            flops=4 * 10**9,
        )

    feat_low, sums_low = inner(0, stem_in)
    near, far, sums_low = tie((near, far, sums_low))
    even_out, odd_out = row_messages(cells, rows, near, far)
    even_out, odd_out, stem_in = tie((even_out, odd_out, stem_in))
    even_in, odd_in = even_pair(even_out), odd_pair(odd_out)
    feat_high, sums_high = inner(1, stem_in)

    rim_rows, rim_cols, pooled, own = call(
        functools.partial(rim_kernel, cells),
        [
            shape_of(2 * CH, COLS, dtype=BF16), shape_of(CH, 256, dtype=BF16), shape_of(CH, SPOTS, dtype=BF16),
            shape_of(2, CH, SPOTS, dtype=BF16),
        ],
        [rows, cols, near, far, even_in, odd_in, sums_low, sums_high, *stem_args],
    )

    own = own.at[1].set(partner(pooled))
    one, band = beside(own, -1), beside(own, 0)
    relay, two = outer(one), beside(own, 1)
    sent = dict(own=own, one=one, band=band)

    def context_call(kernel, phase, outs, args, scratch=(), **more):
        count = len(TILES[phase]) * WIDE
        buffers = [pltpu.VMEM((WIDE, count), BF16), pltpu.VMEM((count, 256), BF16)]
        return call(functools.partial(kernel, cells), outs, args, buffers + list(scratch), **more)

    context, head_w, rim_w, up_bias = context_call(
        early_kernel, 0,
        [
            shape_of(WIDE, SPOTS), shape_of(160, 20 * CH, dtype=BF16), shape_of(40, 4 * CH, dtype=BF16),
            shape_of(CH, 256),
        ],
        [*(sent[name] for name in PHASES[0]), *proj_args, w_head, b_up[None, :]],
    )
    relay, two, context = tie((relay, two, context))
    relay_p, two_p = partner(relay), partner(two)
    band_p, one_p = partner(band), partner(one)

    inner_logits, col_out, row_out = context_call(
        logits_kernel, 1,
        [shape_of(2, ROWS, COLS), shape_of(ROWS + 8, 128), shape_of(8, COLS)],
        [
            feat_low, feat_high, rim_rows, rim_cols, context, two, two_p, relay, relay_p, band_p, one_p,
            *proj_args, w_up, up_bias, head_w, rim_w, b_head,
        ],
        [
            pltpu.VMEM((POOL_ROWS * CH, 256), BF16),
            pltpu.VMEM((POOL_ROWS * CH, COLS), F32),
            pltpu.VMEM(((ROWS + 4) * CH, COLS), BF16),
        ],
        smem=(19,),
    )
    near, far = partner(col_out), outer(col_out)
    row_out = row_sums(cells, row_out, near, far)
    return call(
        functools.partial(sum_kernel, cells),
        shape_of(2, ROWS, COLS),
        [inner_logits, near, far, even_pair(row_out), odd_pair(row_out)],
    )


def solution(mesh):
    sizes = dict(mesh.shape)
    return jax.shard_map(
        functools.partial(body, sizes["cross"], sizes["band"]),
        mesh=mesh,
        in_specs=(P(None, "cross", "band"), P("cross", "band")) + (P(),) * 12,
        out_specs=P(None, "cross", "band"),
        check_vma=False,
    )
```

```python
import functools

import jax
import jax.numpy as jnp
from jax import lax
from jax.experimental import pallas as pl
from jax.experimental.pallas import tpu as pltpu
from jax.sharding import PartitionSpec as P

ROWS, COLS = 64, 512
CH, WIDE, KINDS = 32, 128, 8
POOL_ROWS, POOL_COLS = 16, 128
SPOTS = POOL_ROWS * POOL_COLS
FIRST = 16
HBM = pl.BlockSpec(memory_space=pltpu.HBM)
VMEM = pl.BlockSpec(memory_space=pltpu.VMEM)
SMEM = pl.BlockSpec(memory_space=pltpu.SMEM)
F32, BF16 = jnp.float32, jnp.bfloat16


def iota(shape, dim):
    return lax.broadcasted_iota(jnp.int32, shape, dim)


def shape_of(*dims, dtype=F32):
    return jax.ShapeDtypeStruct(dims, dtype)


def mm(a, b):
    return jnp.dot(a, b, preferred_element_type=F32)


def split(x):
    high = x.astype(BF16)
    return high, (x - high.astype(F32)).astype(BF16)


def column(row):
    count = row.shape[1]
    eye = iota((count, count), 0) == iota((count, count), 1)
    return jnp.sum(jnp.where(eye, row, 0.0), axis=1, keepdims=True)


def placed():
    return lax.axis_index("cross"), lax.axis_index("band")


def flags(last_cross, last_band):
    cross, band = placed()
    one = lambda truth: truth.astype(F32)
    return one(cross > 0), one(cross < last_cross), one(band > 0), one(band < last_band)


def kinds_of(w_in, gain, b_in, gains):
    lane = iota((CH, KINDS), 1)
    kinds = jnp.zeros((CH, KINDS), F32)
    parts = [w_in[k : k + 1, :] for k in range(4)] + [gain[...]] * gains + [b_in[...]]
    parts = [column(part) for part in parts]
    for kind, part in enumerate(parts):
        kinds = jnp.where(lane == kind, part, kinds)
    return kinds


def pool_weights():
    x, q = iota((COLS, POOL_COLS), 0), iota((COLS, POOL_COLS), 1)
    inner = (x // 4 == q) & (x > 0) & (x < COLS - 1)
    return jnp.where(inner, 1.0 / 16, 0.0).astype(BF16)


def halo_kernel(rasters, aerial, rows, cols, message, stem_in):
    ones, none = jnp.ones((1, COLS), F32), jnp.zeros((2, COLS), F32)
    for at, y in enumerate((0, 1, ROWS - 2, ROWS - 1)):
        parts = [rasters[kind, y : y + 1, :].astype(F32) for kind in range(4)]
        rows[at * 8 : (at + 1) * 8, :] = jnp.concatenate(parts + [aerial[y : y + 1, :], ones, none], axis=0)
    lane = iota((ROWS, 128), 1)
    packed = jnp.where((lane < 32) & (lane % 8 == 5), 1.0, 0.0)
    for at, x in enumerate((0, 1, COLS - 2, COLS - 1)):
        first = x // 128 * 128
        for kind in range(5):
            if kind < 4:
                slab = rasters[kind, :, first : first + 128].astype(F32)
            else:
                slab = aerial[:, first : first + 128]
            packed = jnp.where(lane == at * 8 + kind, slab[:, x - first : x - first + 1], packed)
    turned = jnp.transpose(jnp.concatenate([packed, jnp.zeros((128 - ROWS, 128), F32)], axis=0))
    cols[...] = turned[:32]
    message[...] = jnp.concatenate([turned[:8], turned[24:32]], axis=0)
    for y in range(0, ROWS, 8):
        values = jnp.concatenate([rasters[k, y : y + 8, :] for k in range(4)], axis=0).astype(F32)
        high, low = split(aerial[y : y + 8, :])
        tail = jnp.concatenate([jnp.ones((8, COLS), BF16), jnp.zeros((8, COLS), BF16)], axis=0)
        stem_in[y * 8 : y * 8 + 64, :] = jnp.concatenate([values.astype(BF16), high, low, tail], axis=0)


def sides(partner, outer, low, high):
    even = placed()[1] % 2 == 0
    left = jnp.where(even, outer[high], partner[high])
    right = jnp.where(even, partner[low], outer[low])
    return left, right


def row_messages(cells, rows, partner, outer):
    _, _, has_left, has_right = flags(*cells)
    left, right = sides(partner, outer, slice(0, 8), slice(8, 16))
    lane = lax.broadcasted_iota(jnp.int32, (8, 128), 1)

    def row(at, y):
        low, high = left[:, y : y + 1] * has_left, right[:, y : y + 1] * has_right
        side = jnp.where(lane == 0, high, jnp.where(lane == 1, low, 0.0))
        return jnp.concatenate([rows[at * 8 : (at + 1) * 8, :], side], axis=1)

    low, high = row(0, 0), row(3, ROWS - 1)
    even = placed()[0] % 2 == 0
    return jnp.where(even, high, low), jnp.where(even, low, high)


def inner_kernel(
    part, stem_in, w_in, gain, b_in, conv_w, conv_b, features, sums, stem_w, wide_w, stem3
):
    spread = jnp.where(iota((KINDS, 64), 1) // 8 == iota((KINDS, 64), 0), 1.0, 0.0).astype(BF16)
    same = iota((256, 64), 0) // CH == iota((256, 64), 1) % 8
    halves = []
    for piece in split(kinds_of(w_in, gain, b_in, 2)):
        rows = mm(jnp.concatenate([piece] * 8, axis=0), spread)
        halves.append(jnp.where(same, rows, 0.0))
    stem_w[...] = jnp.concatenate(halves, axis=1).astype(BF16)
    wide_w[...] = jnp.zeros(wide_w.shape, BF16)
    taps = conv_w[...]
    for y in range(8):
        wide_w[y * CH : (y + 1) * CH, y * 96 : y * 96 + 288] = taps
    pool_w = pool_weights()
    bias = jnp.broadcast_to(column(conv_b[...]), (CH, COLS))
    bias = jnp.concatenate([bias] * 8, axis=0)

    start, count = (0, FIRST) if part == 0 else (FIRST, ROWS - FIRST)
    blocks = range(max(start // 8 - 1, 0), min((start + count) // 8 + 1, ROWS // 8))
    base = start - 1
    edge = 0 if part == 0 else count + 1
    stem3[edge * 96 : (edge + 1) * 96, :] = jnp.zeros((96, COLS), BF16)
    for block in blocks:
        y = block * 8
        x = stem_in[y * 8 : y * 8 + 64, :]
        out = jnp.maximum(mm(stem_w[...], jnp.concatenate([x, x], axis=0)), 0.0)
        for r in range(8):
            at = y + r - base
            if at < 0 or at > count + 1:
                continue
            s = out[r * CH : (r + 1) * CH, :]
            parts = [pltpu.roll(s, 1, 1), s, pltpu.roll(s, COLS - 1, 1)]
            stem3[at * 96 : (at + 1) * 96, :] = jnp.concatenate(parts, axis=0).astype(BF16)

    for block in range(count // 8):
        out = mm(wide_w[...], stem3[block * 768 : block * 768 + 960, :])
        value = jnp.maximum(out + bias, 0.0).astype(BF16)
        features[block * 256 : (block + 1) * 256, :] = value
        means = mm(value, pool_w)
        for p in range(2):
            rows = [means[p * 128 + r * 32 : p * 128 + (r + 1) * 32, :] for r in range(4)]
            if part == 0 and block == 0 and p == 0:
                rows = rows[1:]
            if part == 1 and block == count // 8 - 1 and p == 1:
                rows = rows[:3]
            at = (block * 2 + p) * POOL_COLS
            sums[:, at : at + POOL_COLS] = sum(rows[1:], rows[0])


def rim_kernel(
    cells, rows, cols, partner, outer, even_message, odd_message, sums_low, sums_high,
    w_in, gain, b_in, conv_w, conv_b, rim_rows, rim_cols, pooled, own,
):
    has_above, has_below, has_left, has_right = flags(*cells)
    left, right = sides(partner, outer, slice(0, 8), slice(8, 16))
    left, right = left * has_left, right * has_right
    even = placed()[0] % 2 == 0
    above = jnp.where(even, odd_message[...], even_message[...]) * has_above
    below = jnp.where(even, even_message[...], odd_message[...]) * has_below
    kind_high, kind_low = split(kinds_of(w_in, gain, b_in, 1))
    stem_w = jnp.concatenate([kind_high, kind_high, kind_low], axis=1)
    bias = column(conv_b[...])

    def stem(x):
        high, low = split(x)
        high = high.astype(F32)
        stacked = jnp.concatenate([high, low.astype(F32), high], axis=0).astype(BF16)
        return jnp.maximum(mm(stem_w, stacked), 0.0)

    def conv(stacked):
        return jnp.maximum(mm(conv_w[...], stacked) + bias, 0.0).astype(BF16)

    def row(at):
        return rows[at * 8 : (at + 1) * 8, :]

    pool_w = pool_weights()
    row_sums = []
    trios = [(above[:, :COLS], row(0), row(1)), (row(2), row(3), below[:, :COLS])]
    for at, trio in enumerate(trios):
        stacked = []
        for x in trio:
            s = stem(x)
            stacked += [pltpu.roll(s, 1, 1), s, pltpu.roll(s, COLS - 1, 1)]
        value = conv(jnp.concatenate(stacked, axis=0).astype(BF16))
        rim_rows[at * CH : (at + 1) * CH, :] = value
        row_sums.append(mm(value, pool_w))

    lane = iota((8, 128), 1)

    def line(inside, top, bottom, x):
        top, bottom = top[:, x : x + 1], bottom[:, x : x + 1]
        return jnp.where(lane < ROWS, inside, jnp.where(lane == ROWS, bottom, 0.0)), top

    x_of = {-1: COLS + 1, COLS: COLS}
    lines = {-1: left, COLS: right}
    for at, x in enumerate((0, 1, COLS - 2, COLS - 1)):
        lines[x] = cols[at * 8 : (at + 1) * 8, :]
    columns = []
    for dx in (-1, 0, 1):
        low, low_top = line(lines[dx], above, below, x_of.get(dx, dx))
        x = COLS - 1 + dx
        high, high_top = line(lines[x], above, below, x_of.get(x, x))
        low = jnp.where(lane == 127, high_top, low)
        high = jnp.where(lane == 127, low_top, high)
        columns.append(stem(jnp.concatenate([low, high], axis=1)))
    s = jnp.concatenate(columns, axis=0)
    stacked = [pltpu.roll(s, 1, 1), s, pltpu.roll(s, 255, 1)]
    value = conv(jnp.concatenate(stacked, axis=0).astype(BF16))
    rim_cols[...] = value
    y, at = iota((256, 128), 0), iota((256, 128), 1)
    picked = (y < ROWS) & (y // 4 == at) | (y >= 128) & (y < 128 + ROWS) & (y // 4 - 16 == at)
    col_sums = mm(value, jnp.where(picked, 1.0 / 16, 0.0).astype(BF16))
    lane = iota((CH, POOL_COLS), 1)
    for p in range(POOL_ROWS):
        at = p * POOL_COLS
        near = sums_low if p < FIRST // 4 else sums_high
        first = at if p < FIRST // 4 else at - FIRST // 4 * POOL_COLS
        last = jnp.where(lane == POOL_COLS - 1, col_sums[:, 16 + p : 17 + p], 0.0)
        total = near[:, first : first + POOL_COLS] + jnp.where(lane == 0, col_sums[:, p : p + 1], last)
        if p == 0:
            total += row_sums[0]
        if p == POOL_ROWS - 1:
            total += row_sums[1]
        pooled[:, at : at + POOL_COLS] = total.astype(BF16)
        own[0, :, at : at + POOL_COLS] = total.astype(BF16)
    own[1, :, :] = jnp.zeros((CH, SPOTS), BF16)


def head_weights(w_head, row_y, row_count, col_y, col_count):
    shape = (10 * row_count, col_count * CH)
    rows = iota((10 * row_count, 2), 0) // row_count % 2 == iota((10 * row_count, 2), 1)
    pick = jnp.where(rows, 1.0, 0.0).astype(BF16)
    dx = iota((10 * row_count, 160), 0) // (2 * row_count) == iota((10 * row_count, 160), 1) // CH
    repeat = iota((160, shape[1]), 0) % CH == iota((160, shape[1]), 1) % CH
    repeat = jnp.where(repeat, 1.0, 0.0).astype(BF16)
    dy = row_y(iota(shape, 0) % row_count) - col_y(iota(shape, 1) // CH)
    total = jnp.zeros(shape, F32)
    for tap in range(5):
        taps = mm(pick, w_head[:, tap * 160 : (tap + 1) * 160])
        taps = mm(jnp.where(dx, taps, 0.0).astype(BF16), repeat)
        total = jnp.where(dy == tap - 2, taps, total)
    return total.astype(BF16)


MAPS = {
    (0, -2): ("band", 0), (0, -1): ("band", 1), (0, 0): ("own", 0), (0, 1): ("own", 1), (0, 2): ("band_p", 1),
    (-1, -2): ("one", 0), (-1, -1): ("one", 1), (-1, 0): ("relay_p", 0), (-1, 1): ("relay_p", 1), (-1, 2): ("two_p", 1),
    (1, -2): ("two", 0), (1, -1): ("two", 1), (1, 0): ("relay", 1), (1, 1): ("relay", 0), (1, 2): ("one_p", 1),
}
PHASES = (("own", "one", "band"), ("two", "two_p", "relay", "relay_p", "band_p", "one_p"))
TILES = [[at for at in range(15) if MAPS[(at // 5 - 1, at % 5 - 2)][0] in names] for names in PHASES]


def context_sum(cells, which, arrays, proj_w, proj_b, ctx_w, weights, proj, finish):
    last_cross, last_band = cells
    cross, band = placed()
    core = band % 2
    sign = 1 - 2 * core
    for k, at in enumerate(which):
        row, col = cross + (at // 5 - 1) * sign, band + (at % 5 - 2) * sign
        inside = (row >= 0) & (row <= last_cross) & (col >= 0) & (col <= last_band)
        one = ctx_w[:, at * WIDE : (at + 1) * WIDE]
        two = ctx_w[:, (14 - at) * WIDE : (15 - at) * WIDE]
        chosen = jnp.where(core == 0, one, two)
        weights[:, k * WIDE : (k + 1) * WIDE] = jnp.where(inside, chosen, jnp.zeros_like(chosen))
    p_bias = jnp.broadcast_to(column(proj_b[...]), (WIDE, 256))
    proj_w = jnp.transpose(proj_w[...].astype(F32)).astype(BF16)

    def project(spots):
        for k, tile in enumerate(which):
            name, half = MAPS[(tile // 5 - 1, tile % 5 - 2)]
            out = mm(proj_w, arrays[name][half, :, spots])
            proj[k * WIDE : (k + 1) * WIDE, spots] = jnp.maximum(out + p_bias, 0.0).astype(BF16)

    spots = [slice(at * 256, (at + 1) * 256) for at in range(SPOTS // 256)]
    project(spots[0])
    for at, spot in enumerate(spots):
        if at + 1 < len(spots):
            project(spots[at + 1])
        finish(at, spot, mm(weights[...], proj[:, spot]))


def early_kernel(cells, *refs):
    count = len(PHASES[0])
    arrays = dict(zip(PHASES[0], refs[:count]))
    proj_w, proj_b, ctx_w, w_head, up_b, context, head_w, rim_w, up_bias, weights, proj = refs[count:]
    up_bias[...] = jnp.broadcast_to(column(up_b[...]), (CH, 256))
    head_w[...] = head_weights(w_head[...], lambda r: r, 16, lambda r: r - 2, 20)
    outside = lambda r: jnp.where(r < 2, r - 2, ROWS - 2 + r)
    rim_w[...] = head_weights(w_head[...], outside, 4, lambda r: jnp.where(r < 2, r, ROWS - 4 + r), 4)
    own = TILES[0].index(7)

    def finish(at, spots, total):
        context[:, spots] = total + proj[own * WIDE : (own + 1) * WIDE, spots].astype(F32)

    context_sum(cells, TILES[0], arrays, proj_w, proj_b, ctx_w, weights, proj, finish)


def logits_kernel(
    cells, low, high, rim_rows, rim_cols, context, two, two_p, relay, relay_p, band_p, one_p,
    proj_w, proj_b, ctx_w, up_w, up_b, head_w, rim_w, head_b,
    logits, col_out, row_out, weights, proj, low_up, lifted, decoded,
):
    arrays = dict(zip(PHASES[1], (two, two_p, relay, relay_p, band_p, one_p)))

    def finish(part, spots, total):
        mixed = jnp.maximum(total + context[:, spots], 0.0).astype(BF16)
        up = mm(up_w[...], mixed) + up_b[...]
        high, low = split(up)
        both = [
            jnp.concatenate([high[:, h * 128 : (h + 1) * 128], low[:, h * 128 : (h + 1) * 128]], axis=1)
            for h in range(2)
        ]
        low_up[part * 64 : (part + 1) * 64, :] = jnp.concatenate(both, axis=0)

    context_sum(cells, TILES[1], arrays, proj_w, proj_b, ctx_w, weights, proj, finish)

    widen = jnp.where(
        iota((256, COLS), 0) % 128 == iota((256, COLS), 1) // 4, 1.0, 0.0
    ).astype(BF16)
    lifted[...] = mm(low_up[...], widen)

    decoded[0:64, :] = jnp.zeros((64, COLS), BF16)
    decoded[66 * CH :, :] = jnp.zeros((64, COLS), BF16)

    lane = iota((CH, 128), 1)
    columns = rim_cols[...].astype(F32)
    for y in range(ROWS):
        if y == 0:
            f = rim_rows[0:CH, :]
        elif y == ROWS - 1:
            f = rim_rows[CH : 2 * CH, :]
        else:
            at = (y if y < FIRST else y - FIRST) * CH
            f = (low if y < FIRST else high)[at : at + CH, :]
        f = f.astype(F32)
        first = jnp.where(lane == 0, columns[:, y : y + 1], f[:, :128])
        last = jnp.where(lane == 127, columns[:, 128 + y : 129 + y], f[:, COLS - 128 :])
        f = jnp.concatenate([first, f[:, 128 : COLS - 128], last], axis=1)
        value = f + lifted[y // 4 * CH : (y // 4 + 1) * CH, :]
        decoded[(y + 2) * CH : (y + 3) * CH, :] = jnp.maximum(value, 0.0).astype(BF16)

    def gather_taps(z, count):
        total = None
        for dx in range(5):
            part = z[dx * count : (dx + 1) * count, :]
            part = jnp.concatenate([part, jnp.zeros((count, 128), F32)], axis=1)
            if dx != 2:
                part = pltpu.roll(part, (dx - 2) % 640, 1)
            total = part if total is None else total + part
        return total

    lane16 = iota((16, 128), 1)
    first_lanes = (lane16 < 2) | (lane16 >= 126)

    def head(block, carry):
        first = pl.multiple_of(block * 16 * CH, 16 * CH)
        total = gather_taps(mm(head_w[...], decoded[pl.ds(first, 20 * CH), :]), 32)
        y = pl.multiple_of(block * 16, 16)
        for k in range(2):
            logits[k, pl.ds(y, 16), :] = total[k * 16 : (k + 1) * 16, :COLS] + head_b[k]
        rim = total[:, COLS:]
        col_out[pl.ds(y, 16), :] = jnp.where(first_lanes, rim[:16], pltpu.roll(rim[16:], 4, 1))
        return carry

    lax.fori_loop(0, ROWS // 16, head, 0, unroll=True)

    ends = jnp.concatenate([decoded[64:128, :], decoded[64 * CH : 66 * CH, :]], axis=0)
    total = gather_taps(mm(rim_w[...], ends), 8)
    row_out[...] = total[:, :COLS]
    col_out[ROWS : ROWS + 8, :] = total[:, COLS:]


def row_sums(cells, row_out, partner, outer):
    _, _, has_left, has_right = flags(*cells)
    corners = slice(ROWS, ROWS + 8)
    left, right = sides(partner, outer, corners, corners)
    lane = lax.broadcasted_iota(jnp.int32, (8, 128), 1)
    low = jnp.where(lane < 2, left * has_left, 0.0)
    high = jnp.where(lane >= 126, right * has_right, 0.0)
    return row_out + jnp.concatenate([low, jnp.zeros((8, COLS - 256), F32), high], axis=1)


def sum_kernel(cells, inner, partner, outer, even_message, odd_message, out):
    has_above, has_below, has_left, has_right = flags(*cells)
    even = placed()[0] % 2 == 0
    above = jnp.where(even, odd_message[...], even_message[...]) * has_above
    below = jnp.where(even, even_message[...], odd_message[...]) * has_below
    left, right = sides(partner, outer, slice(0, ROWS), slice(0, ROWS))
    left, right = left * has_left, right * has_right
    out[...] = inner[...]
    lane = iota((ROWS, 128), 1)
    for k in range(2):
        low = left if k == 0 else pltpu.roll(left, 124, 1)
        out[k, :, 0:128] += jnp.where(lane < 2, low, 0.0)
        high = right if k == 0 else pltpu.roll(right, 124, 1)
        out[k, :, COLS - 128 : COLS] += jnp.where(lane >= 126, high, 0.0)
        out[k, 0:2, :] += above[4 * k + 2 : 4 * k + 4]
        out[k, ROWS - 2 : ROWS, :] += below[4 * k : 4 * k + 2]


def call(kernel, outs, args, scratch=(), smem=(), hbm=(), flops=0):
    scratch = list(scratch)

    def fetching(*refs):
        ins, rest = list(refs[: len(args)]), refs[len(args) :]
        buffers, sems = rest[-len(hbm) - 1 : -1], rest[-1]
        copies = [pltpu.make_async_copy(ins[at], buffers[i], sems.at[i]) for i, at in enumerate(hbm)]
        for copy in copies:
            copy.start()
        for copy in copies:
            copy.wait()
        for at, buffer in zip(hbm, buffers):
            ins[at] = buffer
        kernel(*ins, *rest[: -len(hbm) - 1])

    if hbm:
        scratch += [pltpu.VMEM(args[at].shape, args[at].dtype) for at in hbm]
        scratch += [pltpu.SemaphoreType.DMA((len(hbm),))]
    return pl.pallas_call(
        fetching if hbm else kernel,
        out_shape=outs,
        in_specs=[SMEM if at in smem else HBM if at in hbm else VMEM for at in range(len(args))],
        out_specs=jax.tree.map(lambda _: VMEM, outs),
        scratch_shapes=scratch,
        compiler_params=pltpu.CompilerParams(vmem_limit_bytes=24 * 1024 * 1024),
        cost_estimate=pl.CostEstimate(flops=flops, bytes_accessed=1 << 20, transcendentals=0),
    )(*args)


def body(
    n_cross, n_band, rasters, aerial, w_in, aerial_gain, b_in, w_conv1, b_conv1, w_proj, b_proj,
    w_ctx, w_up, b_up, w_head, b_head,
):
    cells = (n_cross - 1, n_band - 1)
    tie = lax.optimization_barrier

    def moved(x, source):
        route = []
        for cross in range(n_cross):
            for band in range(n_band):
                c, b = source(cross, band)
                route.append(((b % n_band) * n_cross + c % n_cross, band * n_cross + cross))
        return lax.ppermute(x, ("band", "cross"), route)

    def partner(x):
        return moved(x, lambda c, b: (c, b ^ 1))

    def outer(x):
        return moved(x, lambda c, b: (c, ((b + 1) ^ 1) - 1))

    def even_pair(x):
        return moved(x, lambda c, b: (c ^ 1, b))

    def odd_pair(x):
        return moved(x, lambda c, b: (((c + 1) ^ 1) - 1, b))

    def beside(x, u):
        return moved(x, lambda c, b: (c + u * (1 - 2 * (b % 2)), b - 2 + 4 * (b % 2)))

    rows, cols, message, stem_in = call(
        halo_kernel,
        [shape_of(32, COLS), shape_of(32, 128), shape_of(16, 128), shape_of(8 * ROWS, COLS, dtype=BF16)],
        [rasters, aerial],
        flops=8 * 10**10,
    )
    near, far = partner(message), outer(message)

    stem_args = [w_in.T, aerial_gain[None, :], b_in[None, :], w_conv1, b_conv1[None, :]]
    proj_args = [w_proj.T, b_proj[None, :], w_ctx]

    def inner(part, stem_in):
        count = FIRST if part == 0 else ROWS - FIRST
        return call(
            functools.partial(inner_kernel, part),
            [shape_of(count * CH, COLS, dtype=BF16), shape_of(CH, count // 4 * POOL_COLS)],
            [stem_in, *stem_args],
            [
                pltpu.VMEM((256, 128), BF16),
                pltpu.VMEM((256, 960), BF16),
                pltpu.VMEM(((count + 2) * 96, COLS), BF16),
            ],
            flops=4 * 10**9,
        )

    feat_low, sums_low = inner(0, stem_in)
    near, far, sums_low = tie((near, far, sums_low))
    even_out, odd_out = row_messages(cells, rows, near, far)
    even_out, odd_out, stem_in = tie((even_out, odd_out, stem_in))
    even_in, odd_in = even_pair(even_out), odd_pair(odd_out)
    feat_high, sums_high = inner(1, stem_in)

    rim_rows, rim_cols, pooled, own = call(
        functools.partial(rim_kernel, cells),
        [
            shape_of(2 * CH, COLS, dtype=BF16), shape_of(CH, 256, dtype=BF16), shape_of(CH, SPOTS, dtype=BF16),
            shape_of(2, CH, SPOTS, dtype=BF16),
        ],
        [rows, cols, near, far, even_in, odd_in, sums_low, sums_high, *stem_args],
    )

    own = own.at[1].set(partner(pooled))
    one, band = beside(own, -1), beside(own, 0)
    relay, two = outer(one), beside(own, 1)
    sent = dict(own=own, one=one, band=band)

    def context_call(kernel, phase, outs, args, scratch=(), **more):
        count = len(TILES[phase]) * WIDE
        buffers = [pltpu.VMEM((WIDE, count), BF16), pltpu.VMEM((count, SPOTS), BF16)]
        return call(functools.partial(kernel, cells), outs, args, buffers + list(scratch), **more)

    context, head_w, rim_w, up_bias = context_call(
        early_kernel, 0,
        [
            shape_of(WIDE, SPOTS), shape_of(160, 20 * CH, dtype=BF16), shape_of(40, 4 * CH, dtype=BF16),
            shape_of(CH, 256),
        ],
        [*(sent[name] for name in PHASES[0]), *proj_args, w_head, b_up[None, :]],
    )
    relay, two, context = tie((relay, two, context))
    relay_p, two_p = partner(relay), partner(two)
    band_p, one_p = partner(band), partner(one)

    inner_logits, col_out, row_out = context_call(
        logits_kernel, 1,
        [shape_of(2, ROWS, COLS), shape_of(ROWS + 8, 128), shape_of(8, COLS)],
        [
            feat_low, feat_high, rim_rows, rim_cols, context, two, two_p, relay, relay_p, band_p, one_p,
            *proj_args, w_up, up_bias, head_w, rim_w, b_head,
        ],
        [
            pltpu.VMEM((POOL_ROWS * CH, 256), BF16),
            pltpu.VMEM((POOL_ROWS * CH, COLS), F32),
            pltpu.VMEM(((ROWS + 4) * CH, COLS), BF16),
        ],
        smem=(19,),
    )
    near, far = partner(col_out), outer(col_out)
    row_out = row_sums(cells, row_out, near, far)
    return call(
        functools.partial(sum_kernel, cells),
        shape_of(2, ROWS, COLS),
        [inner_logits, near, far, even_pair(row_out), odd_pair(row_out)],
    )


def solution(mesh):
    sizes = dict(mesh.shape)
    return jax.shard_map(
        functools.partial(body, sizes["cross"], sizes["band"]),
        mesh=mesh,
        in_specs=(P(None, "cross", "band"), P("cross", "band")) + (P(),) * 12,
        out_specs=P(None, "cross", "band"),
        check_vma=False,
    )
```

```python
import functools

import jax
import jax.numpy as jnp
from jax import lax
from jax.experimental import pallas as pl
from jax.experimental.pallas import tpu as pltpu
from jax.sharding import PartitionSpec as P

ROWS, COLS = 64, 512
CH, WIDE, KINDS = 32, 128, 8
POOL_ROWS, POOL_COLS = 16, 128
SPOTS = POOL_ROWS * POOL_COLS
FIRST = 8
HBM = pl.BlockSpec(memory_space=pltpu.HBM)
VMEM = pl.BlockSpec(memory_space=pltpu.VMEM)
SMEM = pl.BlockSpec(memory_space=pltpu.SMEM)
F32, BF16 = jnp.float32, jnp.bfloat16


def iota(shape, dim):
    return lax.broadcasted_iota(jnp.int32, shape, dim)


def shape_of(*dims, dtype=F32):
    return jax.ShapeDtypeStruct(dims, dtype)


def mm(a, b):
    return jnp.dot(a, b, preferred_element_type=F32)


def split(x):
    high = x.astype(BF16)
    return high, (x - high.astype(F32)).astype(BF16)


def column(row):
    count = row.shape[1]
    eye = iota((count, count), 0) == iota((count, count), 1)
    return jnp.sum(jnp.where(eye, row, 0.0), axis=1, keepdims=True)


def placed():
    return lax.axis_index("cross"), lax.axis_index("band")


def flags(last_cross, last_band):
    cross, band = placed()
    one = lambda truth: truth.astype(F32)
    return one(cross > 0), one(cross < last_cross), one(band > 0), one(band < last_band)


def kinds_of(w_in, gain, b_in, gains):
    lane = iota((CH, KINDS), 1)
    kinds = jnp.zeros((CH, KINDS), F32)
    parts = [w_in[k : k + 1, :] for k in range(4)] + [gain[...]] * gains + [b_in[...]]
    parts = [column(part) for part in parts]
    for kind, part in enumerate(parts):
        kinds = jnp.where(lane == kind, part, kinds)
    return kinds


def pool_weights():
    x, q = iota((COLS, POOL_COLS), 0), iota((COLS, POOL_COLS), 1)
    inner = (x // 4 == q) & (x > 0) & (x < COLS - 1)
    return jnp.where(inner, 1.0 / 16, 0.0).astype(BF16)


def halo_kernel(rasters, aerial, rows, cols, message, stem_in):
    ones, none = jnp.ones((1, COLS), F32), jnp.zeros((2, COLS), F32)
    for at, y in enumerate((0, 1, ROWS - 2, ROWS - 1)):
        parts = [rasters[kind, y : y + 1, :].astype(F32) for kind in range(4)]
        rows[at * 8 : (at + 1) * 8, :] = jnp.concatenate(parts + [aerial[y : y + 1, :], ones, none], axis=0)
    lane = iota((ROWS, 128), 1)
    packed = jnp.where((lane < 32) & (lane % 8 == 5), 1.0, 0.0)
    for at, x in enumerate((0, 1, COLS - 2, COLS - 1)):
        first = x // 128 * 128
        for kind in range(5):
            if kind < 4:
                slab = rasters[kind, :, first : first + 128].astype(F32)
            else:
                slab = aerial[:, first : first + 128]
            packed = jnp.where(lane == at * 8 + kind, slab[:, x - first : x - first + 1], packed)
    turned = jnp.transpose(jnp.concatenate([packed, jnp.zeros((128 - ROWS, 128), F32)], axis=0))
    cols[...] = turned[:32]
    message[...] = jnp.concatenate([turned[:8], turned[24:32]], axis=0)
    for y in range(0, ROWS, 8):
        values = jnp.concatenate([rasters[k, y : y + 8, :] for k in range(4)], axis=0).astype(F32)
        high, low = split(aerial[y : y + 8, :])
        tail = jnp.concatenate([jnp.ones((8, COLS), BF16), jnp.zeros((8, COLS), BF16)], axis=0)
        stem_in[y * 8 : y * 8 + 64, :] = jnp.concatenate([values.astype(BF16), high, low, tail], axis=0)


def sides(partner, outer, low, high):
    even = placed()[1] % 2 == 0
    left = jnp.where(even, outer[high], partner[high])
    right = jnp.where(even, partner[low], outer[low])
    return left, right


def row_messages(cells, rows, partner, outer):
    _, _, has_left, has_right = flags(*cells)
    left, right = sides(partner, outer, slice(0, 8), slice(8, 16))
    lane = lax.broadcasted_iota(jnp.int32, (8, 128), 1)

    def row(at, y):
        low, high = left[:, y : y + 1] * has_left, right[:, y : y + 1] * has_right
        side = jnp.where(lane == 0, high, jnp.where(lane == 1, low, 0.0))
        return jnp.concatenate([rows[at * 8 : (at + 1) * 8, :], side], axis=1)

    low, high = row(0, 0), row(3, ROWS - 1)
    even = placed()[0] % 2 == 0
    return jnp.where(even, high, low), jnp.where(even, low, high)


def inner_kernel(
    part, stem_in, w_in, gain, b_in, conv_w, conv_b, features, sums, stem_w, wide_w, stem3
):
    spread = jnp.where(iota((KINDS, 64), 1) // 8 == iota((KINDS, 64), 0), 1.0, 0.0).astype(BF16)
    same = iota((256, 64), 0) // CH == iota((256, 64), 1) % 8
    halves = []
    for piece in split(kinds_of(w_in, gain, b_in, 2)):
        rows = mm(jnp.concatenate([piece] * 8, axis=0), spread)
        halves.append(jnp.where(same, rows, 0.0))
    stem_w[...] = jnp.concatenate(halves, axis=1).astype(BF16)
    wide_w[...] = jnp.zeros(wide_w.shape, BF16)
    taps = conv_w[...]
    for y in range(8):
        wide_w[y * CH : (y + 1) * CH, y * 96 : y * 96 + 288] = taps
    pool_w = pool_weights()
    bias = jnp.broadcast_to(column(conv_b[...]), (CH, COLS))
    bias = jnp.concatenate([bias] * 8, axis=0)

    start, count = (0, FIRST) if part == 0 else (FIRST, ROWS - FIRST)
    blocks = range(max(start // 8 - 1, 0), min((start + count) // 8 + 1, ROWS // 8))
    base = start - 1
    edge = 0 if part == 0 else count + 1
    stem3[edge * 96 : (edge + 1) * 96, :] = jnp.zeros((96, COLS), BF16)
    for block in blocks:
        y = block * 8
        x = stem_in[y * 8 : y * 8 + 64, :]
        out = jnp.maximum(mm(stem_w[...], jnp.concatenate([x, x], axis=0)), 0.0)
        for r in range(8):
            at = y + r - base
            if at < 0 or at > count + 1:
                continue
            s = out[r * CH : (r + 1) * CH, :]
            parts = [pltpu.roll(s, 1, 1), s, pltpu.roll(s, COLS - 1, 1)]
            stem3[at * 96 : (at + 1) * 96, :] = jnp.concatenate(parts, axis=0).astype(BF16)

    for block in range(count // 8):
        out = mm(wide_w[...], stem3[block * 768 : block * 768 + 960, :])
        value = jnp.maximum(out + bias, 0.0).astype(BF16)
        features[block * 256 : (block + 1) * 256, :] = value
        means = mm(value, pool_w)
        for p in range(2):
            rows = [means[p * 128 + r * 32 : p * 128 + (r + 1) * 32, :] for r in range(4)]
            if part == 0 and block == 0 and p == 0:
                rows = rows[1:]
            if part == 1 and block == count // 8 - 1 and p == 1:
                rows = rows[:3]
            at = (block * 2 + p) * POOL_COLS
            sums[:, at : at + POOL_COLS] = sum(rows[1:], rows[0])


def rim_kernel(
    cells, rows, cols, partner, outer, even_message, odd_message, sums_low, sums_high,
    w_in, gain, b_in, conv_w, conv_b, rim_rows, rim_cols, pooled, own,
):
    has_above, has_below, has_left, has_right = flags(*cells)
    left, right = sides(partner, outer, slice(0, 8), slice(8, 16))
    left, right = left * has_left, right * has_right
    even = placed()[0] % 2 == 0
    above = jnp.where(even, odd_message[...], even_message[...]) * has_above
    below = jnp.where(even, even_message[...], odd_message[...]) * has_below
    kind_high, kind_low = split(kinds_of(w_in, gain, b_in, 1))
    stem_w = jnp.concatenate([kind_high, kind_high, kind_low], axis=1)
    bias = column(conv_b[...])

    def stem(x):
        high, low = split(x)
        high = high.astype(F32)
        stacked = jnp.concatenate([high, low.astype(F32), high], axis=0).astype(BF16)
        return jnp.maximum(mm(stem_w, stacked), 0.0)

    def conv(stacked):
        return jnp.maximum(mm(conv_w[...], stacked) + bias, 0.0).astype(BF16)

    def row(at):
        return rows[at * 8 : (at + 1) * 8, :]

    pool_w = pool_weights()
    row_sums = []
    trios = [(above[:, :COLS], row(0), row(1)), (row(2), row(3), below[:, :COLS])]
    for at, trio in enumerate(trios):
        stacked = []
        for x in trio:
            s = stem(x)
            stacked += [pltpu.roll(s, 1, 1), s, pltpu.roll(s, COLS - 1, 1)]
        value = conv(jnp.concatenate(stacked, axis=0).astype(BF16))
        rim_rows[at * CH : (at + 1) * CH, :] = value
        row_sums.append(mm(value, pool_w))

    lane = iota((8, 128), 1)

    def line(inside, top, bottom, x):
        top, bottom = top[:, x : x + 1], bottom[:, x : x + 1]
        return jnp.where(lane < ROWS, inside, jnp.where(lane == ROWS, bottom, 0.0)), top

    x_of = {-1: COLS + 1, COLS: COLS}
    lines = {-1: left, COLS: right}
    for at, x in enumerate((0, 1, COLS - 2, COLS - 1)):
        lines[x] = cols[at * 8 : (at + 1) * 8, :]
    columns = []
    for dx in (-1, 0, 1):
        low, low_top = line(lines[dx], above, below, x_of.get(dx, dx))
        x = COLS - 1 + dx
        high, high_top = line(lines[x], above, below, x_of.get(x, x))
        low = jnp.where(lane == 127, high_top, low)
        high = jnp.where(lane == 127, low_top, high)
        columns.append(stem(jnp.concatenate([low, high], axis=1)))
    s = jnp.concatenate(columns, axis=0)
    stacked = [pltpu.roll(s, 1, 1), s, pltpu.roll(s, 255, 1)]
    value = conv(jnp.concatenate(stacked, axis=0).astype(BF16))
    rim_cols[...] = value
    y, at = iota((256, 128), 0), iota((256, 128), 1)
    picked = (y < ROWS) & (y // 4 == at) | (y >= 128) & (y < 128 + ROWS) & (y // 4 - 16 == at)
    col_sums = mm(value, jnp.where(picked, 1.0 / 16, 0.0).astype(BF16))
    lane = iota((CH, POOL_COLS), 1)
    for p in range(POOL_ROWS):
        at = p * POOL_COLS
        near = sums_low if p < FIRST // 4 else sums_high
        first = at if p < FIRST // 4 else at - FIRST // 4 * POOL_COLS
        last = jnp.where(lane == POOL_COLS - 1, col_sums[:, 16 + p : 17 + p], 0.0)
        total = near[:, first : first + POOL_COLS] + jnp.where(lane == 0, col_sums[:, p : p + 1], last)
        if p == 0:
            total += row_sums[0]
        if p == POOL_ROWS - 1:
            total += row_sums[1]
        pooled[:, at : at + POOL_COLS] = total.astype(BF16)
        own[0, :, at : at + POOL_COLS] = total.astype(BF16)
    own[1, :, :] = jnp.zeros((CH, SPOTS), BF16)


def head_weights(w_head, row_y, row_count, col_y, col_count):
    shape = (10 * row_count, col_count * CH)
    rows = iota((10 * row_count, 2), 0) // row_count % 2 == iota((10 * row_count, 2), 1)
    pick = jnp.where(rows, 1.0, 0.0).astype(BF16)
    dx = iota((10 * row_count, 160), 0) // (2 * row_count) == iota((10 * row_count, 160), 1) // CH
    repeat = iota((160, shape[1]), 0) % CH == iota((160, shape[1]), 1) % CH
    repeat = jnp.where(repeat, 1.0, 0.0).astype(BF16)
    dy = row_y(iota(shape, 0) % row_count) - col_y(iota(shape, 1) // CH)
    total = jnp.zeros(shape, F32)
    for tap in range(5):
        taps = mm(pick, w_head[:, tap * 160 : (tap + 1) * 160])
        taps = mm(jnp.where(dx, taps, 0.0).astype(BF16), repeat)
        total = jnp.where(dy == tap - 2, taps, total)
    return total.astype(BF16)


MAPS = {
    (0, -2): ("band", 0), (0, -1): ("band", 1), (0, 0): ("own", 0), (0, 1): ("own", 1), (0, 2): ("band_p", 1),
    (-1, -2): ("one", 0), (-1, -1): ("one", 1), (-1, 0): ("relay_p", 0), (-1, 1): ("relay_p", 1), (-1, 2): ("two_p", 1),
    (1, -2): ("two", 0), (1, -1): ("two", 1), (1, 0): ("relay", 1), (1, 1): ("relay", 0), (1, 2): ("one_p", 1),
}
PHASES = (("own", "one", "band"), ("two", "two_p", "relay", "relay_p", "band_p", "one_p"))
TILES = [[at for at in range(15) if MAPS[(at // 5 - 1, at % 5 - 2)][0] in names] for names in PHASES]


def context_sum(cells, which, arrays, proj_w, proj_b, ctx_w, weights, proj, finish):
    last_cross, last_band = cells
    cross, band = placed()
    core = band % 2
    sign = 1 - 2 * core
    for k, at in enumerate(which):
        row, col = cross + (at // 5 - 1) * sign, band + (at % 5 - 2) * sign
        inside = (row >= 0) & (row <= last_cross) & (col >= 0) & (col <= last_band)
        one = ctx_w[:, at * WIDE : (at + 1) * WIDE]
        two = ctx_w[:, (14 - at) * WIDE : (15 - at) * WIDE]
        chosen = jnp.where(core == 0, one, two)
        weights[:, k * WIDE : (k + 1) * WIDE] = jnp.where(inside, chosen, jnp.zeros_like(chosen))
    p_bias = jnp.broadcast_to(column(proj_b[...]), (WIDE, 256))
    proj_w = jnp.transpose(proj_w[...].astype(F32)).astype(BF16)

    def project(spots):
        for k, tile in enumerate(which):
            name, half = MAPS[(tile // 5 - 1, tile % 5 - 2)]
            out = mm(proj_w, arrays[name][half, :, spots])
            proj[k * WIDE : (k + 1) * WIDE, spots] = jnp.maximum(out + p_bias, 0.0).astype(BF16)

    spots = [slice(at * 256, (at + 1) * 256) for at in range(SPOTS // 256)]
    project(spots[0])
    for at, spot in enumerate(spots):
        if at + 1 < len(spots):
            project(spots[at + 1])
        finish(at, spot, mm(weights[...], proj[:, spot]))


def early_kernel(cells, *refs):
    count = len(PHASES[0])
    arrays = dict(zip(PHASES[0], refs[:count]))
    proj_w, proj_b, ctx_w, w_head, up_b, context, head_w, rim_w, up_bias, weights, proj = refs[count:]
    up_bias[...] = jnp.broadcast_to(column(up_b[...]), (CH, 256))
    head_w[...] = head_weights(w_head[...], lambda r: r, 16, lambda r: r - 2, 20)
    outside = lambda r: jnp.where(r < 2, r - 2, ROWS - 2 + r)
    rim_w[...] = head_weights(w_head[...], outside, 4, lambda r: jnp.where(r < 2, r, ROWS - 4 + r), 4)
    own = TILES[0].index(7)

    def finish(at, spots, total):
        context[:, spots] = total + proj[own * WIDE : (own + 1) * WIDE, spots].astype(F32)

    context_sum(cells, TILES[0], arrays, proj_w, proj_b, ctx_w, weights, proj, finish)


def logits_kernel(
    cells, low, high, rim_rows, rim_cols, context, two, two_p, relay, relay_p, band_p, one_p,
    proj_w, proj_b, ctx_w, up_w, up_b, head_w, rim_w, head_b,
    logits, col_out, row_out, weights, proj, low_up, lifted, decoded,
):
    arrays = dict(zip(PHASES[1], (two, two_p, relay, relay_p, band_p, one_p)))

    def finish(part, spots, total):
        mixed = jnp.maximum(total + context[:, spots], 0.0).astype(BF16)
        up = mm(up_w[...], mixed) + up_b[...]
        high, low = split(up)
        both = [
            jnp.concatenate([high[:, h * 128 : (h + 1) * 128], low[:, h * 128 : (h + 1) * 128]], axis=1)
            for h in range(2)
        ]
        low_up[part * 64 : (part + 1) * 64, :] = jnp.concatenate(both, axis=0)

    context_sum(cells, TILES[1], arrays, proj_w, proj_b, ctx_w, weights, proj, finish)

    widen = jnp.where(
        iota((256, COLS), 0) % 128 == iota((256, COLS), 1) // 4, 1.0, 0.0
    ).astype(BF16)
    lifted[...] = mm(low_up[...], widen)

    decoded[0:64, :] = jnp.zeros((64, COLS), BF16)
    decoded[66 * CH :, :] = jnp.zeros((64, COLS), BF16)

    lane = iota((CH, 128), 1)
    columns = rim_cols[...].astype(F32)
    for y in range(ROWS):
        if y == 0:
            f = rim_rows[0:CH, :]
        elif y == ROWS - 1:
            f = rim_rows[CH : 2 * CH, :]
        else:
            at = (y if y < FIRST else y - FIRST) * CH
            f = (low if y < FIRST else high)[at : at + CH, :]
        f = f.astype(F32)
        first = jnp.where(lane == 0, columns[:, y : y + 1], f[:, :128])
        last = jnp.where(lane == 127, columns[:, 128 + y : 129 + y], f[:, COLS - 128 :])
        f = jnp.concatenate([first, f[:, 128 : COLS - 128], last], axis=1)
        value = f + lifted[y // 4 * CH : (y // 4 + 1) * CH, :]
        decoded[(y + 2) * CH : (y + 3) * CH, :] = jnp.maximum(value, 0.0).astype(BF16)

    def gather_taps(z, count):
        total = None
        for dx in range(5):
            part = z[dx * count : (dx + 1) * count, :]
            part = jnp.concatenate([part, jnp.zeros((count, 128), F32)], axis=1)
            if dx != 2:
                part = pltpu.roll(part, (dx - 2) % 640, 1)
            total = part if total is None else total + part
        return total

    lane16 = iota((16, 128), 1)
    first_lanes = (lane16 < 2) | (lane16 >= 126)

    def head(block, carry):
        first = pl.multiple_of(block * 16 * CH, 16 * CH)
        total = gather_taps(mm(head_w[...], decoded[pl.ds(first, 20 * CH), :]), 32)
        y = pl.multiple_of(block * 16, 16)
        for k in range(2):
            logits[k, pl.ds(y, 16), :] = total[k * 16 : (k + 1) * 16, :COLS] + head_b[k]
        rim = total[:, COLS:]
        col_out[pl.ds(y, 16), :] = jnp.where(first_lanes, rim[:16], pltpu.roll(rim[16:], 4, 1))
        return carry

    lax.fori_loop(0, ROWS // 16, head, 0, unroll=True)

    ends = jnp.concatenate([decoded[64:128, :], decoded[64 * CH : 66 * CH, :]], axis=0)
    total = gather_taps(mm(rim_w[...], ends), 8)
    row_out[...] = total[:, :COLS]
    col_out[ROWS : ROWS + 8, :] = total[:, COLS:]


def row_sums(cells, row_out, partner, outer):
    _, _, has_left, has_right = flags(*cells)
    corners = slice(ROWS, ROWS + 8)
    left, right = sides(partner, outer, corners, corners)
    lane = lax.broadcasted_iota(jnp.int32, (8, 128), 1)
    low = jnp.where(lane < 2, left * has_left, 0.0)
    high = jnp.where(lane >= 126, right * has_right, 0.0)
    return row_out + jnp.concatenate([low, jnp.zeros((8, COLS - 256), F32), high], axis=1)


def sum_kernel(cells, inner, partner, outer, even_message, odd_message, out):
    has_above, has_below, has_left, has_right = flags(*cells)
    even = placed()[0] % 2 == 0
    above = jnp.where(even, odd_message[...], even_message[...]) * has_above
    below = jnp.where(even, even_message[...], odd_message[...]) * has_below
    left, right = sides(partner, outer, slice(0, ROWS), slice(0, ROWS))
    left, right = left * has_left, right * has_right
    out[...] = inner[...]
    lane = iota((ROWS, 128), 1)
    for k in range(2):
        low = left if k == 0 else pltpu.roll(left, 124, 1)
        out[k, :, 0:128] += jnp.where(lane < 2, low, 0.0)
        high = right if k == 0 else pltpu.roll(right, 124, 1)
        out[k, :, COLS - 128 : COLS] += jnp.where(lane >= 126, high, 0.0)
        out[k, 0:2, :] += above[4 * k + 2 : 4 * k + 4]
        out[k, ROWS - 2 : ROWS, :] += below[4 * k : 4 * k + 2]


def call(kernel, outs, args, scratch=(), smem=(), hbm=(), flops=0):
    scratch = list(scratch)

    def fetching(*refs):
        ins, rest = list(refs[: len(args)]), refs[len(args) :]
        buffers, sems = rest[-len(hbm) - 1 : -1], rest[-1]
        copies = [pltpu.make_async_copy(ins[at], buffers[i], sems.at[i]) for i, at in enumerate(hbm)]
        for copy in copies:
            copy.start()
        for copy in copies:
            copy.wait()
        for at, buffer in zip(hbm, buffers):
            ins[at] = buffer
        kernel(*ins, *rest[: -len(hbm) - 1])

    if hbm:
        scratch += [pltpu.VMEM(args[at].shape, args[at].dtype) for at in hbm]
        scratch += [pltpu.SemaphoreType.DMA((len(hbm),))]
    return pl.pallas_call(
        fetching if hbm else kernel,
        out_shape=outs,
        in_specs=[SMEM if at in smem else HBM if at in hbm else VMEM for at in range(len(args))],
        out_specs=jax.tree.map(lambda _: VMEM, outs),
        scratch_shapes=scratch,
        compiler_params=pltpu.CompilerParams(vmem_limit_bytes=24 * 1024 * 1024),
        cost_estimate=pl.CostEstimate(flops=flops, bytes_accessed=1 << 20, transcendentals=0),
    )(*args)


def body(
    n_cross, n_band, rasters, aerial, w_in, aerial_gain, b_in, w_conv1, b_conv1, w_proj, b_proj,
    w_ctx, w_up, b_up, w_head, b_head,
):
    cells = (n_cross - 1, n_band - 1)
    tie = lax.optimization_barrier

    def moved(x, source):
        route = []
        for cross in range(n_cross):
            for band in range(n_band):
                c, b = source(cross, band)
                route.append(((b % n_band) * n_cross + c % n_cross, band * n_cross + cross))
        return lax.ppermute(x, ("band", "cross"), route)

    def partner(x):
        return moved(x, lambda c, b: (c, b ^ 1))

    def outer(x):
        return moved(x, lambda c, b: (c, ((b + 1) ^ 1) - 1))

    def even_pair(x):
        return moved(x, lambda c, b: (c ^ 1, b))

    def odd_pair(x):
        return moved(x, lambda c, b: (((c + 1) ^ 1) - 1, b))

    def beside(x, u):
        return moved(x, lambda c, b: (c + u * (1 - 2 * (b % 2)), b - 2 + 4 * (b % 2)))

    rows, cols, message, stem_in = call(
        halo_kernel,
        [shape_of(32, COLS), shape_of(32, 128), shape_of(16, 128), shape_of(8 * ROWS, COLS, dtype=BF16)],
        [rasters, aerial],
        flops=8 * 10**10,
    )
    near, far = partner(message), outer(message)

    stem_args = [w_in.T, aerial_gain[None, :], b_in[None, :], w_conv1, b_conv1[None, :]]
    proj_args = [w_proj.T, b_proj[None, :], w_ctx]

    def inner(part, stem_in):
        count = FIRST if part == 0 else ROWS - FIRST
        return call(
            functools.partial(inner_kernel, part),
            [shape_of(count * CH, COLS, dtype=BF16), shape_of(CH, count // 4 * POOL_COLS)],
            [stem_in, *stem_args],
            [
                pltpu.VMEM((256, 128), BF16),
                pltpu.VMEM((256, 960), BF16),
                pltpu.VMEM(((count + 2) * 96, COLS), BF16),
            ],
            flops=4 * 10**9,
        )

    feat_low, sums_low = inner(0, stem_in)
    near, far, sums_low = tie((near, far, sums_low))
    even_out, odd_out = row_messages(cells, rows, near, far)
    even_out, odd_out, stem_in = tie((even_out, odd_out, stem_in))
    even_in, odd_in = even_pair(even_out), odd_pair(odd_out)
    feat_high, sums_high = inner(1, stem_in)

    rim_rows, rim_cols, pooled, own = call(
        functools.partial(rim_kernel, cells),
        [
            shape_of(2 * CH, COLS, dtype=BF16), shape_of(CH, 256, dtype=BF16), shape_of(CH, SPOTS, dtype=BF16),
            shape_of(2, CH, SPOTS, dtype=BF16),
        ],
        [rows, cols, near, far, even_in, odd_in, sums_low, sums_high, *stem_args],
    )

    own = own.at[1].set(partner(pooled))
    one, band = beside(own, -1), beside(own, 0)
    relay, two = outer(one), beside(own, 1)
    sent = dict(own=own, one=one, band=band)

    def context_call(kernel, phase, outs, args, scratch=(), **more):
        count = len(TILES[phase]) * WIDE
        buffers = [pltpu.VMEM((WIDE, count), BF16), pltpu.VMEM((count, SPOTS), BF16)]
        return call(functools.partial(kernel, cells), outs, args, buffers + list(scratch), **more)

    context, head_w, rim_w, up_bias = context_call(
        early_kernel, 0,
        [
            shape_of(WIDE, SPOTS), shape_of(160, 20 * CH, dtype=BF16), shape_of(40, 4 * CH, dtype=BF16),
            shape_of(CH, 256),
        ],
        [*(sent[name] for name in PHASES[0]), *proj_args, w_head, b_up[None, :]],
    )
    relay, context = tie((relay, context))
    relay_p, two_p = partner(relay), partner(two)
    band_p, one_p = partner(band), partner(one)

    inner_logits, col_out, row_out = context_call(
        logits_kernel, 1,
        [shape_of(2, ROWS, COLS), shape_of(ROWS + 8, 128), shape_of(8, COLS)],
        [
            feat_low, feat_high, rim_rows, rim_cols, context, two, two_p, relay, relay_p, band_p, one_p,
            *proj_args, w_up, up_bias, head_w, rim_w, b_head,
        ],
        [
            pltpu.VMEM((POOL_ROWS * CH, 256), BF16),
            pltpu.VMEM((POOL_ROWS * CH, COLS), F32),
            pltpu.VMEM(((ROWS + 4) * CH, COLS), BF16),
        ],
        smem=(19,),
    )
    near, far = partner(col_out), outer(col_out)
    row_out = row_sums(cells, row_out, near, far)
    return call(
        functools.partial(sum_kernel, cells),
        shape_of(2, ROWS, COLS),
        [inner_logits, near, far, even_pair(row_out), odd_pair(row_out)],
    )


def solution(mesh):
    sizes = dict(mesh.shape)
    return jax.shard_map(
        functools.partial(body, sizes["cross"], sizes["band"]),
        mesh=mesh,
        in_specs=(P(None, "cross", "band"), P("cross", "band")) + (P(),) * 12,
        out_specs=P(None, "cross", "band"),
        check_vma=False,
    )
```

```python
import functools

import jax
import jax.numpy as jnp
from jax import lax
from jax.experimental import pallas as pl
from jax.experimental.pallas import tpu as pltpu
from jax.sharding import PartitionSpec as P

ROWS, COLS = 64, 512
CH, WIDE, KINDS = 32, 128, 8
POOL_ROWS, POOL_COLS = 16, 128
SPOTS = POOL_ROWS * POOL_COLS
FIRST = 8
HBM = pl.BlockSpec(memory_space=pltpu.HBM)
VMEM = pl.BlockSpec(memory_space=pltpu.VMEM)
SMEM = pl.BlockSpec(memory_space=pltpu.SMEM)
F32, BF16 = jnp.float32, jnp.bfloat16


def iota(shape, dim):
    return lax.broadcasted_iota(jnp.int32, shape, dim)


def shape_of(*dims, dtype=F32):
    return jax.ShapeDtypeStruct(dims, dtype)


def mm(a, b):
    return jnp.dot(a, b, preferred_element_type=F32)


def split(x):
    high = x.astype(BF16)
    return high, (x - high.astype(F32)).astype(BF16)


def column(row):
    count = row.shape[1]
    eye = iota((count, count), 0) == iota((count, count), 1)
    return jnp.sum(jnp.where(eye, row, 0.0), axis=1, keepdims=True)


def placed():
    return lax.axis_index("cross"), lax.axis_index("band")


def flags(last_cross, last_band):
    cross, band = placed()
    one = lambda truth: truth.astype(F32)
    return one(cross > 0), one(cross < last_cross), one(band > 0), one(band < last_band)


def kinds_of(w_in, gain, b_in, gains):
    lane = iota((CH, KINDS), 1)
    kinds = jnp.zeros((CH, KINDS), F32)
    parts = [w_in[k : k + 1, :] for k in range(4)] + [gain[...]] * gains + [b_in[...]]
    parts = [column(part) for part in parts]
    for kind, part in enumerate(parts):
        kinds = jnp.where(lane == kind, part, kinds)
    return kinds


def pool_weights():
    x, q = iota((COLS, POOL_COLS), 0), iota((COLS, POOL_COLS), 1)
    inner = (x // 4 == q) & (x > 0) & (x < COLS - 1)
    return jnp.where(inner, 1.0 / 16, 0.0).astype(BF16)


def halo_kernel(rasters, aerial, rows, cols, message, stem_in):
    ones, none = jnp.ones((1, COLS), F32), jnp.zeros((2, COLS), F32)
    for at, y in enumerate((0, 1, ROWS - 2, ROWS - 1)):
        parts = [rasters[kind, y : y + 1, :].astype(F32) for kind in range(4)]
        rows[at * 8 : (at + 1) * 8, :] = jnp.concatenate(parts + [aerial[y : y + 1, :], ones, none], axis=0)
    lane = iota((ROWS, 128), 1)
    packed = jnp.where((lane < 32) & (lane % 8 == 5), 1.0, 0.0)
    for at, x in enumerate((0, 1, COLS - 2, COLS - 1)):
        first = x // 128 * 128
        for kind in range(5):
            if kind < 4:
                slab = rasters[kind, :, first : first + 128].astype(F32)
            else:
                slab = aerial[:, first : first + 128]
            packed = jnp.where(lane == at * 8 + kind, slab[:, x - first : x - first + 1], packed)
    turned = jnp.transpose(jnp.concatenate([packed, jnp.zeros((128 - ROWS, 128), F32)], axis=0))
    cols[...] = turned[:32]
    message[...] = jnp.concatenate([turned[:8], turned[24:32]], axis=0)
    for y in range(0, ROWS, 8):
        values = jnp.concatenate([rasters[k, y : y + 8, :] for k in range(4)], axis=0).astype(F32)
        high, low = split(aerial[y : y + 8, :])
        tail = jnp.concatenate([jnp.ones((8, COLS), BF16), jnp.zeros((8, COLS), BF16)], axis=0)
        stem_in[y * 8 : y * 8 + 64, :] = jnp.concatenate([values.astype(BF16), high, low, tail], axis=0)


def sides(partner, outer, low, high):
    even = placed()[1] % 2 == 0
    left = jnp.where(even, outer[high], partner[high])
    right = jnp.where(even, partner[low], outer[low])
    return left, right


def row_messages(cells, rows, partner, outer):
    _, _, has_left, has_right = flags(*cells)
    left, right = sides(partner, outer, slice(0, 8), slice(8, 16))
    lane = lax.broadcasted_iota(jnp.int32, (8, 128), 1)

    def row(at, y):
        low, high = left[:, y : y + 1] * has_left, right[:, y : y + 1] * has_right
        side = jnp.where(lane == 0, high, jnp.where(lane == 1, low, 0.0))
        return jnp.concatenate([rows[at * 8 : (at + 1) * 8, :], side], axis=1)

    low, high = row(0, 0), row(3, ROWS - 1)
    even = placed()[0] % 2 == 0
    return jnp.where(even, high, low), jnp.where(even, low, high)


def inner_kernel(
    part, stem_in, w_in, gain, b_in, conv_w, conv_b, features, sums, stem_w, wide_w, stem3
):
    spread = jnp.where(iota((KINDS, 64), 1) // 8 == iota((KINDS, 64), 0), 1.0, 0.0).astype(BF16)
    same = iota((256, 64), 0) // CH == iota((256, 64), 1) % 8
    halves = []
    for piece in split(kinds_of(w_in, gain, b_in, 2)):
        rows = mm(jnp.concatenate([piece] * 8, axis=0), spread)
        halves.append(jnp.where(same, rows, 0.0))
    stem_w[...] = jnp.concatenate(halves, axis=1).astype(BF16)
    wide_w[...] = jnp.zeros(wide_w.shape, BF16)
    taps = conv_w[...]
    for y in range(8):
        wide_w[y * CH : (y + 1) * CH, y * 96 : y * 96 + 288] = taps
    pool_w = pool_weights()
    bias = jnp.broadcast_to(column(conv_b[...]), (CH, COLS))
    bias = jnp.concatenate([bias] * 8, axis=0)

    start, count = (0, FIRST) if part == 0 else (FIRST, ROWS - FIRST)
    blocks = range(max(start // 8 - 1, 0), min((start + count) // 8 + 1, ROWS // 8))
    base = start - 1
    edge = 0 if part == 0 else count + 1
    stem3[edge * 96 : (edge + 1) * 96, :] = jnp.zeros((96, COLS), BF16)
    for block in blocks:
        y = block * 8
        x = stem_in[y * 8 : y * 8 + 64, :]
        out = jnp.maximum(mm(stem_w[...], jnp.concatenate([x, x], axis=0)), 0.0)
        for r in range(8):
            at = y + r - base
            if at < 0 or at > count + 1:
                continue
            s = out[r * CH : (r + 1) * CH, :]
            parts = [pltpu.roll(s, 1, 1), s, pltpu.roll(s, COLS - 1, 1)]
            stem3[at * 96 : (at + 1) * 96, :] = jnp.concatenate(parts, axis=0).astype(BF16)

    for block in range(count // 8):
        out = mm(wide_w[...], stem3[block * 768 : block * 768 + 960, :])
        value = jnp.maximum(out + bias, 0.0).astype(BF16)
        features[block * 256 : (block + 1) * 256, :] = value
        means = mm(value, pool_w)
        for p in range(2):
            rows = [means[p * 128 + r * 32 : p * 128 + (r + 1) * 32, :] for r in range(4)]
            if part == 0 and block == 0 and p == 0:
                rows = rows[1:]
            if part == 1 and block == count // 8 - 1 and p == 1:
                rows = rows[:3]
            at = (block * 2 + p) * POOL_COLS
            sums[:, at : at + POOL_COLS] = sum(rows[1:], rows[0])


def rim_kernel(
    cells, rows, cols, partner, outer, even_message, odd_message, sums_low, sums_high,
    w_in, gain, b_in, conv_w, conv_b, rim_rows, rim_cols, pooled, own,
):
    has_above, has_below, has_left, has_right = flags(*cells)
    left, right = sides(partner, outer, slice(0, 8), slice(8, 16))
    left, right = left * has_left, right * has_right
    even = placed()[0] % 2 == 0
    above = jnp.where(even, odd_message[...], even_message[...]) * has_above
    below = jnp.where(even, even_message[...], odd_message[...]) * has_below
    kind_high, kind_low = split(kinds_of(w_in, gain, b_in, 1))
    stem_w = jnp.concatenate([kind_high, kind_high, kind_low], axis=1)
    bias = column(conv_b[...])

    def stem(x):
        high, low = split(x)
        high = high.astype(F32)
        stacked = jnp.concatenate([high, low.astype(F32), high], axis=0).astype(BF16)
        return jnp.maximum(mm(stem_w, stacked), 0.0)

    def conv(stacked):
        return jnp.maximum(mm(conv_w[...], stacked) + bias, 0.0).astype(BF16)

    def row(at):
        return rows[at * 8 : (at + 1) * 8, :]

    pool_w = pool_weights()
    row_sums = []
    trios = [(above[:, :COLS], row(0), row(1)), (row(2), row(3), below[:, :COLS])]
    for at, trio in enumerate(trios):
        stacked = []
        for x in trio:
            s = stem(x)
            stacked += [pltpu.roll(s, 1, 1), s, pltpu.roll(s, COLS - 1, 1)]
        value = conv(jnp.concatenate(stacked, axis=0).astype(BF16))
        rim_rows[at * CH : (at + 1) * CH, :] = value
        row_sums.append(mm(value, pool_w))

    lane = iota((8, 128), 1)

    def line(inside, top, bottom, x):
        top, bottom = top[:, x : x + 1], bottom[:, x : x + 1]
        return jnp.where(lane < ROWS, inside, jnp.where(lane == ROWS, bottom, 0.0)), top

    x_of = {-1: COLS + 1, COLS: COLS}
    lines = {-1: left, COLS: right}
    for at, x in enumerate((0, 1, COLS - 2, COLS - 1)):
        lines[x] = cols[at * 8 : (at + 1) * 8, :]
    columns = []
    for dx in (-1, 0, 1):
        low, low_top = line(lines[dx], above, below, x_of.get(dx, dx))
        x = COLS - 1 + dx
        high, high_top = line(lines[x], above, below, x_of.get(x, x))
        low = jnp.where(lane == 127, high_top, low)
        high = jnp.where(lane == 127, low_top, high)
        columns.append(stem(jnp.concatenate([low, high], axis=1)))
    s = jnp.concatenate(columns, axis=0)
    stacked = [pltpu.roll(s, 1, 1), s, pltpu.roll(s, 255, 1)]
    value = conv(jnp.concatenate(stacked, axis=0).astype(BF16))
    rim_cols[...] = value
    y, at = iota((256, 128), 0), iota((256, 128), 1)
    picked = (y < ROWS) & (y // 4 == at) | (y >= 128) & (y < 128 + ROWS) & (y // 4 - 16 == at)
    col_sums = mm(value, jnp.where(picked, 1.0 / 16, 0.0).astype(BF16))
    lane = iota((CH, POOL_COLS), 1)
    for p in range(POOL_ROWS):
        at = p * POOL_COLS
        near = sums_low if p < FIRST // 4 else sums_high
        first = at if p < FIRST // 4 else at - FIRST // 4 * POOL_COLS
        last = jnp.where(lane == POOL_COLS - 1, col_sums[:, 16 + p : 17 + p], 0.0)
        total = near[:, first : first + POOL_COLS] + jnp.where(lane == 0, col_sums[:, p : p + 1], last)
        if p == 0:
            total += row_sums[0]
        if p == POOL_ROWS - 1:
            total += row_sums[1]
        pooled[:, at : at + POOL_COLS] = total.astype(BF16)
        own[0, :, at : at + POOL_COLS] = total.astype(BF16)
    own[1, :, :] = jnp.zeros((CH, SPOTS), BF16)


def head_weights(w_head, row_y, row_count, col_y, col_count):
    shape = (10 * row_count, col_count * CH)
    rows = iota((10 * row_count, 2), 0) // row_count % 2 == iota((10 * row_count, 2), 1)
    pick = jnp.where(rows, 1.0, 0.0).astype(BF16)
    dx = iota((10 * row_count, 160), 0) // (2 * row_count) == iota((10 * row_count, 160), 1) // CH
    repeat = iota((160, shape[1]), 0) % CH == iota((160, shape[1]), 1) % CH
    repeat = jnp.where(repeat, 1.0, 0.0).astype(BF16)
    dy = row_y(iota(shape, 0) % row_count) - col_y(iota(shape, 1) // CH)
    total = jnp.zeros(shape, F32)
    for tap in range(5):
        taps = mm(pick, w_head[:, tap * 160 : (tap + 1) * 160])
        taps = mm(jnp.where(dx, taps, 0.0).astype(BF16), repeat)
        total = jnp.where(dy == tap - 2, taps, total)
    return total.astype(BF16)


MAPS = {
    (0, -2): ("band", 0), (0, -1): ("band", 1), (0, 0): ("own", 0), (0, 1): ("own", 1), (0, 2): ("band_p", 1),
    (-1, -2): ("one", 0), (-1, -1): ("one", 1), (-1, 0): ("relay_p", 0), (-1, 1): ("relay_p", 1), (-1, 2): ("two_p", 1),
    (1, -2): ("two", 0), (1, -1): ("two", 1), (1, 0): ("relay", 1), (1, 1): ("relay", 0), (1, 2): ("one_p", 1),
}
PHASES = (("own", "one", "band"), ("two_p", "relay", "relay_p"), ("one_p", "band_p", "two"))
TILES = [[at for at in range(15) if MAPS[(at // 5 - 1, at % 5 - 2)][0] in names] for names in PHASES]


def context_sum(cells, which, arrays, proj_w, proj_b, ctx_w, weights, proj, finish):
    last_cross, last_band = cells
    cross, band = placed()
    core = band % 2
    sign = 1 - 2 * core
    for k, at in enumerate(which):
        row, col = cross + (at // 5 - 1) * sign, band + (at % 5 - 2) * sign
        inside = (row >= 0) & (row <= last_cross) & (col >= 0) & (col <= last_band)
        one = ctx_w[:, at * WIDE : (at + 1) * WIDE]
        two = ctx_w[:, (14 - at) * WIDE : (15 - at) * WIDE]
        chosen = jnp.where(core == 0, one, two)
        weights[:, k * WIDE : (k + 1) * WIDE] = jnp.where(inside, chosen, jnp.zeros_like(chosen))
    p_bias = jnp.broadcast_to(column(proj_b[...]), (WIDE, 256))
    proj_w = jnp.transpose(proj_w[...].astype(F32)).astype(BF16)

    def project(spots):
        for k, tile in enumerate(which):
            name, half = MAPS[(tile // 5 - 1, tile % 5 - 2)]
            out = mm(proj_w, arrays[name][half, :, spots])
            proj[k * WIDE : (k + 1) * WIDE, spots] = jnp.maximum(out + p_bias, 0.0).astype(BF16)

    spots = [slice(at * 256, (at + 1) * 256) for at in range(SPOTS // 256)]
    project(spots[0])
    for at, spot in enumerate(spots):
        if at + 1 < len(spots):
            project(spots[at + 1])
        finish(at, spot, mm(weights[...], proj[:, spot]))


def early_kernel(cells, *refs):
    count = len(PHASES[0])
    arrays = dict(zip(PHASES[0], refs[:count]))
    proj_w, proj_b, ctx_w, w_head, up_b, context, head_w, rim_w, up_bias, weights, proj = refs[count:]
    up_bias[...] = jnp.broadcast_to(column(up_b[...]), (CH, 256))
    head_w[...] = head_weights(w_head[...], lambda r: r, 16, lambda r: r - 2, 20)
    outside = lambda r: jnp.where(r < 2, r - 2, ROWS - 2 + r)
    rim_w[...] = head_weights(w_head[...], outside, 4, lambda r: jnp.where(r < 2, r, ROWS - 4 + r), 4)
    own = TILES[0].index(7)

    def finish(at, spots, total):
        context[:, spots] = total + proj[own * WIDE : (own + 1) * WIDE, spots].astype(F32)

    context_sum(cells, TILES[0], arrays, proj_w, proj_b, ctx_w, weights, proj, finish)


def middle_kernel(cells, one_p, band_p, two, before, proj_w, proj_b, ctx_w, context, weights, proj):
    arrays = dict(zip(PHASES[2], (one_p, band_p, two)))

    def finish(at, spots, total):
        context[:, spots] = total + before[:, spots]

    context_sum(cells, TILES[2], arrays, proj_w, proj_b, ctx_w, weights, proj, finish)


def logits_kernel(
    cells, low, high, rim_rows, rim_cols, context, two_p, relay, relay_p,
    proj_w, proj_b, ctx_w, up_w, up_b, head_w, rim_w, head_b,
    logits, col_out, row_out, weights, proj, low_up, lifted, decoded,
):
    arrays = dict(zip(PHASES[1], (two_p, relay, relay_p)))

    def finish(part, spots, total):
        mixed = jnp.maximum(total + context[:, spots], 0.0).astype(BF16)
        up = mm(up_w[...], mixed) + up_b[...]
        high, low = split(up)
        both = [
            jnp.concatenate([high[:, h * 128 : (h + 1) * 128], low[:, h * 128 : (h + 1) * 128]], axis=1)
            for h in range(2)
        ]
        low_up[part * 64 : (part + 1) * 64, :] = jnp.concatenate(both, axis=0)

    context_sum(cells, TILES[1], arrays, proj_w, proj_b, ctx_w, weights, proj, finish)

    widen = jnp.where(
        iota((256, COLS), 0) % 128 == iota((256, COLS), 1) // 4, 1.0, 0.0
    ).astype(BF16)
    lifted[...] = mm(low_up[...], widen)

    decoded[0:64, :] = jnp.zeros((64, COLS), BF16)
    decoded[66 * CH :, :] = jnp.zeros((64, COLS), BF16)

    lane = iota((CH, 128), 1)
    columns = rim_cols[...].astype(F32)
    for y in range(ROWS):
        if y == 0:
            f = rim_rows[0:CH, :]
        elif y == ROWS - 1:
            f = rim_rows[CH : 2 * CH, :]
        else:
            at = (y if y < FIRST else y - FIRST) * CH
            f = (low if y < FIRST else high)[at : at + CH, :]
        f = f.astype(F32)
        first = jnp.where(lane == 0, columns[:, y : y + 1], f[:, :128])
        last = jnp.where(lane == 127, columns[:, 128 + y : 129 + y], f[:, COLS - 128 :])
        f = jnp.concatenate([first, f[:, 128 : COLS - 128], last], axis=1)
        value = f + lifted[y // 4 * CH : (y // 4 + 1) * CH, :]
        decoded[(y + 2) * CH : (y + 3) * CH, :] = jnp.maximum(value, 0.0).astype(BF16)

    def gather_taps(z, count):
        total = None
        for dx in range(5):
            part = z[dx * count : (dx + 1) * count, :]
            part = jnp.concatenate([part, jnp.zeros((count, 128), F32)], axis=1)
            if dx != 2:
                part = pltpu.roll(part, (dx - 2) % 640, 1)
            total = part if total is None else total + part
        return total

    lane16 = iota((16, 128), 1)
    first_lanes = (lane16 < 2) | (lane16 >= 126)

    def head(block, carry):
        first = pl.multiple_of(block * 16 * CH, 16 * CH)
        total = gather_taps(mm(head_w[...], decoded[pl.ds(first, 20 * CH), :]), 32)
        y = pl.multiple_of(block * 16, 16)
        for k in range(2):
            logits[k, pl.ds(y, 16), :] = total[k * 16 : (k + 1) * 16, :COLS] + head_b[k]
        rim = total[:, COLS:]
        col_out[pl.ds(y, 16), :] = jnp.where(first_lanes, rim[:16], pltpu.roll(rim[16:], 4, 1))
        return carry

    lax.fori_loop(0, ROWS // 16, head, 0, unroll=True)

    ends = jnp.concatenate([decoded[64:128, :], decoded[64 * CH : 66 * CH, :]], axis=0)
    total = gather_taps(mm(rim_w[...], ends), 8)
    row_out[...] = total[:, :COLS]
    col_out[ROWS : ROWS + 8, :] = total[:, COLS:]


def row_sums(cells, row_out, partner, outer):
    _, _, has_left, has_right = flags(*cells)
    corners = slice(ROWS, ROWS + 8)
    left, right = sides(partner, outer, corners, corners)
    lane = lax.broadcasted_iota(jnp.int32, (8, 128), 1)
    low = jnp.where(lane < 2, left * has_left, 0.0)
    high = jnp.where(lane >= 126, right * has_right, 0.0)
    return row_out + jnp.concatenate([low, jnp.zeros((8, COLS - 256), F32), high], axis=1)


def sum_kernel(cells, inner, partner, outer, even_message, odd_message, out):
    has_above, has_below, has_left, has_right = flags(*cells)
    even = placed()[0] % 2 == 0
    above = jnp.where(even, odd_message[...], even_message[...]) * has_above
    below = jnp.where(even, even_message[...], odd_message[...]) * has_below
    left, right = sides(partner, outer, slice(0, ROWS), slice(0, ROWS))
    left, right = left * has_left, right * has_right
    out[...] = inner[...]
    lane = iota((ROWS, 128), 1)
    for k in range(2):
        low = left if k == 0 else pltpu.roll(left, 124, 1)
        out[k, :, 0:128] += jnp.where(lane < 2, low, 0.0)
        high = right if k == 0 else pltpu.roll(right, 124, 1)
        out[k, :, COLS - 128 : COLS] += jnp.where(lane >= 126, high, 0.0)
        out[k, 0:2, :] += above[4 * k + 2 : 4 * k + 4]
        out[k, ROWS - 2 : ROWS, :] += below[4 * k : 4 * k + 2]


def call(kernel, outs, args, scratch=(), smem=(), hbm=(), flops=0):
    scratch = list(scratch)

    def fetching(*refs):
        ins, rest = list(refs[: len(args)]), refs[len(args) :]
        buffers, sems = rest[-len(hbm) - 1 : -1], rest[-1]
        copies = [pltpu.make_async_copy(ins[at], buffers[i], sems.at[i]) for i, at in enumerate(hbm)]
        for copy in copies:
            copy.start()
        for copy in copies:
            copy.wait()
        for at, buffer in zip(hbm, buffers):
            ins[at] = buffer
        kernel(*ins, *rest[: -len(hbm) - 1])

    if hbm:
        scratch += [pltpu.VMEM(args[at].shape, args[at].dtype) for at in hbm]
        scratch += [pltpu.SemaphoreType.DMA((len(hbm),))]
    return pl.pallas_call(
        fetching if hbm else kernel,
        out_shape=outs,
        in_specs=[SMEM if at in smem else HBM if at in hbm else VMEM for at in range(len(args))],
        out_specs=jax.tree.map(lambda _: VMEM, outs),
        scratch_shapes=scratch,
        compiler_params=pltpu.CompilerParams(vmem_limit_bytes=24 * 1024 * 1024),
        cost_estimate=pl.CostEstimate(flops=flops, bytes_accessed=1 << 20, transcendentals=0),
    )(*args)


def body(
    n_cross, n_band, rasters, aerial, w_in, aerial_gain, b_in, w_conv1, b_conv1, w_proj, b_proj,
    w_ctx, w_up, b_up, w_head, b_head,
):
    cells = (n_cross - 1, n_band - 1)
    tie = lax.optimization_barrier

    def moved(x, source):
        route = []
        for cross in range(n_cross):
            for band in range(n_band):
                c, b = source(cross, band)
                route.append(((b % n_band) * n_cross + c % n_cross, band * n_cross + cross))
        return lax.ppermute(x, ("band", "cross"), route)

    def partner(x):
        return moved(x, lambda c, b: (c, b ^ 1))

    def outer(x):
        return moved(x, lambda c, b: (c, ((b + 1) ^ 1) - 1))

    def even_pair(x):
        return moved(x, lambda c, b: (c ^ 1, b))

    def odd_pair(x):
        return moved(x, lambda c, b: (((c + 1) ^ 1) - 1, b))

    def beside(x, u):
        return moved(x, lambda c, b: (c + u * (1 - 2 * (b % 2)), b - 2 + 4 * (b % 2)))

    rows, cols, message, stem_in = call(
        halo_kernel,
        [shape_of(32, COLS), shape_of(32, 128), shape_of(16, 128), shape_of(8 * ROWS, COLS, dtype=BF16)],
        [rasters, aerial],
        flops=8 * 10**10,
    )
    near, far = partner(message), outer(message)

    stem_args = [w_in.T, aerial_gain[None, :], b_in[None, :], w_conv1, b_conv1[None, :]]
    proj_args = [w_proj.T, b_proj[None, :], w_ctx]

    def inner(part, stem_in):
        count = FIRST if part == 0 else ROWS - FIRST
        return call(
            functools.partial(inner_kernel, part),
            [shape_of(count * CH, COLS, dtype=BF16), shape_of(CH, count // 4 * POOL_COLS)],
            [stem_in, *stem_args],
            [
                pltpu.VMEM((256, 128), BF16),
                pltpu.VMEM((256, 960), BF16),
                pltpu.VMEM(((count + 2) * 96, COLS), BF16),
            ],
            flops=4 * 10**9,
        )

    feat_low, sums_low = inner(0, stem_in)
    near, far, sums_low = tie((near, far, sums_low))
    even_out, odd_out = row_messages(cells, rows, near, far)
    even_out, odd_out, stem_in = tie((even_out, odd_out, stem_in))
    even_in, odd_in = even_pair(even_out), odd_pair(odd_out)
    feat_high, sums_high = inner(1, stem_in)

    rim_rows, rim_cols, pooled, own = call(
        functools.partial(rim_kernel, cells),
        [
            shape_of(2 * CH, COLS, dtype=BF16), shape_of(CH, 256, dtype=BF16), shape_of(CH, SPOTS, dtype=BF16),
            shape_of(2, CH, SPOTS, dtype=BF16),
        ],
        [rows, cols, near, far, even_in, odd_in, sums_low, sums_high, *stem_args],
    )

    own = own.at[1].set(partner(pooled))
    one, band = beside(own, -1), beside(own, 0)
    relay, two = outer(one), beside(own, 1)
    sent = dict(own=own, one=one, band=band)

    def context_call(kernel, phase, outs, args, scratch=(), **more):
        count = len(TILES[phase]) * WIDE
        buffers = [pltpu.VMEM((WIDE, count), BF16), pltpu.VMEM((count, SPOTS), BF16)]
        return call(functools.partial(kernel, cells), outs, args, buffers + list(scratch), **more)

    context, head_w, rim_w, up_bias = context_call(
        early_kernel, 0,
        [
            shape_of(WIDE, SPOTS), shape_of(160, 20 * CH, dtype=BF16), shape_of(40, 4 * CH, dtype=BF16),
            shape_of(CH, 256),
        ],
        [*(sent[name] for name in PHASES[0]), *proj_args, w_head, b_up[None, :]],
    )
    relay, context = tie((relay, context))
    relay_p, two_p = partner(relay), partner(two)
    band_p, one_p = partner(band), partner(one)
    context = context_call(
        middle_kernel, 2, shape_of(WIDE, SPOTS), [one_p, band_p, two, context, *proj_args]
    )

    inner_logits, col_out, row_out = context_call(
        logits_kernel, 1,
        [shape_of(2, ROWS, COLS), shape_of(ROWS + 8, 128), shape_of(8, COLS)],
        [
            feat_low, feat_high, rim_rows, rim_cols, context, two_p, relay, relay_p,
            *proj_args, w_up, up_bias, head_w, rim_w, b_head,
        ],
        [
            pltpu.VMEM((POOL_ROWS * CH, 256), BF16),
            pltpu.VMEM((POOL_ROWS * CH, COLS), F32),
            pltpu.VMEM(((ROWS + 4) * CH, COLS), BF16),
        ],
        smem=(16,),
    )
    near, far = partner(col_out), outer(col_out)
    row_out = row_sums(cells, row_out, near, far)
    return call(
        functools.partial(sum_kernel, cells),
        shape_of(2, ROWS, COLS),
        [inner_logits, near, far, even_pair(row_out), odd_pair(row_out)],
    )


def solution(mesh):
    sizes = dict(mesh.shape)
    return jax.shard_map(
        functools.partial(body, sizes["cross"], sizes["band"]),
        mesh=mesh,
        in_specs=(P(None, "cross", "band"), P("cross", "band")) + (P(),) * 12,
        out_specs=P(None, "cross", "band"),
        check_vma=False,
    )
```
